32 devices in a mesh: gx: 4 (over z), gy: 8 (over y, x, core).
Axes of the slice: x: 2, y: 2, z: 4, core: 2. Of those that a mesh axis runs over, the one named last changes fastest.
Arguments:
- refl_left: float32 [32, 256, 256], P(('gx', 'gy')), may hold values from -1 to 1, as said below
- refl_right: float32 [32, 256, 256], P(('gx', 'gy')), may hold values from -1 to 1, as said below
- trans: float32 [32, 256, 256], P(('gx', 'gy')), may hold values from -2 to 2
Outputs:
- prefix_left: float32 [32, 256, 256], P(('gx', 'gy'))
- prefix_right: float32 [32, 256, 256], P(('gx', 'gy'))
- prefix_trans: float32 [32, 256, 256], P(('gx', 'gy'))
The draws below stay inside these ranges and needn't reach their ends.
Inputs may be any that keep to these rules, and one draw needn't show every extreme that they name: `refl_left`: every section's reflection matrix is symmetric. `refl_right`: every section's reflection matrix is symmetric.
All inputs are finite; a program needn't handle non-finite values.
Results may differ from the reference program's by a relative error of at most 0.0003.
Values sent between devices are 32-bit elements; how exact they have to be, the bound alone decides.
No kernel may reach another device: no remote copies, remote signals or barrier semaphores. Data moves between devices by JAX's collectives and lax.ppermute only.
A program may use at most 64 MiB of HBM per device.

```python
import jax
import jax.numpy as jnp
from jax import lax

M = 256
NS_STEPS = 5
SECTIONS = 32


def symmetric_reflection(key):
    noise = jax.random.normal(key, (SECTIONS, M, M), jnp.float32)
    noise = (noise + jnp.swapaxes(noise, 1, 2)) * 0.5 ** 0.5
    return noise * (143.0 * M) ** (-0.5)


def draw_refl_left(key, part):
    return symmetric_reflection(jax.random.fold_in(key, 31))


def draw_refl_right(key, part):
    return symmetric_reflection(jax.random.fold_in(key, 47))


def draw_trans(key, part):
    first, second, third = jax.random.split(jax.random.fold_in(key, 17), 3)
    signs = jnp.where(jax.random.uniform(first, (SECTIONS, M)) < 0.5, -1.0, 1.0)
    diag = signs * jax.random.uniform(second, (SECTIONS, M), jnp.float32, 0.955, 0.995)
    noise = jax.random.normal(third, (SECTIONS, M, M), jnp.float32)
    noise = noise * (0.2 / M ** 0.5)
    return noise + diag[:, :, None] * jnp.eye(M, dtype=jnp.float32)[None]


def setup_inputs(seed: int = 0) -> dict:
    streams_of = jax.random.split(jax.random.key(seed), 4)
    refl_left = draw_refl_left(jax.random.fold_in(streams_of[3], 71), 0)
    refl_right = draw_refl_right(jax.random.fold_in(streams_of[3], 71), 0)
    trans = draw_trans(jax.random.fold_in(streams_of[3], 71), 0)
    return {"refl_left": refl_left, "refl_right": refl_right, "trans": trans}


def mult(left, right):
    return jnp.dot(left, right, precision=lax.Precision.HIGHEST)


def star(first, second):
    eye = jnp.eye(first.shape[1], dtype=first.dtype)
    coupling = mult(first[1], second[0])
    inverse = eye + coupling
    for step in range(NS_STEPS):
        inverse = mult(inverse, 2.0 * eye - mult(eye - coupling, inverse))
    ahead = mult(inverse, first[2])
    trans_new = mult(second[2], ahead)
    left_new = first[0] + mult(first[2].T, mult(second[0], ahead))
    right_new = second[1] + mult(second[2], mult(inverse, mult(first[1], second[2].T)))
    return jnp.stack([left_new, right_new, trans_new])


def reference(refl_left, refl_right, trans):
    size = refl_left.shape[1]
    zeros = jnp.zeros((size, size), refl_left.dtype)
    start = jnp.stack([zeros, zeros, jnp.eye(size, dtype=refl_left.dtype)])

    def advance(carry, section):
        merged = star(carry, jnp.stack(section))
        return merged, merged

    final, prefixes = lax.scan(advance, start, (refl_left, refl_right, trans))
    return prefixes[:, 0], prefixes[:, 1], prefixes[:, 2]
```

```python
import functools

import jax
import jax.numpy as jnp
from jax import lax
from jax.experimental import pallas as pl
from jax.experimental.pallas import tpu as pltpu
from jax.sharding import PartitionSpec as P

AXES = ("gx", "gy")
NS_STEPS = 5
F32 = jnp.float32
BF16 = jnp.bfloat16
NN = (((1,), (0,)), ((), ()))
NT = (((1,), (1,)), ((), ()))


def swap(block, distance):
    count = lax.axis_size(AXES)
    return lax.ppermute(block, AXES, [(i, i ^ distance) for i in range(count)])


def split(x):
    high = x.astype(BF16)
    return high, (x - high.astype(F32)).astype(BF16)


def dot1(a, b, dims=NN):
    return lax.dot_general(a, b, dims, preferred_element_type=F32)


def dot3(a, b, dims=NN):
    return dot1(a[0], b[0], dims) + (dot1(a[0], b[1], dims) + dot1(a[1], b[0], dims))


def half(x):
    return x.astype(BF16)


def inverse_less_eye(coupling):
    rest, power = coupling, half(coupling)
    for _ in range(NS_STEPS - 1):
        squared = dot1(power, power)
        power = half(squared)
        rest = rest + squared + dot1(half(rest), power)
    rest = half(rest)
    high, low = split(coupling)
    rest32 = rest.astype(F32)
    residual = (coupling - rest32) + (dot1(high, rest) + dot1(low, rest))
    return rest32 + residual + dot1(rest, half(residual))


def star(first, second):
    a_left, a_right, a_trans = first
    b_left, b_right, b_trans = second
    a2, b1, at, bt = split(a_right), split(b_left), split(a_trans), split(b_trans)
    inner = dot3(a2, bt, NT)
    coupling = dot3(a2, b1)
    rest = split(inverse_less_eye(coupling))
    ahead = split(a_trans + dot3(rest, at))
    back = split(inner + dot3(rest, split(inner)))
    trans = dot3(bt, ahead)
    right = b_right + dot3(bt, back)
    lead = split(dot3(b1, ahead))
    flipped = split(a_trans.T)
    left = a_left + dot3(flipped, lead)
    return left, right, trans


def place():
    return lax.axis_index("gx") * lax.axis_size("gy") + lax.axis_index("gy")


def rows_cols(m):
    return lax.broadcasted_iota(jnp.int32, (m, m), 0), lax.broadcasted_iota(jnp.int32, (m, m), 1)


def pack(total, core, message_ref):
    left, right, trans = total
    m = left.shape[0]
    h = m // 2
    row, col = rows_cols(m)
    both = jnp.where(row >= col, left, right)
    diagonal = jnp.sum(jnp.where(row == col, right, 0.0), axis=0, keepdims=True)
    message_ref[0:h, :] = jnp.where(core == 0, both[:h], both[h:])
    message_ref[h:m, :] = jnp.where(core == 0, trans[:h], trans[h:])
    message_ref[m:, :] = jnp.broadcast_to(diagonal, (8, m))


def unpack(near_ref, far_ref, core):
    m = near_ref.shape[1]
    h = m // 2

    def whole(lo, hi):
        near, far = near_ref[lo:hi, :], far_ref[lo:hi, :]
        top = jnp.where(core == 0, near, far)
        return jnp.concatenate([top, jnp.where(core == 0, far, near)], 0)

    both, trans = whole(0, h), whole(h, m)
    turned = both.T
    row, col = rows_cols(m)
    left = jnp.where(row >= col, both, turned)
    right = jnp.where(row < col, both, jnp.where(row > col, turned, near_ref[m : m + 1, :]))
    return left, right, trans


def choose(pick, yes, no):
    return tuple(jnp.where(pick, a, b) for a, b in zip(yes, no))


def first_kernel(own1, own2, own3, got1, got2, got3, total_ref, prefix_ref, message_ref):
    me = place()
    upper = me & 1 == 1
    own = own1[0], own2[0], own3[0]
    got = got1[0], got2[0], got3[0]
    total = star(choose(upper, got, own), choose(upper, own, got))
    pack(total, me & 1, message_ref)
    for i, (t, o) in enumerate(zip(total, own)):
        total_ref[i] = t
        prefix_ref[i] = jnp.where(upper, t, o)


def middle_kernel(distance, total_in, prefix_in, near_ref, far_ref, total_ref, prefix_ref, message_ref):
    me = place()
    upper = me & distance != 0
    got = unpack(near_ref, far_ref, me & 1)
    mine = total_in[0], total_in[1], total_in[2]
    prefix = prefix_in[0], prefix_in[1], prefix_in[2]
    total = star(choose(upper, got, mine), choose(upper, mine, got))
    pack(total, me & 1, message_ref)
    longer = star(got, prefix)
    for i in range(3):
        total_ref[i] = total[i]
        prefix_ref[i] = jnp.where(upper, longer[i], prefix[i])


def last_kernel(distance, prefix_in, near_ref, far_ref, left_ref, right_ref, trans_ref):
    me = place()
    upper = me & distance != 0
    got = unpack(near_ref, far_ref, me & 1)
    prefix = prefix_in[0], prefix_in[1], prefix_in[2]
    longer = star(got, prefix)
    for i, ref in enumerate((left_ref, right_ref, trans_ref)):
        ref[0] = jnp.where(upper, longer[i], prefix[i])


def call(kernel, outs, *args):
    vmem = pl.BlockSpec(memory_space=pltpu.VMEM)
    return pl.pallas_call(
        kernel,
        out_shape=[jax.ShapeDtypeStruct(s, F32) for s in outs],
        in_specs=[vmem] * len(args),
        out_specs=[vmem] * len(outs),
        compiler_params=pltpu.CompilerParams(vmem_limit_bytes=40 * 2**20),
    )(*args)


def shards(refl_left, refl_right, trans):
    m = trans.shape[1]
    levels = lax.axis_size(AXES).bit_length() - 1
    own = refl_left, refl_right, trans
    got = [swap(x, 1) for x in own]
    stack, message = (3, m, m), (m + 8, m)
    total, prefix, send = call(first_kernel, [stack, stack, message], *own, *got)
    for level in range(1, levels):
        near = swap(send, 1 << level)
        far = swap(near, 1)
        if level < levels - 1:
            kernel = functools.partial(middle_kernel, 1 << level)
            total, prefix, send = call(kernel, [stack, stack, message], total, prefix, near, far)
        else:
            kernel = functools.partial(last_kernel, 1 << level)
            return tuple(call(kernel, [(1, m, m)] * 3, prefix, near, far))


def solution(mesh):
    spec = P(AXES, None, None)
    return jax.shard_map(
        shards,
        mesh=mesh,
        in_specs=(spec,) * 3,
        out_specs=(spec,) * 3,
        check_vma=False,
    )
```

```python
import functools

import jax
import jax.numpy as jnp
from jax import lax
from jax.experimental import pallas as pl
from jax.experimental.pallas import tpu as pltpu
from jax.sharding import PartitionSpec as P

AXES = ("gx", "gy")
NS_STEPS = 5
PAD = 8
F32 = jnp.float32
BF16 = jnp.bfloat16
NN = (((1,), (0,)), ((), ()))
NT = (((1,), (1,)), ((), ()))


def swap(block, distance):
    count = lax.axis_size(AXES)
    return lax.ppermute(block, AXES, [(i, i ^ distance) for i in range(count)])


def split(x):
    high = x.astype(BF16)
    return high, (x - high.astype(F32)).astype(BF16)


def dot1(a, b, dims=NN):
    return lax.dot_general(a, b, dims, preferred_element_type=F32)


def dot3(a, b, dims=NN):
    return dot1(a[0], b[0], dims) + (dot1(a[0], b[1], dims) + dot1(a[1], b[0], dims))


def half(x):
    return x.astype(BF16)


def inverse_less_eye(coupling):
    rest, power = coupling, half(coupling)
    for _ in range(NS_STEPS - 1):
        squared = dot1(power, power)
        power = half(squared)
        rest = rest + squared + dot1(half(rest), power)
    rest = half(rest)
    high, low = split(coupling)
    rest32 = rest.astype(F32)
    residual = (coupling - rest32) + (dot1(high, rest) + dot1(low, rest))
    return rest32 + residual + dot1(rest, half(residual))


def before_trans(own, facing):
    near, away, out = own
    f, o, s = split(facing), split(near), split(out)
    coupling = dot3(f, o)
    inner = split(dot3(f, s, NT))
    rest = split(inverse_less_eye(coupling))
    leading = out + dot3(s, rest)
    mirror = near + dot3(o, rest)
    return leading, mirror, away + dot3(split(leading), inner)


def after_trans(leading, mirror, away, into):
    q = split(into)
    trans = dot3(split(leading), q)
    bounced = split(dot3(split(mirror), q))
    return trans, away + dot3(split(into.T), bounced)


def place():
    return lax.axis_index("gx") * lax.axis_size("gy") + lax.axis_index("gy")


def bit(me, distance):
    return me & distance != 0


def lower_upper(h):
    row = lax.broadcasted_iota(jnp.int32, (h, h), 0)
    col = lax.broadcasted_iota(jnp.int32, (h, h), 1)
    return row > col, row < col


def pack_symmetric(x, core, ref, start):
    h = x.shape[0] // 2
    q = h // 2
    below, above = lower_upper(h)
    a, b, c = x[:h, :h], x[:h, h:], x[h:, h:]
    diagonal = jnp.sum(jnp.where(below | above, 0.0, c), axis=0, keepdims=True)
    both = jnp.concatenate([b, jnp.where(above, c, a)], 1)
    ref[start : start + q, :] = jnp.where(core, both[q:], both[:q])
    diagonal = jnp.concatenate([diagonal, diagonal], 1)
    ref[start + q : start + q + PAD, :] = jnp.broadcast_to(diagonal, (PAD, 2 * h))


def joined(near_ref, far_ref, core, lo, hi):
    near, far = near_ref[lo:hi, :], far_ref[lo:hi, :]
    return jnp.concatenate([jnp.where(core, far, near), jnp.where(core, near, far)], 0)


def unpack_symmetric(near_ref, far_ref, core, start):
    h = near_ref.shape[1] // 2
    q = h // 2
    below, above = lower_upper(h)
    both = joined(near_ref, far_ref, core, start, start + q)
    diagonal = near_ref[start + q : start + q + 1, :h]
    b, w = both[:, :h], both[:, h:]
    turned = w.T
    a = jnp.where(above, turned, w)
    c = jnp.where(above, w, jnp.where(below, turned, diagonal))
    return jnp.concatenate([jnp.concatenate([a, b], 1), jnp.concatenate([b.T, c], 1)], 0)


def unpack_second(near_ref, far_ref, core):
    h = near_ref.shape[1] // 2
    return joined(near_ref, far_ref, core, 0, h), unpack_symmetric(near_ref, far_ref, core, h)


def send_total(own_side, other_side, trans, same, core, own_ref, first_ref, second_ref):
    turned = trans.T
    near = jnp.where(same, other_side, own_side)
    away = jnp.where(same, own_side, other_side)
    h = trans.shape[0] // 2
    back = jnp.where(same, turned, trans)
    own_ref[0] = near
    own_ref[1] = away
    own_ref[2] = jnp.where(same, trans, turned)
    pack_symmetric(near, core, first_ref, 0)
    second_ref[0:h, :] = jnp.where(core, back[h:], back[:h])
    pack_symmetric(away, core, second_ref, h)


def first_kernel(section_ref, got1, got2, got3, own_ref, prefix_ref, first_ref, second_ref):
    me = place()
    upper = bit(me, 1)
    left, right, trans = section_ref[0], section_ref[1], section_ref[2]
    pick = lambda a, b: jnp.where(upper, a, b)
    own = pick(left, right), pick(right, left), pick(trans, trans.T)
    leading, mirror, own_side = before_trans(own, pick(got2[0], got1[0]))
    into = pick(got3[0], got3[0].T)
    through, other_side = after_trans(leading, mirror, pick(got1[0], got2[0]), into)
    send_total(own_side, other_side, through, upper == bit(me, 2), upper, own_ref, first_ref, second_ref)
    prefix_ref[0] = pick(other_side, left)
    prefix_ref[1] = pick(own_side, right)
    prefix_ref[2] = pick(through, trans)


def early_kernel(own_ref, near_ref, far_ref, half_ref):
    core = bit(place(), 1)
    facing = unpack_symmetric(near_ref, far_ref, core, 0)
    for i, x in enumerate(before_trans((own_ref[0], own_ref[1], own_ref[2]), facing)):
        half_ref[i] = x


def late_kernel(distance, half_ref, near_ref, far_ref, own_ref, first_ref, second_ref):
    me = place()
    core = bit(me, 1)
    into, away = unpack_second(near_ref, far_ref, core)
    trans, other_side = after_trans(half_ref[0], half_ref[1], away, into)
    same = bit(me, distance) == bit(me, 2 * distance)
    send_total(half_ref[2], other_side, trans, same, core, own_ref, first_ref, second_ref)


def prefix_kernel(distance, old_ref, near1, far1, near2, far2, new_ref):
    me = place()
    core, upper = bit(me, 1), bit(me, distance)
    facing = unpack_symmetric(near1, far1, core, 0)
    leading, mirror, right = before_trans((old_ref[0], old_ref[1], old_ref[2]), facing)
    into, away = unpack_second(near2, far2, core)
    trans, left = after_trans(leading, mirror, away, into)
    for i, x in enumerate((left, right, trans)):
        new_ref[i] = jnp.where(upper, x, old_ref[i])


def last_kernel(distance, old_ref, half_ref, near_ref, far_ref, left_ref, right_ref, trans_ref):
    me = place()
    core, upper = bit(me, 1), bit(me, distance)
    into, away = unpack_second(near_ref, far_ref, core)
    trans, left = after_trans(half_ref[0], half_ref[1], away, into)
    right_ref[0] = jnp.where(upper, half_ref[2], old_ref[1])
    trans_ref[0] = jnp.where(upper, trans, old_ref[2])
    left_ref[0] = jnp.where(upper, left, old_ref[0])


def call(kernel, products, outs, *args):
    vmem = pl.BlockSpec(memory_space=pltpu.VMEM)
    m = args[0].shape[-1]
    return pl.pallas_call(
        kernel,
        out_shape=[jax.ShapeDtypeStruct(s, F32) for s in outs],
        in_specs=[vmem] * len(args),
        out_specs=[vmem] * len(outs),
        cost_estimate=pl.CostEstimate(flops=2 * products * m**3, bytes_accessed=4 * m**2 * len(args), transcendentals=0),
        compiler_params=pltpu.CompilerParams(vmem_limit_bytes=40 * 2**20),
    )(*args)


def shards(refl_left, refl_right, trans):
    m = trans.shape[1]
    levels = lax.axis_size(AXES).bit_length() - 1
    stack = (3, m, m)
    first, second = (m // 4 + PAD, m), (m // 2 + m // 4 + PAD, m)
    sections = refl_left, refl_right, trans
    got = [swap(x, 1) for x in sections]
    section = jnp.concatenate(sections, 0)
    own, prefix, send1, send2 = call(first_kernel, 36, [stack, stack, first, second], section, *got)
    pending = None
    for level in range(1, levels):
        distance = 1 << level
        bind = lambda kernel: functools.partial(kernel, distance)
        near1, near2 = swap(send1, distance), swap(send2, distance)
        if pending is not None:
            (prefix,) = pending(prefix)
            near1, prefix = lax.optimization_barrier((near1, prefix))
        far1 = swap(near1, 1)
        if level == levels - 1:
            (halfway,) = call(early_kernel, 27, [stack], prefix, near1, far1)
            near2, halfway = lax.optimization_barrier((near2, halfway))
            far2 = swap(near2, 1)
            return tuple(call(bind(last_kernel), 9, [(1, m, m)] * 3, prefix, halfway, near2, far2))
        (halfway,) = call(early_kernel, 27, [stack], own, near1, far1)
        near2, halfway = lax.optimization_barrier((near2, halfway))
        far2 = swap(near2, 1)
        own, send1, send2 = call(bind(late_kernel), 9, [stack, first, second], halfway, near2, far2)
        pending = lambda old, kernel=bind(prefix_kernel), got=(near1, far1, near2, far2): call(kernel, 36, [stack], old, *got)


def solution(mesh):
    spec = P(AXES, None, None)
    return jax.shard_map(
        shards,
        mesh=mesh,
        in_specs=(spec,) * 3,
        out_specs=(spec,) * 3,
        check_vma=False,
    )
```

```python
import functools

import jax
import jax.numpy as jnp
from jax import lax
from jax.experimental import pallas as pl
from jax.experimental.pallas import tpu as pltpu
from jax.sharding import PartitionSpec as P

AXES = ("gx", "gy")
NS_STEPS = 5
PAD = 8
F32 = jnp.float32
BF16 = jnp.bfloat16
NN = (((1,), (0,)), ((), ()))
NT = (((1,), (1,)), ((), ()))


def swap(block, distance):
    count = lax.axis_size(AXES)
    return lax.ppermute(block, AXES, [(i, i ^ distance) for i in range(count)])


def split(x):
    high = x.astype(BF16)
    return high, (x - high.astype(F32)).astype(BF16)


def dot1(a, b, dims=NN):
    h = a.shape[0] // 2
    parts = [lax.dot_general(x, b, dims, preferred_element_type=F32) for x in (a[:h], a[h:])]
    return jnp.concatenate(parts, 0)


def dot3(a, b, dims=NN):
    return dot1(a[0], b[0], dims) + (dot1(a[0], b[1], dims) + dot1(a[1], b[0], dims))


def half(x):
    return x.astype(BF16)


def four_steps(power):
    rest, power = power, half(power)
    for _ in range(NS_STEPS - 1):
        squared = dot1(power, power)
        power = half(squared)
        rest = rest + squared + dot1(half(rest), power)
    return half(rest)


def before_trans(own, facing):
    near, away, out = own
    f, o, s = split(facing), split(near), split(out)
    rough = dot1(f[0], o[0])
    rest = four_steps(rough)
    coupling = rough + (dot1(f[0], o[1]) + dot1(f[1], o[0]))
    inner = split(dot3(f, s, NT))
    high, low = split(coupling)
    error = half((coupling - rest.astype(F32)) + (dot1(high, rest) + dot1(low, rest)))
    leading = out + (dot1(s[0], rest) + dot1(s[1], rest))
    mirror = near + (dot1(o[0], rest) + dot1(o[1], rest))
    leading = leading + dot1(half(leading), error)
    mirror = mirror + dot1(half(mirror), error)
    return leading, mirror, away + dot3(split(leading), inner)


def after_trans(leading, mirror, away, into):
    q = split(into)
    trans = dot3(split(leading), q)
    bounced = split(dot3(split(mirror), q))
    return trans, away + dot3(split(into.T), bounced)


def place():
    return lax.axis_index("gx") * lax.axis_size("gy") + lax.axis_index("gy")


def bit(me, distance):
    return me & distance != 0


def lower_upper(h):
    row = lax.broadcasted_iota(jnp.int32, (h, h), 0)
    col = lax.broadcasted_iota(jnp.int32, (h, h), 1)
    return row > col, row < col


def pack_symmetric(x, core, ref, start):
    h = x.shape[0] // 2
    q = h // 2
    below, above = lower_upper(h)
    a, b, c = x[:h, :h], x[:h, h:], x[h:, h:]
    diagonal = jnp.sum(jnp.where(below | above, 0.0, c), axis=0, keepdims=True)
    both = jnp.concatenate([b, jnp.where(above, c, a)], 1)
    ref[start : start + q, :] = jnp.where(core, both[q:], both[:q])
    diagonal = jnp.concatenate([diagonal, diagonal], 1)
    ref[start + q : start + q + PAD, :] = jnp.broadcast_to(diagonal, (PAD, 2 * h))


def joined(near_ref, far_ref, core, lo, hi):
    near, far = near_ref[lo:hi, :], far_ref[lo:hi, :]
    return jnp.concatenate([jnp.where(core, far, near), jnp.where(core, near, far)], 0)


def unpack_symmetric(near_ref, far_ref, core, start):
    h = near_ref.shape[1] // 2
    q = h // 2
    below, above = lower_upper(h)
    both = joined(near_ref, far_ref, core, start, start + q)
    diagonal = near_ref[start + q : start + q + 1, :h]
    b, w = both[:, :h], both[:, h:]
    turned = w.T
    a = jnp.where(above, turned, w)
    c = jnp.where(above, w, jnp.where(below, turned, diagonal))
    return jnp.concatenate([jnp.concatenate([a, b], 1), jnp.concatenate([b.T, c], 1)], 0)


def unpack_second(near_ref, far_ref, core):
    h = near_ref.shape[1] // 2
    return joined(near_ref, far_ref, core, 0, h), unpack_symmetric(near_ref, far_ref, core, h)


def send_total(own_side, other_side, trans, same, core, own_ref, first_ref, second_ref):
    turned = trans.T
    near = jnp.where(same, other_side, own_side)
    away = jnp.where(same, own_side, other_side)
    h = trans.shape[0] // 2
    back = jnp.where(same, turned, trans)
    own_ref[0] = near
    own_ref[1] = away
    own_ref[2] = jnp.where(same, trans, turned)
    pack_symmetric(near, core, first_ref, 0)
    second_ref[0:h, :] = jnp.where(core, back[h:], back[:h])
    pack_symmetric(away, core, second_ref, h)


def first_kernel(section_ref, got1, got2, got3, own_ref, prefix_ref, first_ref, second_ref):
    me = place()
    upper = bit(me, 1)
    left, right, trans = section_ref[0], section_ref[1], section_ref[2]
    pick = lambda a, b: jnp.where(upper, a, b)
    own = pick(left, right), pick(right, left), pick(trans, trans.T)
    leading, mirror, own_side = before_trans(own, pick(got2[0], got1[0]))
    into = pick(got3[0], got3[0].T)
    through, other_side = after_trans(leading, mirror, pick(got1[0], got2[0]), into)
    send_total(own_side, other_side, through, upper == bit(me, 2), upper, own_ref, first_ref, second_ref)
    prefix_ref[0] = pick(other_side, left)
    prefix_ref[1] = pick(own_side, right)
    prefix_ref[2] = pick(through, trans)


def early_kernel(own_ref, near_ref, far_ref, half_ref):
    core = bit(place(), 1)
    facing = unpack_symmetric(near_ref, far_ref, core, 0)
    for i, x in enumerate(before_trans((own_ref[0], own_ref[1], own_ref[2]), facing)):
        half_ref[i] = x


def late_kernel(distance, half_ref, near_ref, far_ref, own_ref, first_ref, second_ref):
    me = place()
    core = bit(me, 1)
    into, away = unpack_second(near_ref, far_ref, core)
    trans, other_side = after_trans(half_ref[0], half_ref[1], away, into)
    same = bit(me, distance) == bit(me, 2 * distance)
    send_total(half_ref[2], other_side, trans, same, core, own_ref, first_ref, second_ref)


def prefix_kernel(distance, old_ref, near1, far1, near2, far2, new_ref):
    me = place()
    core, upper = bit(me, 1), bit(me, distance)
    facing = unpack_symmetric(near1, far1, core, 0)
    leading, mirror, right = before_trans((old_ref[0], old_ref[1], old_ref[2]), facing)
    into, away = unpack_second(near2, far2, core)
    trans, left = after_trans(leading, mirror, away, into)
    for i, x in enumerate((left, right, trans)):
        new_ref[i] = jnp.where(upper, x, old_ref[i])


def last_kernel(distance, old_ref, half_ref, near_ref, far_ref, left_ref, right_ref, trans_ref):
    me = place()
    core, upper = bit(me, 1), bit(me, distance)
    into, away = unpack_second(near_ref, far_ref, core)
    trans, left = after_trans(half_ref[0], half_ref[1], away, into)
    right_ref[0] = jnp.where(upper, half_ref[2], old_ref[1])
    trans_ref[0] = jnp.where(upper, trans, old_ref[2])
    left_ref[0] = jnp.where(upper, left, old_ref[0])


def call(kernel, products, outs, *args):
    vmem = pl.BlockSpec(memory_space=pltpu.VMEM)
    m = args[0].shape[-1]
    return pl.pallas_call(
        kernel,
        out_shape=[jax.ShapeDtypeStruct(s, F32) for s in outs],
        in_specs=[vmem] * len(args),
        out_specs=[vmem] * len(outs),
        cost_estimate=pl.CostEstimate(flops=2 * products * m**3, bytes_accessed=4 * m**2 * len(args), transcendentals=0),
        compiler_params=pltpu.CompilerParams(vmem_limit_bytes=40 * 2**20),
    )(*args)


def shards(refl_left, refl_right, trans):
    m = trans.shape[1]
    levels = lax.axis_size(AXES).bit_length() - 1
    stack = (3, m, m)
    first, second = (m // 4 + PAD, m), (m // 2 + m // 4 + PAD, m)
    sections = refl_left, refl_right, trans
    got = [swap(x, 1) for x in sections]
    section = jnp.concatenate(sections, 0)
    own, prefix, send1, send2 = call(first_kernel, 36, [stack, stack, first, second], section, *got)
    pending = None
    for level in range(1, levels):
        distance = 1 << level
        bind = lambda kernel: functools.partial(kernel, distance)
        near1, near2 = swap(send1, distance), swap(send2, distance)
        if pending is not None:
            (prefix,) = pending(prefix)
            near1, prefix = lax.optimization_barrier((near1, prefix))
        far1 = swap(near1, 1)
        if level == levels - 1:
            (halfway,) = call(early_kernel, 27, [stack], prefix, near1, far1)
            near2, halfway = lax.optimization_barrier((near2, halfway))
            far2 = swap(near2, 1)
            return tuple(call(bind(last_kernel), 9, [(1, m, m)] * 3, prefix, halfway, near2, far2))
        (halfway,) = call(early_kernel, 27, [stack], own, near1, far1)
        near2, halfway = lax.optimization_barrier((near2, halfway))
        far2 = swap(near2, 1)
        own, send1, send2 = call(bind(late_kernel), 9, [stack, first, second], halfway, near2, far2)
        pending = lambda old, kernel=bind(prefix_kernel), got=(near1, far1, near2, far2): call(kernel, 36, [stack], old, *got)


def solution(mesh):
    spec = P(AXES, None, None)
    return jax.shard_map(
        shards,
        mesh=mesh,
        in_specs=(spec,) * 3,
        out_specs=(spec,) * 3,
        check_vma=False,
    )
```

```python
import functools

import jax
import jax.numpy as jnp
from jax import lax
from jax.experimental import pallas as pl
from jax.experimental.pallas import tpu as pltpu
from jax.sharding import PartitionSpec as P

AXES = ("gx", "gy")
NS_STEPS = 5
PAD = 8
F32 = jnp.float32
BF16 = jnp.bfloat16
NN = (((1,), (0,)), ((), ()))
NT = (((1,), (1,)), ((), ()))


def swap(block, distance):
    count = lax.axis_size(AXES)
    return lax.ppermute(block, AXES, [(i, i ^ distance) for i in range(count)])


def pair(block, first, second):
    count = lax.axis_size(AXES)
    quarter = count // 4
    shift = (second - first) * quarter
    step = {first: lambda i: i + shift, second: lambda i: i - shift}
    return lax.ppermute(block, AXES, [(i, step.get(i // quarter, lambda i: i ^ 1)(i)) for i in range(count)])


def shift(block, distance):
    count = lax.axis_size(AXES)
    return lax.ppermute(block, AXES, [(i, i + distance) for i in range(count - distance)])


def after(value, *done):
    return lax.optimization_barrier((value, *done))[0]


def split(x):
    high = x.astype(BF16)
    return high, (x - high.astype(F32)).astype(BF16)


def dot1(a, b, dims=NN):
    h = a.shape[0] // 2
    parts = [lax.dot_general(x, b, dims, preferred_element_type=F32) for x in (a[:h], a[h:])]
    return jnp.concatenate(parts, 0)


def dot3(a, b, dims=NN):
    return dot1(a[0], b[0], dims) + (dot1(a[0], b[1], dims) + dot1(a[1], b[0], dims))


def half(x):
    return x.astype(BF16)


def four_steps(power):
    rest, power = power, half(power)
    for _ in range(NS_STEPS - 1):
        squared = dot1(power, power)
        power = half(squared)
        rest = rest + squared + dot1(half(rest), power)
    return half(rest)


def before_trans(own, facing):
    near, away, out = own
    f, o, s = split(facing), split(near), split(out)
    rough = dot1(f[0], o[0])
    rest = four_steps(rough)
    coupling = rough + (dot1(f[0], o[1]) + dot1(f[1], o[0]))
    inner = split(dot3(f, s, NT))
    high, low = split(coupling)
    error = half((coupling - rest.astype(F32)) + (dot1(high, rest) + dot1(low, rest)))
    leading = out + (dot1(s[0], rest) + dot1(s[1], rest))
    mirror = near + (dot1(o[0], rest) + dot1(o[1], rest))
    leading = leading + dot1(half(leading), error)
    mirror = mirror + dot1(half(mirror), error)
    return leading, mirror, away + dot3(split(leading), inner)


def after_trans(leading, mirror, away, into):
    q = split(into)
    trans = dot3(split(leading), q)
    bounced = split(dot3(split(mirror), q))
    return trans, away + dot3(split(into.T), bounced)


def place():
    return lax.axis_index("gx") * lax.axis_size("gy") + lax.axis_index("gy")


def bit(me, distance):
    return me & distance != 0


def lower_upper(h):
    row = lax.broadcasted_iota(jnp.int32, (h, h), 0)
    col = lax.broadcasted_iota(jnp.int32, (h, h), 1)
    return row > col, row < col


def pack_symmetric(x):
    h = x.shape[0] // 2
    below, above = lower_upper(h)
    a, b, c = x[:h, :h], x[:h, h:], x[h:, h:]
    diagonal = jnp.sum(jnp.where(below | above, 0.0, c), axis=0, keepdims=True)
    diagonal = jnp.broadcast_to(jnp.concatenate([diagonal, diagonal], 1), (PAD, 2 * h))
    return jnp.concatenate([b, jnp.where(above, c, a)], 1), diagonal


def unpack_symmetric(rows, diagonal):
    h = rows.shape[0]
    below, above = lower_upper(h)
    b, w = rows[:, :h], rows[:, h:]
    turned = w.T
    a = jnp.where(above, turned, w)
    c = jnp.where(above, w, jnp.where(below, turned, diagonal[:1, :h]))
    return jnp.concatenate([jnp.concatenate([a, b], 1), jnp.concatenate([b.T, c], 1)], 0)


def own_half(x, core):
    h = x.shape[0] // 2
    return jnp.where(core, x[h:], x[:h])


def joined(near, far, core):
    return jnp.concatenate([jnp.where(core, far, near), jnp.where(core, near, far)], 0)


def unpack_first(near, far, core):
    return joined(near[:-PAD], far[:-PAD], core), near[-PAD:]


def unpack_second(near, far, core):
    h = near.shape[1] // 2
    return joined(near[:h], far[:h], core), unpack_symmetric(*unpack_first(near[h:], far[h:], core))


def pack_message(facing, away, into, core, first_ref, second_ref, early_ref=None):
    rows, diagonal = pack_symmetric(facing)
    more, more_diagonal = pack_symmetric(away)
    second = jnp.concatenate([own_half(into, core), own_half(more, core), more_diagonal], 0)
    first_ref[...] = jnp.concatenate([own_half(rows, core), diagonal], 0)
    second_ref[...] = second
    if early_ref is not None:
        early_ref[...] = jnp.concatenate([rows, diagonal, second], 0)


def send_total(own_side, other_side, trans, me, distance, quarter, own_ref, *message_refs):
    core, upper = bit(me, 1), bit(me, distance)
    turned = trans.T
    if 2 * distance == quarter:
        left, right = jnp.where(upper, other_side, own_side), jnp.where(upper, own_side, other_side)
        trans = jnp.where(upper, trans, turned)
        state, message = (left, right, trans), (right, left, trans)
    else:
        same = upper == bit(me, 2 * distance)
        near, away = jnp.where(same, other_side, own_side), jnp.where(same, own_side, other_side)
        state = near, away, jnp.where(same, trans, turned)
        message = near, away, jnp.where(same, turned, trans)
    pack_message(*message, core, *message_refs)
    for i, x in enumerate(state):
        own_ref[i] = x


def first_kernel(quarter, section_ref, got1, got2, got3, prefix_ref, own_ref, *message_refs):
    me = place()
    upper = bit(me, 1)
    left, right, trans = section_ref[0], section_ref[1], section_ref[2]
    choose = lambda a, b: jnp.where(upper, a, b)
    own = choose(left, right), choose(right, left), choose(trans, trans.T)
    leading, mirror, own_side = before_trans(own, choose(got2[0], got1[0]))
    into = choose(got3[0], got3[0].T)
    through, other_side = after_trans(leading, mirror, choose(got1[0], got2[0]), into)
    send_total(own_side, other_side, through, me, 1, quarter, own_ref, *message_refs)
    prefix_ref[0] = choose(other_side, left)
    prefix_ref[1] = choose(own_side, right)
    prefix_ref[2] = choose(through, trans)


def early_kernel(distance, quarter, own_ref, near_ref, far_ref, half_ref):
    me = place()

    def body():
        facing = unpack_symmetric(*unpack_first(near_ref[...], far_ref[...], bit(me, 1)))
        for i, x in enumerate(before_trans((own_ref[0], own_ref[1], own_ref[2]), facing)):
            half_ref[i] = x

    only_group(1, me, distance, quarter, body, half_ref)


def late_kernel(distance, quarter, half_ref, near_ref, far_ref, *out_refs):
    me = place()
    core = bit(me, 1)

    def body():
        into, away = unpack_second(near_ref[...], far_ref[...], core)
        trans, other_side = after_trans(half_ref[0], half_ref[1], away, into)
        if distance == quarter:
            pack_message(half_ref[2], other_side, trans, core, *out_refs)
        else:
            send_total(half_ref[2], other_side, trans, me, distance, quarter, *out_refs)

    only_group(1, me, distance, quarter, body, *out_refs)


def only_group(group, me, distance, quarter, body, *out_refs):
    if distance != quarter:
        body()
        return
    pl.when(me // quarter == group)(body)

    @pl.when(me // quarter != group)
    def _():
        for ref in out_refs:
            ref[...] = jnp.zeros_like(ref)


def prefix_kernel(distance, quarter, old_ref, near1, far1, near2, far2, new_ref):
    me = place()
    core = bit(me, 1)
    grown = me >= quarter if distance == quarter else bit(me, distance)
    old = old_ref[0], old_ref[1], old_ref[2]
    facing = unpack_symmetric(*unpack_first(near1[...], far1[...], core))
    leading, mirror, right = before_trans(old, facing)
    into, away = unpack_second(near2[...], far2[...], core)
    trans, left = after_trans(leading, mirror, away, into)
    for i, x in enumerate((left, right, trans)):
        new_ref[i] = jnp.where(grown, x, old[i])


def last_early_kernel(quarter, own_ref, near_ref, far_ref, near_early, half_ref):
    me = place()
    picked = me // quarter == 2
    rows, diagonal = unpack_first(near_ref[...], far_ref[...], bit(me, 1))
    h = rows.shape[0]
    rows = jnp.where(picked, near_early[:h, :], rows)
    diagonal = jnp.where(picked, near_early[h : h + PAD, :], diagonal)
    for i, x in enumerate(before_trans((own_ref[0], own_ref[1], own_ref[2]), unpack_symmetric(rows, diagonal))):
        half_ref[i] = x


def last_kernel(quarter, old_ref, half_ref, near_ref, far_ref, near_early, far_early, left_ref, right_ref, trans_ref):
    me = place()
    group, cut = me // quarter, near_early.shape[0] - near_ref.shape[0]
    near = jnp.where(group == 2, near_early[cut:, :], near_ref[...])
    far = jnp.where(group == 2, far_early[cut:, :], far_ref[...])
    into, away = unpack_second(near, far, bit(me, 1))
    trans, left = after_trans(half_ref[0], half_ref[1], away, into)
    grown = group >= 2
    right_ref[0] = jnp.where(grown, half_ref[2], old_ref[1])
    trans_ref[0] = jnp.where(grown, trans, old_ref[2])
    left_ref[0] = jnp.where(grown, left, old_ref[0])


def call(kernel, products, outs, *args):
    vmem = pl.BlockSpec(memory_space=pltpu.VMEM)
    m = args[0].shape[-1]
    return pl.pallas_call(
        kernel,
        out_shape=[jax.ShapeDtypeStruct(s, F32) for s in outs],
        in_specs=[vmem] * len(args),
        out_specs=[vmem] * len(outs),
        cost_estimate=pl.CostEstimate(flops=2 * products * m**3, bytes_accessed=4 * m**2 * len(args), transcendentals=0),
        compiler_params=pltpu.CompilerParams(vmem_limit_bytes=40 * 2**20),
    )(*args)


def shards(refl_left, refl_right, trans):
    m = trans.shape[1]
    quarter = lax.axis_size(AXES) // 4
    stack, first, second = (3, m, m), (m // 4 + PAD, m), (m // 2 + m // 4 + PAD, m)
    whole = (m // 2 + PAD + second[0], m)
    sections = refl_left, refl_right, trans
    got = [swap(x, 1) for x in sections]
    section = jnp.concatenate(sections, 0)

    def message(distance):
        return [stack, first, second] + [whole] * (2 * distance == quarter)

    prefix, own, *send = call(functools.partial(first_kernel, quarter), 36, [stack] + message(1), section, *got)
    pending = None
    distance = 2
    while True:
        bind = lambda kernel: functools.partial(kernel, distance, quarter)
        move = shift if distance == quarter else swap
        near1, near2 = move(send[0], distance), move(send[1], distance)
        if distance == quarter:
            early = pair(send[2], 0, 2)
        if pending is not None:
            (prefix,) = pending(prefix)
            near1 = after(near1, prefix)
        far1 = swap(near1, 1)
        (halfway,) = call(bind(early_kernel), 27, [stack], own, near1, far1)
        near2 = after(near2, halfway)
        far2 = swap(near2, 1)
        got = near1, far1, near2, far2
        if distance == quarter:
            break
        own, *send = call(bind(late_kernel), 9, message(distance), halfway, near2, far2)
        pending = lambda old, kernel=bind(prefix_kernel), got=got: call(kernel, 36, [stack], old, *got)
        distance *= 2

    send = call(bind(late_kernel), 9, [first, second], halfway, near2, far2)
    near1, near2 = pair(send[0], 1, 3), pair(send[1], 1, 3)
    (prefix,) = call(bind(prefix_kernel), 36, [stack], after(prefix, early), *got)
    near1 = after(near1, prefix)
    far1 = swap(near1, 1)
    (halfway,) = call(functools.partial(last_early_kernel, quarter), 27, [stack], prefix, near1, far1, early)
    near2 = after(near2, halfway)
    far2 = swap(near2, 1)

    args = prefix, halfway, near2, far2, early, swap(early, 1)
    return tuple(call(functools.partial(last_kernel, quarter), 9, [(1, m, m)] * 3, *args))


def solution(mesh):
    spec = P(AXES, None, None)
    return jax.shard_map(
        shards,
        mesh=mesh,
        in_specs=(spec,) * 3,
        out_specs=(spec,) * 3,
        check_vma=False,
    )
```

```python
import functools

import jax
import jax.numpy as jnp
from jax import lax
from jax.experimental import pallas as pl
from jax.experimental.pallas import tpu as pltpu
from jax.sharding import PartitionSpec as P

AXES = ("gx", "gy")
NS_STEPS = 5
PAD = 8
F32 = jnp.float32
BF16 = jnp.bfloat16
NN = (((1,), (0,)), ((), ()))
NT = (((1,), (1,)), ((), ()))


def swap(block, distance):
    count = lax.axis_size(AXES)
    return lax.ppermute(block, AXES, [(i, i ^ distance) for i in range(count)])


def pair(block, first, second):
    count = lax.axis_size(AXES)
    quarter = count // 4
    shift = (second - first) * quarter
    step = {first: lambda i: i + shift, second: lambda i: i - shift}
    return lax.ppermute(block, AXES, [(i, step.get(i // quarter, lambda i: i ^ 1)(i)) for i in range(count)])


def split(x):
    high = x.astype(BF16)
    return high, (x - high.astype(F32)).astype(BF16)


def dot1(a, b, dims=NN):
    h = a.shape[0] // 2
    parts = [lax.dot_general(x, b, dims, preferred_element_type=F32) for x in (a[:h], a[h:])]
    return jnp.concatenate(parts, 0)


def dot3(a, b, dims=NN):
    return dot1(a[0], b[0], dims) + (dot1(a[0], b[1], dims) + dot1(a[1], b[0], dims))


def half(x):
    return x.astype(BF16)


def four_steps(power):
    rest, power = power, half(power)
    for _ in range(NS_STEPS - 1):
        squared = dot1(power, power)
        power = half(squared)
        rest = rest + squared + dot1(half(rest), power)
    return half(rest)


def before_trans(own, facing):
    near, away, out = own
    f, o, s = split(facing), split(near), split(out)
    rough = dot1(f[0], o[0])
    rest = four_steps(rough)
    coupling = rough + (dot1(f[0], o[1]) + dot1(f[1], o[0]))
    inner = split(dot3(f, s, NT))
    high, low = split(coupling)
    error = half((coupling - rest.astype(F32)) + (dot1(high, rest) + dot1(low, rest)))
    leading = out + (dot1(s[0], rest) + dot1(s[1], rest))
    mirror = near + (dot1(o[0], rest) + dot1(o[1], rest))
    leading = leading + dot1(half(leading), error)
    mirror = mirror + dot1(half(mirror), error)
    return leading, mirror, away + dot3(split(leading), inner)


def after_trans(leading, mirror, away, into):
    q = split(into)
    trans = dot3(split(leading), q)
    bounced = split(dot3(split(mirror), q))
    return trans, away + dot3(split(into.T), bounced)


def place():
    return lax.axis_index("gx") * lax.axis_size("gy") + lax.axis_index("gy")


def bit(me, distance):
    return me & distance != 0


def lower_upper(h):
    row = lax.broadcasted_iota(jnp.int32, (h, h), 0)
    col = lax.broadcasted_iota(jnp.int32, (h, h), 1)
    return row > col, row < col


def pack_symmetric(x, core, ref, start):
    h = x.shape[0] // 2
    q = h // 2
    below, above = lower_upper(h)
    a, b, c = x[:h, :h], x[:h, h:], x[h:, h:]
    diagonal = jnp.sum(jnp.where(below | above, 0.0, c), axis=0, keepdims=True)
    both = jnp.concatenate([b, jnp.where(above, c, a)], 1)
    ref[start : start + q, :] = jnp.where(core, both[q:], both[:q])
    diagonal = jnp.concatenate([diagonal, diagonal], 1)
    ref[start + q : start + q + PAD, :] = jnp.broadcast_to(diagonal, (PAD, 2 * h))


def joined(near_ref, far_ref, core, lo, hi):
    near, far = near_ref[lo:hi, :], far_ref[lo:hi, :]
    return jnp.concatenate([jnp.where(core, far, near), jnp.where(core, near, far)], 0)


def unpack_symmetric(near_ref, far_ref, core, start):
    h = near_ref.shape[1] // 2
    q = h // 2
    below, above = lower_upper(h)
    both = joined(near_ref, far_ref, core, start, start + q)
    diagonal = near_ref[start + q : start + q + 1, :h]
    b, w = both[:, :h], both[:, h:]
    turned = w.T
    a = jnp.where(above, turned, w)
    c = jnp.where(above, w, jnp.where(below, turned, diagonal))
    return jnp.concatenate([jnp.concatenate([a, b], 1), jnp.concatenate([b.T, c], 1)], 0)


def unpack_second(near_ref, far_ref, core):
    h = near_ref.shape[1] // 2
    return joined(near_ref, far_ref, core, 0, h), unpack_symmetric(near_ref, far_ref, core, h)


def send_total(own_side, other_side, trans, same, core, first_ref, second_ref, own_ref):
    turned = trans.T
    near = jnp.where(same, other_side, own_side)
    away = jnp.where(same, own_side, other_side)
    back = jnp.where(same, turned, trans)
    own_ref[0] = near
    own_ref[1] = away
    own_ref[2] = jnp.where(same, trans, turned)
    pack_symmetric(near, core, first_ref, 0)
    pack_second(back, away, core, second_ref)


def first_kernel(section_ref, got1, got2, got3, prefix_ref, *send_refs):
    me = place()
    upper = bit(me, 1)
    left, right, trans = section_ref[0], section_ref[1], section_ref[2]
    pick = lambda a, b: jnp.where(upper, a, b)
    own = pick(left, right), pick(right, left), pick(trans, trans.T)
    leading, mirror, own_side = before_trans(own, pick(got2[0], got1[0]))
    into = pick(got3[0], got3[0].T)
    through, other_side = after_trans(leading, mirror, pick(got1[0], got2[0]), into)
    send_total(own_side, other_side, through, upper == bit(me, 2), upper, *send_refs)
    prefix_ref[0] = pick(other_side, left)
    prefix_ref[1] = pick(own_side, right)
    prefix_ref[2] = pick(through, trans)


def early_kernel(own_ref, near_ref, far_ref, half_ref, *first_ref):
    core = bit(place(), 1)
    facing = unpack_symmetric(near_ref, far_ref, core, 0)
    half = before_trans((own_ref[0], own_ref[1], own_ref[2]), facing)
    for ref in first_ref:
        pack_symmetric(half[2], core, ref, 0)
    for i, x in enumerate(half):
        half_ref[i] = x


def final_kernel(half_ref, near_ref, far_ref, second_ref):
    core = bit(place(), 1)
    into, away = unpack_second(near_ref, far_ref, core)
    trans, other_side = after_trans(half_ref[0], half_ref[1], away, into)
    pack_second(trans, other_side, core, second_ref)


def pack_second(back, away, core, ref):
    h = back.shape[0] // 2
    ref[0:h, :] = jnp.where(core, back[h:], back[:h])
    pack_symmetric(away, core, ref, h)


def late_kernel(distance, half_ref, near_ref, far_ref, *send_refs):
    me = place()
    core = bit(me, 1)
    into, away = unpack_second(near_ref, far_ref, core)
    trans, other_side = after_trans(half_ref[0], half_ref[1], away, into)
    same = bit(me, distance) == bit(me, 2 * distance)
    send_total(half_ref[2], other_side, trans, same, core, *send_refs)


def prefix_kernel(distance, old_ref, near1, far1, near2, far2, new_ref):
    me = place()
    core, upper = bit(me, 1), bit(me, distance)
    facing = unpack_symmetric(near1, far1, core, 0)
    leading, mirror, right = before_trans((old_ref[0], old_ref[1], old_ref[2]), facing)
    into, away = unpack_second(near2, far2, core)
    trans, left = after_trans(leading, mirror, away, into)
    for i, x in enumerate((left, right, trans)):
        new_ref[i] = jnp.where(upper, x, old_ref[i])


def by_third(distance, me, near2, far2, near3, far3):
    third = bit(me, distance // 2)
    return jnp.where(third, near3[...], near2[...]), jnp.where(third, far3[...], far2[...])


def last_early_kernel(distance, own_ref, near2, far2, near3, far3, half_ref):
    me = place()
    facing = unpack_symmetric(*by_third(distance, me, near2, far2, near3, far3), bit(me, 1), 0)
    for i, x in enumerate(before_trans((own_ref[0], own_ref[1], own_ref[2]), facing)):
        half_ref[i] = x


def last_kernel(distance, old_ref, half_ref, near2, far2, near3, far3, left_ref, right_ref, trans_ref):
    me = place()
    upper = bit(me, distance)
    into, away = unpack_second(*by_third(distance, me, near2, far2, near3, far3), bit(me, 1))
    trans, left = after_trans(half_ref[0], half_ref[1], away, into)
    right_ref[0] = jnp.where(upper, half_ref[2], old_ref[1])
    trans_ref[0] = jnp.where(upper, trans, old_ref[2])
    left_ref[0] = jnp.where(upper, left, old_ref[0])


def call(kernel, products, outs, *args):
    vmem = pl.BlockSpec(memory_space=pltpu.VMEM)
    m = args[0].shape[-1]
    return pl.pallas_call(
        kernel,
        out_shape=[jax.ShapeDtypeStruct(s, F32) for s in outs],
        in_specs=[vmem] * len(args),
        out_specs=[vmem] * len(outs),
        cost_estimate=pl.CostEstimate(flops=2 * products * m**3, bytes_accessed=4 * m**2 * len(args), transcendentals=0),
        compiler_params=pltpu.CompilerParams(vmem_limit_bytes=40 * 2**20),
    )(*args)


def shards(refl_left, refl_right, trans):
    m = trans.shape[1]
    levels = lax.axis_size(AXES).bit_length() - 1
    stack = (3, m, m)
    first, second = (m // 4 + PAD, m), (m // 2 + m // 4 + PAD, m)
    sections = refl_left, refl_right, trans
    got = [swap(x, 1) for x in sections]
    section = jnp.concatenate(sections, 0)
    prefix, send1, send2, own = call(first_kernel, 36, [stack, first, second, stack], section, *got)
    pending = None
    for level in range(1, levels - 1):
        distance = 1 << level
        bind = lambda kernel: functools.partial(kernel, distance)
        near1, near2 = swap(send1, distance), swap(send2, distance)
        if pending is not None:
            (prefix,) = pending(prefix)
            near1, prefix = lax.optimization_barrier((near1, prefix))
        far1 = swap(near1, 1)
        outs = [stack] + [first] * (level == levels - 2)
        halfway, *sends = call(early_kernel, 27, outs, own, near1, far1)
        near2, halfway = lax.optimization_barrier((near2, halfway))
        far2 = swap(near2, 1)
        pending = lambda old, kernel=bind(prefix_kernel), got=(near1, far1, near2, far2): call(kernel, 36, [stack], old, *got)
        if level < levels - 2:
            send1, send2, own = call(bind(late_kernel), 9, [first, second, stack], halfway, near2, far2)

    distance *= 2
    (send1,) = sends
    first3, first2 = pair(send1, 1, 3), pair(send1, 1, 2)
    (send2,) = call(final_kernel, 9, [second], halfway, near2, far2)
    near3, near2 = pair(send2, 1, 3), pair(send2, 1, 2)
    first3, first2, prefix = lax.optimization_barrier((first3, first2, prefix))
    (prefix,) = pending(prefix)
    args = prefix, first2, swap(first2, 1), first3, swap(first3, 1)
    (halfway,) = call(functools.partial(last_early_kernel, distance), 27, [stack], *args)
    near2, near3, halfway = lax.optimization_barrier((near2, near3, halfway))
    args = prefix, halfway, near2, swap(near2, 1), near3, swap(near3, 1)
    return tuple(call(functools.partial(last_kernel, distance), 9, [(1, m, m)] * 3, *args))


def solution(mesh):
    spec = P(AXES, None, None)
    return jax.shard_map(
        shards,
        mesh=mesh,
        in_specs=(spec,) * 3,
        out_specs=(spec,) * 3,
        check_vma=False,
    )
```

```python
import functools

import jax
import jax.numpy as jnp
from jax import lax
from jax.experimental import pallas as pl
from jax.experimental.pallas import tpu as pltpu
from jax.sharding import PartitionSpec as P

AXES = ("gx", "gy")
NS_STEPS = 5
PAD = 8
F32 = jnp.float32
BF16 = jnp.bfloat16
NN = (((1,), (0,)), ((), ()))
NT = (((1,), (1,)), ((), ()))


def swap(block, distance):
    count = lax.axis_size(AXES)
    return lax.ppermute(block, AXES, [(i, i ^ distance) for i in range(count)])


def pair(block, first, second):
    count = lax.axis_size(AXES)
    quarter = count // 4
    shift = (second - first) * quarter
    step = {first: lambda i: i + shift, second: lambda i: i - shift}
    return lax.ppermute(block, AXES, [(i, step.get(i // quarter, lambda i: i ^ 1)(i)) for i in range(count)])


def split(x):
    high = x.astype(BF16)
    return high, (x - high.astype(F32)).astype(BF16)


def dot1(a, b, dims=NN):
    h = a.shape[0] // 2
    parts = [lax.dot_general(x, b, dims, preferred_element_type=F32) for x in (a[:h], a[h:])]
    return jnp.concatenate(parts, 0)


def dot3(a, b, dims=NN):
    return dot1(a[0], b[0], dims) + (dot1(a[0], b[1], dims) + dot1(a[1], b[0], dims))


def half(x):
    return x.astype(BF16)


def four_steps(power):
    rest, power = power, half(power)
    for _ in range(NS_STEPS - 1):
        squared = dot1(power, power)
        power = half(squared)
        rest = rest + squared + dot1(half(rest), power)
    return half(rest)


def before_trans(own, facing):
    near, away, out = own
    f, o, s = split(facing), split(near), split(out)
    rough = dot1(f[0], o[0])
    rest = four_steps(rough)
    coupling = rough + (dot1(f[0], o[1]) + dot1(f[1], o[0]))
    inner = split(dot3(f, s, NT))
    high, low = split(coupling)
    error = half((coupling - rest.astype(F32)) + (dot1(high, rest) + dot1(low, rest)))
    leading = out + (dot1(s[0], rest) + dot1(s[1], rest))
    mirror = near + (dot1(o[0], rest) + dot1(o[1], rest))
    leading = leading + dot1(half(leading), error)
    mirror = mirror + dot1(half(mirror), error)
    return leading, mirror, away + dot3(split(leading), inner)


def after_trans(leading, mirror, away, into):
    q = split(into)
    trans = dot3(split(leading), q)
    bounced = split(dot3(split(mirror), q))
    return trans, away + dot3(split(into.T), bounced)


def place():
    return lax.axis_index("gx") * lax.axis_size("gy") + lax.axis_index("gy")


def bit(me, distance):
    return me & distance != 0


def lower_upper(h):
    row = lax.broadcasted_iota(jnp.int32, (h, h), 0)
    col = lax.broadcasted_iota(jnp.int32, (h, h), 1)
    return row > col, row < col


def pack_symmetric(x, core, ref, start):
    h = x.shape[0] // 2
    q = h // 2
    below, above = lower_upper(h)
    a, b, c = x[:h, :h], x[:h, h:], x[h:, h:]
    diagonal = jnp.sum(jnp.where(below | above, 0.0, c), axis=0, keepdims=True)
    both = jnp.concatenate([b, jnp.where(above, c, a)], 1)
    ref[start : start + q, :] = jnp.where(core, both[q:], both[:q])
    diagonal = jnp.concatenate([diagonal, diagonal], 1)
    ref[start + q : start + q + PAD, :] = jnp.broadcast_to(diagonal, (PAD, 2 * h))


def joined(near_ref, far_ref, core, lo, hi):
    near, far = near_ref[lo:hi, :], far_ref[lo:hi, :]
    return jnp.concatenate([jnp.where(core, far, near), jnp.where(core, near, far)], 0)


def unpack_symmetric(near_ref, far_ref, core, start):
    h = near_ref.shape[1] // 2
    q = h // 2
    below, above = lower_upper(h)
    both = joined(near_ref, far_ref, core, start, start + q)
    diagonal = near_ref[start + q : start + q + 1, :h]
    b, w = both[:, :h], both[:, h:]
    turned = w.T
    a = jnp.where(above, turned, w)
    c = jnp.where(above, w, jnp.where(below, turned, diagonal))
    return jnp.concatenate([jnp.concatenate([a, b], 1), jnp.concatenate([b.T, c], 1)], 0)


def unpack_second(near_ref, far_ref, core):
    h = near_ref.shape[1] // 2
    return joined(near_ref, far_ref, core, 0, h), unpack_symmetric(near_ref, far_ref, core, h)


def send_total(own_side, other_side, trans, same, core, first_ref, second_ref, own_ref):
    turned = trans.T
    near = jnp.where(same, other_side, own_side)
    away = jnp.where(same, own_side, other_side)
    back = jnp.where(same, turned, trans)
    own_ref[0] = near
    own_ref[1] = away
    own_ref[2] = jnp.where(same, trans, turned)
    pack_symmetric(near, core, first_ref, 0)
    pack_second(back, away, core, second_ref)


def first_kernel(section_ref, got1, got2, got3, prefix_ref, *send_refs):
    me = place()
    upper = bit(me, 1)
    left, right, trans = section_ref[0], section_ref[1], section_ref[2]
    pick = lambda a, b: jnp.where(upper, a, b)
    own = pick(left, right), pick(right, left), pick(trans, trans.T)
    leading, mirror, own_side = before_trans(own, pick(got2[0], got1[0]))
    into = pick(got3[0], got3[0].T)
    through, other_side = after_trans(leading, mirror, pick(got1[0], got2[0]), into)
    send_total(own_side, other_side, through, upper == bit(me, 2), upper, *send_refs)
    prefix_ref[0] = pick(other_side, left)
    prefix_ref[1] = pick(own_side, right)
    prefix_ref[2] = pick(through, trans)


def early_kernel(own_ref, near_ref, far_ref, half_ref, *first_ref):
    core = bit(place(), 1)
    facing = unpack_symmetric(near_ref, far_ref, core, 0)
    half = before_trans((own_ref[0], own_ref[1], own_ref[2]), facing)
    for ref in first_ref:
        pack_symmetric(half[2], core, ref, 0)
    for i, x in enumerate(half):
        half_ref[i] = x


def final_kernel(half_ref, near_ref, far_ref, second_ref):
    core = bit(place(), 1)
    into, away = unpack_second(near_ref, far_ref, core)
    trans, other_side = after_trans(half_ref[0], half_ref[1], away, into)
    pack_second(trans, other_side, core, second_ref)


def pack_second(back, away, core, ref):
    h = back.shape[0] // 2
    ref[0:h, :] = jnp.where(core, back[h:], back[:h])
    pack_symmetric(away, core, ref, h)


def late_kernel(distance, half_ref, near_ref, far_ref, *send_refs):
    me = place()
    core = bit(me, 1)
    into, away = unpack_second(near_ref, far_ref, core)
    trans, other_side = after_trans(half_ref[0], half_ref[1], away, into)
    same = bit(me, distance) == bit(me, 2 * distance)
    send_total(half_ref[2], other_side, trans, same, core, *send_refs)


def prefix_kernel(distance, old_ref, near1, far1, near2, far2, new_ref):
    me = place()
    core, upper = bit(me, 1), bit(me, distance)
    facing = unpack_symmetric(near1, far1, core, 0)
    leading, mirror, right = before_trans((old_ref[0], old_ref[1], old_ref[2]), facing)
    into, away = unpack_second(near2, far2, core)
    trans, left = after_trans(leading, mirror, away, into)
    for i, x in enumerate((left, right, trans)):
        new_ref[i] = jnp.where(upper, x, old_ref[i])


def by_third(distance, me, near2, far2, near3, far3):
    third = bit(me, distance // 2)
    return jnp.where(third, near3[...], near2[...]), jnp.where(third, far3[...], far2[...])


def last_early_kernel(distance, old_ref, near2, far2, near3, far3, half_ref, right_ref):
    me = place()
    right_ref[0] = old_ref[1]

    @pl.when(bit(me, distance))
    def _():
        facing = unpack_symmetric(*by_third(distance, me, near2, far2, near3, far3), bit(me, 1), 0)
        leading, mirror, right = before_trans((old_ref[0], old_ref[1], old_ref[2]), facing)
        half_ref[0] = leading
        half_ref[1] = mirror
        right_ref[0] = right


def last_kernel(distance, old_ref, half_ref, near2, far2, near3, far3, left_out, trans_out, left_ref, trans_ref, sems):
    me = place()
    upper = bit(me, distance)
    left_copy = pltpu.make_async_copy(left_ref, left_out, sems.at[0])
    trans_copy = pltpu.make_async_copy(trans_ref, trans_out, sems.at[1])

    @pl.when(upper)
    def _():
        into, away = unpack_second(*by_third(distance, me, near2, far2, near3, far3), bit(me, 1))
        q = split(into)
        trans_ref[0] = dot3(split(half_ref[0]), q)
        trans_copy.start()
        bounced = split(dot3(split(half_ref[1]), q))
        left_ref[0] = away + dot3(split(into.T), bounced)
        left_copy.start()

    @pl.when(jnp.logical_not(upper))
    def _():
        trans_ref[0] = old_ref[2]
        trans_copy.start()
        left_ref[0] = old_ref[0]
        left_copy.start()

    trans_copy.wait()
    left_copy.wait()


def call(kernel, products, outs, *args, out_space=pltpu.VMEM, scratch=()):
    vmem = pl.BlockSpec(memory_space=pltpu.VMEM)
    m = args[0].shape[-1]
    return pl.pallas_call(
        kernel,
        out_shape=[jax.ShapeDtypeStruct(s, F32) for s in outs],
        in_specs=[vmem] * len(args),
        out_specs=[pl.BlockSpec(memory_space=out_space)] * len(outs),
        scratch_shapes=scratch,
        cost_estimate=pl.CostEstimate(flops=2 * products * m**3, bytes_accessed=4 * m**2 * len(args), transcendentals=0),
        compiler_params=pltpu.CompilerParams(vmem_limit_bytes=40 * 2**20),
    )(*args)


def shards(refl_left, refl_right, trans):
    m = trans.shape[1]
    levels = lax.axis_size(AXES).bit_length() - 1
    stack = (3, m, m)
    first, second = (m // 4 + PAD, m), (m // 2 + m // 4 + PAD, m)
    sections = refl_left, refl_right, trans
    got = [swap(x, 1) for x in sections]
    section = jnp.concatenate(sections, 0)
    prefix, send1, send2, own = call(first_kernel, 36, [stack, first, second, stack], section, *got)
    pending = None
    for level in range(1, levels - 1):
        distance = 1 << level
        bind = lambda kernel: functools.partial(kernel, distance)
        near1, near2 = swap(send1, distance), swap(send2, distance)
        if pending is not None:
            (prefix,) = pending(prefix)
            near1, prefix = lax.optimization_barrier((near1, prefix))
        far1 = swap(near1, 1)
        outs = [stack] + [first] * (level == levels - 2)
        halfway, *sends = call(early_kernel, 27, outs, own, near1, far1)
        near2, halfway = lax.optimization_barrier((near2, halfway))
        far2 = swap(near2, 1)
        pending = lambda old, kernel=bind(prefix_kernel), got=(near1, far1, near2, far2): call(kernel, 36, [stack], old, *got)
        if level < levels - 2:
            send1, send2, own = call(bind(late_kernel), 9, [first, second, stack], halfway, near2, far2)

    distance *= 2
    (send1,) = sends
    first3, first2 = pair(send1, 1, 3), pair(send1, 1, 2)
    (send2,) = call(final_kernel, 9, [second], halfway, near2, far2)
    near3, near2 = pair(send2, 1, 3), pair(send2, 1, 2)
    first3, first2, prefix = lax.optimization_barrier((first3, first2, prefix))
    (prefix,) = pending(prefix)
    args = prefix, first2, swap(first2, 1), first3, swap(first3, 1)
    outs = [(2, m, m), (1, m, m)]
    halfway, right = call(functools.partial(last_early_kernel, distance), 27, outs, *args)
    near3, halfway = lax.optimization_barrier((near3, halfway))
    far3 = swap(near3, 1)
    near2, far3 = lax.optimization_barrier((near2, far3))
    args = prefix, halfway, near2, swap(near2, 1), near3, far3
    one = (1, m, m)
    scratch = [pltpu.VMEM(one, F32), pltpu.VMEM(one, F32), pltpu.SemaphoreType.DMA((2,))]
    kernel = functools.partial(last_kernel, distance)
    left, trans = call(kernel, 9, [one, one], *args, out_space=pltpu.HBM, scratch=scratch)
    return left, right, trans


def solution(mesh):
    spec = P(AXES, None, None)
    return jax.shard_map(
        shards,
        mesh=mesh,
        in_specs=(spec,) * 3,
        out_specs=(spec,) * 3,
        check_vma=False,
    )
```

```python
import functools

import jax
import jax.numpy as jnp
from jax import lax
from jax.experimental import pallas as pl
from jax.experimental.pallas import tpu as pltpu
from jax.sharding import PartitionSpec as P

AXES = ("gx", "gy")
NS_STEPS = 5
PAD = 8
F32 = jnp.float32
BF16 = jnp.bfloat16
NN = (((1,), (0,)), ((), ()))
NT = (((1,), (1,)), ((), ()))


def swap(block, distance):
    count = lax.axis_size(AXES)
    return lax.ppermute(block, AXES, [(i, i ^ distance) for i in range(count)])


def pair(block, first, second):
    count = lax.axis_size(AXES)
    quarter = count // 4
    shift = (second - first) * quarter
    step = {first: lambda i: i + shift, second: lambda i: i - shift}
    return lax.ppermute(block, AXES, [(i, step.get(i // quarter, lambda i: i ^ 1)(i)) for i in range(count)])


def split(x):
    high = x.astype(BF16)
    return high, (x - high.astype(F32)).astype(BF16)


def dot1(a, b, dims=NN):
    h = a.shape[0] // 2
    parts = [lax.dot_general(x, b, dims, preferred_element_type=F32) for x in (a[:h], a[h:])]
    return jnp.concatenate(parts, 0)


def dot3(a, b, dims=NN):
    return dot1(a[0], b[0], dims) + (dot1(a[0], b[1], dims) + dot1(a[1], b[0], dims))


def half(x):
    return x.astype(BF16)


def four_steps(power):
    rest, power = power, half(power)
    for _ in range(NS_STEPS - 1):
        squared = dot1(power, power)
        power = half(squared)
        rest = rest + squared + dot1(half(rest), power)
    return half(rest)


def before_trans(own, facing):
    near, away, out = own
    f, o, s = split(facing), split(near), split(out)
    rough = dot1(f[0], o[0])
    rest = four_steps(rough)
    coupling = rough + (dot1(f[0], o[1]) + dot1(f[1], o[0]))
    inner = split(dot3(f, s, NT))
    high, low = split(coupling)
    error = half((coupling - rest.astype(F32)) + (dot1(high, rest) + dot1(low, rest)))
    leading = out + (dot1(s[0], rest) + dot1(s[1], rest))
    mirror = near + (dot1(o[0], rest) + dot1(o[1], rest))
    leading = leading + dot1(half(leading), error)
    mirror = mirror + dot1(half(mirror), error)
    return leading, mirror, away + dot3(split(leading), inner)


def after_trans(leading, mirror, away, into):
    q = split(into)
    trans = dot3(split(leading), q)
    bounced = split(dot3(split(mirror), q))
    return trans, away + dot3(split(into.T), bounced)


def place():
    return lax.axis_index("gx") * lax.axis_size("gy") + lax.axis_index("gy")


def bit(me, distance):
    return me & distance != 0


def lower_upper(h):
    row = lax.broadcasted_iota(jnp.int32, (h, h), 0)
    col = lax.broadcasted_iota(jnp.int32, (h, h), 1)
    return row > col, row < col


def pack_symmetric(x, core, ref, start):
    h = x.shape[0] // 2
    q = h // 2
    below, above = lower_upper(h)
    a, b, c = x[:h, :h], x[:h, h:], x[h:, h:]
    diagonal = jnp.sum(jnp.where(below | above, 0.0, c), axis=0, keepdims=True)
    both = jnp.concatenate([b, jnp.where(above, c, a)], 1)
    ref[start : start + q, :] = jnp.where(core, both[q:], both[:q])
    diagonal = jnp.concatenate([diagonal, diagonal], 1)
    ref[start + q : start + q + PAD, :] = jnp.broadcast_to(diagonal, (PAD, 2 * h))


def joined(near_ref, far_ref, core, lo, hi):
    near, far = near_ref[lo:hi, :], far_ref[lo:hi, :]
    return jnp.concatenate([jnp.where(core, far, near), jnp.where(core, near, far)], 0)


def unpack_symmetric(near_ref, far_ref, core, start):
    h = near_ref.shape[1] // 2
    q = h // 2
    below, above = lower_upper(h)
    both = joined(near_ref, far_ref, core, start, start + q)
    diagonal = near_ref[start + q : start + q + 1, :h]
    b, w = both[:, :h], both[:, h:]
    turned = w.T
    a = jnp.where(above, turned, w)
    c = jnp.where(above, w, jnp.where(below, turned, diagonal))
    return jnp.concatenate([jnp.concatenate([a, b], 1), jnp.concatenate([b.T, c], 1)], 0)


def unpack_second(near_ref, far_ref, core):
    h = near_ref.shape[1] // 2
    return joined(near_ref, far_ref, core, 0, h), unpack_symmetric(near_ref, far_ref, core, h)


def send_total(own_side, other_side, trans, same, core, first_ref, second_ref, own_ref):
    turned = trans.T
    near = jnp.where(same, other_side, own_side)
    away = jnp.where(same, own_side, other_side)
    back = jnp.where(same, turned, trans)
    own_ref[0] = near
    own_ref[1] = away
    own_ref[2] = jnp.where(same, trans, turned)
    pack_symmetric(near, core, first_ref, 0)
    pack_second(back, away, core, second_ref)


def first_kernel(section_ref, got1, got2, got3, prefix_ref, *send_refs):
    me = place()
    upper = bit(me, 1)
    left, right, trans = section_ref[0], section_ref[1], section_ref[2]
    pick = lambda a, b: jnp.where(upper, a, b)
    own = pick(left, right), pick(right, left), pick(trans, trans.T)
    leading, mirror, own_side = before_trans(own, pick(got2[0], got1[0]))
    into = pick(got3[0], got3[0].T)
    through, other_side = after_trans(leading, mirror, pick(got1[0], got2[0]), into)
    send_total(own_side, other_side, through, upper == bit(me, 2), upper, *send_refs)
    prefix_ref[0] = pick(other_side, left)
    prefix_ref[1] = pick(own_side, right)
    prefix_ref[2] = pick(through, trans)


def early_kernel(own_ref, near_ref, far_ref, half_ref, *first_ref):
    core = bit(place(), 1)
    facing = unpack_symmetric(near_ref, far_ref, core, 0)
    half = before_trans((own_ref[0], own_ref[1], own_ref[2]), facing)
    for ref in first_ref:
        pack_symmetric(half[2], core, ref, 0)
    for i, x in enumerate(half):
        half_ref[i] = x


def final_kernel(distance, half_ref, near_ref, far_ref, second_ref):
    me = place()
    core, upper = bit(me, 1), bit(me, distance)
    into, away = unpack_second(near_ref, far_ref, core)
    trans, other_side = after_trans(half_ref[0], half_ref[1], away, into)
    left = jnp.where(upper, other_side, half_ref[2])
    pack_second(jnp.where(upper, trans, trans.T), left, core, second_ref)


def pack_second(back, away, core, ref):
    h = back.shape[0] // 2
    ref[0:h, :] = jnp.where(core, back[h:], back[:h])
    pack_symmetric(away, core, ref, h)


def late_kernel(distance, half_ref, near_ref, far_ref, *send_refs):
    me = place()
    core = bit(me, 1)
    into, away = unpack_second(near_ref, far_ref, core)
    trans, other_side = after_trans(half_ref[0], half_ref[1], away, into)
    same = bit(me, distance) == bit(me, 2 * distance)
    send_total(half_ref[2], other_side, trans, same, core, *send_refs)


def prefix_kernel(distance, old_ref, near1, far1, near2, far2, new_ref):
    me = place()
    core, upper = bit(me, 1), bit(me, distance)
    facing = unpack_symmetric(near1, far1, core, 0)
    leading, mirror, right = before_trans((old_ref[0], old_ref[1], old_ref[2]), facing)
    into, away = unpack_second(near2, far2, core)
    trans, left = after_trans(leading, mirror, away, into)
    for i, x in enumerate((left, right, trans)):
        new_ref[i] = jnp.where(upper, x, old_ref[i])


def by_third(distance, me, near2, far2, near3, far3):
    third = bit(me, distance // 2)
    return jnp.where(third, near3[...], near2[...]), jnp.where(third, far3[...], far2[...])


def last_early_kernel(distance, old_ref, near2, far2, near3, far3, half_ref):
    me = place()

    @pl.when(bit(me, distance))
    def _():
        facing = unpack_symmetric(*by_third(distance, me, near2, far2, near3, far3), bit(me, 1), 0)
        for i, x in enumerate(before_trans((old_ref[0], old_ref[1], old_ref[2]), facing)):
            half_ref[i] = x


def last_kernel(distance, old_ref, half_ref, near_ref, far_ref, left_out, right_out, trans_out, new_ref, sems):
    me = place()
    upper = bit(me, distance)
    left_copy = pltpu.make_async_copy(new_ref.at[0:1], left_out, sems.at[0])
    trans_copy = pltpu.make_async_copy(new_ref.at[2:3], trans_out, sems.at[1])
    right_copy = pltpu.make_async_copy(new_ref.at[1:2], right_out, sems.at[2])
    new_ref[1] = jnp.where(upper, half_ref[2], old_ref[1])
    right_copy.start()

    @pl.when(upper)
    def _():
        into, away = unpack_second(near_ref, far_ref, bit(me, 1))
        q = split(into)
        new_ref[2] = dot3(split(half_ref[0]), q)
        trans_copy.start()
        bounced = split(dot3(split(half_ref[1]), q))
        new_ref[0] = away + dot3(split(into.T), bounced)
        left_copy.start()

    @pl.when(jnp.logical_not(upper))
    def _():
        new_ref[2] = old_ref[2]
        trans_copy.start()
        new_ref[0] = old_ref[0]
        left_copy.start()

    right_copy.wait()
    trans_copy.wait()
    left_copy.wait()


def call(kernel, products, outs, *args, out_space=pltpu.VMEM, scratch=()):
    vmem = pl.BlockSpec(memory_space=pltpu.VMEM)
    m = args[0].shape[-1]
    return pl.pallas_call(
        kernel,
        out_shape=[jax.ShapeDtypeStruct(s, F32) for s in outs],
        in_specs=[vmem] * len(args),
        out_specs=[pl.BlockSpec(memory_space=out_space)] * len(outs),
        scratch_shapes=scratch,
        cost_estimate=pl.CostEstimate(flops=2 * products * m**3, bytes_accessed=4 * m**2 * len(args), transcendentals=0),
        compiler_params=pltpu.CompilerParams(vmem_limit_bytes=40 * 2**20),
    )(*args)


def shards(refl_left, refl_right, trans):
    m = trans.shape[1]
    levels = lax.axis_size(AXES).bit_length() - 1
    stack = (3, m, m)
    first, second = (m // 4 + PAD, m), (m // 2 + m // 4 + PAD, m)
    sections = refl_left, refl_right, trans
    got = [swap(x, 1) for x in sections]
    section = jnp.concatenate(sections, 0)
    prefix, send1, send2, own = call(first_kernel, 36, [stack, first, second, stack], section, *got)
    pending = None
    for level in range(1, levels - 1):
        distance = 1 << level
        bind = lambda kernel: functools.partial(kernel, distance)
        near1, near2 = swap(send1, distance), swap(send2, distance)
        if pending is not None:
            (prefix,) = pending(prefix)
            near1, prefix = lax.optimization_barrier((near1, prefix))
        far1 = swap(near1, 1)
        outs = [stack] + [first] * (level == levels - 2)
        halfway, *sends = call(early_kernel, 27, outs, own, near1, far1)
        near2, halfway = lax.optimization_barrier((near2, halfway))
        far2 = swap(near2, 1)
        pending = lambda old, kernel=bind(prefix_kernel), got=(near1, far1, near2, far2): call(kernel, 36, [stack], old, *got)
        if level < levels - 2:
            send1, send2, own = call(bind(late_kernel), 9, [first, second, stack], halfway, near2, far2)

    (send1,) = sends
    first3, first2 = pair(send1, 1, 3), pair(send1, 1, 2)
    (send2,) = call(bind(final_kernel), 9, [second], halfway, near2, far2)
    distance *= 2
    near2 = swap(send2, distance)
    first3, first2, prefix = lax.optimization_barrier((first3, first2, prefix))
    (prefix,) = pending(prefix)
    args = prefix, first2, swap(first2, 1), first3, swap(first3, 1)
    (halfway,) = call(functools.partial(last_early_kernel, distance), 27, [stack], *args)
    near2, halfway = lax.optimization_barrier((near2, halfway))
    args = prefix, halfway, near2, swap(near2, 1)
    scratch = [pltpu.VMEM(stack, F32), pltpu.SemaphoreType.DMA((3,))]
    kernel = functools.partial(last_kernel, distance)
    return tuple(call(kernel, 9, [(1, m, m)] * 3, *args, out_space=pltpu.HBM, scratch=scratch))


def solution(mesh):
    spec = P(AXES, None, None)
    return jax.shard_map(
        shards,
        mesh=mesh,
        in_specs=(spec,) * 3,
        out_specs=(spec,) * 3,
        check_vma=False,
    )
```

```python
import functools

import jax
import jax.numpy as jnp
from jax import lax
from jax.experimental import pallas as pl
from jax.experimental.pallas import tpu as pltpu
from jax.sharding import PartitionSpec as P

AXES = ("gx", "gy")
NS_STEPS = 5
PAD = 8
F32 = jnp.float32
BF16 = jnp.bfloat16
NN = (((1,), (0,)), ((), ()))
NT = (((1,), (1,)), ((), ()))


def swap(block, distance):
    count = lax.axis_size(AXES)
    return lax.ppermute(block, AXES, [(i, i ^ distance) for i in range(count)])


def pair(block, first, second):
    count = lax.axis_size(AXES)
    quarter = count // 4
    shift = (second - first) * quarter
    step = {first: lambda i: i + shift, second: lambda i: i - shift}
    return lax.ppermute(block, AXES, [(i, step.get(i // quarter, lambda i: i ^ 1)(i)) for i in range(count)])


def give(block, first, second):
    quarter = lax.axis_size(AXES) // 4
    return lax.ppermute(block, AXES, [(first * quarter + i, second * quarter + i) for i in range(quarter)])


def split(x):
    high = x.astype(BF16)
    return high, (x - high.astype(F32)).astype(BF16)


def dot1(a, b, dims=NN):
    h = a.shape[0] // 2
    parts = [lax.dot_general(x, b, dims, preferred_element_type=F32) for x in (a[:h], a[h:])]
    return jnp.concatenate(parts, 0)


def dot3(a, b, dims=NN):
    return dot1(a[0], b[0], dims) + (dot1(a[0], b[1], dims) + dot1(a[1], b[0], dims))


def half(x):
    return x.astype(BF16)


def four_steps(power):
    rest, power = power, half(power)
    for _ in range(NS_STEPS - 1):
        squared = dot1(power, power)
        power = half(squared)
        rest = rest + squared + dot1(half(rest), power)
    return half(rest)


def before_trans(own, facing):
    near, away, out = own
    f, o, s = split(facing), split(near), split(out)
    rough = dot1(f[0], o[0])
    rest = four_steps(rough)
    coupling = rough + (dot1(f[0], o[1]) + dot1(f[1], o[0]))
    inner = split(dot3(f, s, NT))
    high, low = split(coupling)
    error = half((coupling - rest.astype(F32)) + (dot1(high, rest) + dot1(low, rest)))
    leading = out + (dot1(s[0], rest) + dot1(s[1], rest))
    mirror = near + (dot1(o[0], rest) + dot1(o[1], rest))
    leading = leading + dot1(half(leading), error)
    mirror = mirror + dot1(half(mirror), error)
    return leading, mirror, away + dot3(split(leading), inner)


def after_trans(leading, mirror, away, into):
    q = split(into)
    trans = dot3(split(leading), q)
    bounced = split(dot3(split(mirror), q))
    return trans, away + dot3(split(into.T), bounced)


def place():
    return lax.axis_index("gx") * lax.axis_size("gy") + lax.axis_index("gy")


def bit(me, distance):
    return me & distance != 0


def lower_upper(h):
    row = lax.broadcasted_iota(jnp.int32, (h, h), 0)
    col = lax.broadcasted_iota(jnp.int32, (h, h), 1)
    return row > col, row < col


def pack_symmetric(x, core, ref, start):
    h = x.shape[0] // 2
    q = h // 2
    below, above = lower_upper(h)
    a, b, c = x[:h, :h], x[:h, h:], x[h:, h:]
    diagonal = jnp.sum(jnp.where(below | above, 0.0, c), axis=0, keepdims=True)
    both = jnp.concatenate([b, jnp.where(above, c, a)], 1)
    ref[start : start + q, :] = jnp.where(core, both[q:], both[:q])
    diagonal = jnp.concatenate([diagonal, diagonal], 1)
    ref[start + q : start + q + PAD, :] = jnp.broadcast_to(diagonal, (PAD, 2 * h))


def joined(near_ref, far_ref, core, lo, hi):
    near, far = near_ref[lo:hi, :], far_ref[lo:hi, :]
    return jnp.concatenate([jnp.where(core, far, near), jnp.where(core, near, far)], 0)


def unpack_symmetric(near_ref, far_ref, core, start):
    h = near_ref.shape[1] // 2
    q = h // 2
    below, above = lower_upper(h)
    both = joined(near_ref, far_ref, core, start, start + q)
    diagonal = near_ref[start + q : start + q + 1, :h]
    b, w = both[:, :h], both[:, h:]
    turned = w.T
    a = jnp.where(above, turned, w)
    c = jnp.where(above, w, jnp.where(below, turned, diagonal))
    return jnp.concatenate([jnp.concatenate([a, b], 1), jnp.concatenate([b.T, c], 1)], 0)


def unpack_second(near_ref, far_ref, core):
    h = near_ref.shape[1] // 2
    return joined(near_ref, far_ref, core, 0, h), unpack_symmetric(near_ref, far_ref, core, h)


def send_total(own_side, other_side, trans, same, core, first_ref, second_ref, own_ref):
    turned = trans.T
    near = jnp.where(same, other_side, own_side)
    away = jnp.where(same, own_side, other_side)
    back = jnp.where(same, turned, trans)
    own_ref[0] = near
    own_ref[1] = away
    own_ref[2] = jnp.where(same, trans, turned)
    pack_symmetric(near, core, first_ref, 0)
    pack_second(back, away, core, second_ref)


def first_kernel(section_ref, got1, got2, got3, prefix_ref, *send_refs):
    me = place()
    upper = bit(me, 1)
    left, right, trans = section_ref[0], section_ref[1], section_ref[2]
    pick = lambda a, b: jnp.where(upper, a, b)
    own = pick(left, right), pick(right, left), pick(trans, trans.T)
    leading, mirror, own_side = before_trans(own, pick(got2[0], got1[0]))
    into = pick(got3[0], got3[0].T)
    through, other_side = after_trans(leading, mirror, pick(got1[0], got2[0]), into)
    send_total(own_side, other_side, through, upper == bit(me, 2), upper, *send_refs)
    prefix_ref[0] = pick(other_side, left)
    prefix_ref[1] = pick(own_side, right)
    prefix_ref[2] = pick(through, trans)


def early_kernel(own_ref, near_ref, far_ref, half_ref, *first_ref):
    core = bit(place(), 1)
    facing = unpack_symmetric(near_ref, far_ref, core, 0)
    half = before_trans((own_ref[0], own_ref[1], own_ref[2]), facing)
    for ref in first_ref:
        pack_symmetric(half[2], core, ref, 0)
    for i, x in enumerate(half):
        half_ref[i] = x


def final_kernel(half_ref, near_ref, far_ref, second_ref):
    core = bit(place(), 1)
    into, away = unpack_second(near_ref, far_ref, core)
    trans, other_side = after_trans(half_ref[0], half_ref[1], away, into)
    pack_second(trans, other_side, core, second_ref)


def pack_second(back, away, core, ref):
    h = back.shape[0] // 2
    ref[0:h, :] = jnp.where(core, back[h:], back[:h])
    pack_symmetric(away, core, ref, h)


def late_kernel(distance, half_ref, near_ref, far_ref, *send_refs):
    me = place()
    core = bit(me, 1)
    into, away = unpack_second(near_ref, far_ref, core)
    trans, other_side = after_trans(half_ref[0], half_ref[1], away, into)
    same = bit(me, distance) == bit(me, 2 * distance)
    send_total(half_ref[2], other_side, trans, same, core, *send_refs)


def prefix_kernel(distance, old_ref, near1, far1, near2, far2, new_ref):
    me = place()
    core, upper = bit(me, 1), bit(me, distance)
    facing = unpack_symmetric(near1, far1, core, 0)
    leading, mirror, right = before_trans((old_ref[0], old_ref[1], old_ref[2]), facing)
    into, away = unpack_second(near2, far2, core)
    trans, left = after_trans(leading, mirror, away, into)
    for i, x in enumerate((left, right, trans)):
        new_ref[i] = jnp.where(upper, x, old_ref[i])


def by_third(distance, me, near2, far2, near3, far3):
    third = bit(me, distance // 2)
    return jnp.where(third, near3[...], near2[...]), jnp.where(third, far3[...], far2[...])


def last_early_kernel(distance, old_ref, near2, far2, near3, far3, half_ref):
    me = place()

    @pl.when(bit(me, distance))
    def _():
        facing = unpack_symmetric(*by_third(distance, me, near2, far2, near3, far3), bit(me, 1), 0)
        for i, x in enumerate(before_trans((old_ref[0], old_ref[1], old_ref[2]), facing)):
            half_ref[i] = x


def last_kernel(distance, old_ref, half_ref, near2, far2, near3, far3, left_out, right_out, trans_out, new_ref, sems):
    me = place()
    upper = bit(me, distance)
    left_copy = pltpu.make_async_copy(new_ref.at[0:1], left_out, sems.at[0])
    trans_copy = pltpu.make_async_copy(new_ref.at[2:3], trans_out, sems.at[1])
    right_copy = pltpu.make_async_copy(new_ref.at[1:2], right_out, sems.at[2])
    new_ref[1] = jnp.where(upper, half_ref[2], old_ref[1])
    right_copy.start()

    @pl.when(upper)
    def _():
        into, away = unpack_second(*by_third(distance, me, near2, far2, near3, far3), bit(me, 1))
        q = split(into)
        new_ref[2] = dot3(split(half_ref[0]), q)
        trans_copy.start()
        bounced = split(dot3(split(half_ref[1]), q))
        new_ref[0] = away + dot3(split(into.T), bounced)
        left_copy.start()

    @pl.when(jnp.logical_not(upper))
    def _():
        new_ref[2] = old_ref[2]
        trans_copy.start()
        new_ref[0] = old_ref[0]
        left_copy.start()

    right_copy.wait()
    trans_copy.wait()
    left_copy.wait()


def call(kernel, products, outs, *args, out_space=pltpu.VMEM, scratch=()):
    vmem = pl.BlockSpec(memory_space=pltpu.VMEM)
    m = args[0].shape[-1]
    return pl.pallas_call(
        kernel,
        out_shape=[jax.ShapeDtypeStruct(s, F32) for s in outs],
        in_specs=[vmem] * len(args),
        out_specs=[pl.BlockSpec(memory_space=out_space)] * len(outs),
        scratch_shapes=scratch,
        cost_estimate=pl.CostEstimate(flops=2 * products * m**3, bytes_accessed=4 * m**2 * len(args), transcendentals=0),
        compiler_params=pltpu.CompilerParams(vmem_limit_bytes=40 * 2**20),
    )(*args)


def shards(refl_left, refl_right, trans):
    m = trans.shape[1]
    levels = lax.axis_size(AXES).bit_length() - 1
    stack = (3, m, m)
    first, second = (m // 4 + PAD, m), (m // 2 + m // 4 + PAD, m)
    sections = refl_left, refl_right, trans
    got = [swap(x, 1) for x in sections]
    section = jnp.concatenate(sections, 0)
    prefix, send1, send2, own = call(first_kernel, 36, [stack, first, second, stack], section, *got)
    pending = None
    for level in range(1, levels - 1):
        distance = 1 << level
        bind = lambda kernel: functools.partial(kernel, distance)
        near1, near2 = swap(send1, distance), swap(send2, distance)
        if pending is not None:
            (prefix,) = pending(prefix)
            near1, prefix = lax.optimization_barrier((near1, prefix))
        far1 = swap(near1, 1)
        outs = [stack] + [first] * (level == levels - 2)
        halfway, *sends = call(early_kernel, 27, outs, own, near1, far1)
        near2, halfway = lax.optimization_barrier((near2, halfway))
        far2 = swap(near2, 1)
        pending = lambda old, kernel=bind(prefix_kernel), got=(near1, far1, near2, far2): call(kernel, 36, [stack], old, *got)
        if level < levels - 2:
            send1, send2, own = call(bind(late_kernel), 9, [first, second, stack], halfway, near2, far2)

    distance *= 2
    (send1,) = sends
    first3, first2 = pair(send1, 1, 3), pair(send1, 1, 2)
    (send2,) = call(final_kernel, 9, [second], halfway, near2, far2)
    near3, near2 = give(send2, 1, 3), give(send2, 1, 2)
    first3, first2, prefix = lax.optimization_barrier((first3, first2, prefix))
    (prefix,) = pending(prefix)
    args = prefix, first2, swap(first2, 1), first3, swap(first3, 1)
    (halfway,) = call(functools.partial(last_early_kernel, distance), 27, [stack], *args)
    near3, halfway = lax.optimization_barrier((near3, halfway))
    far3 = swap(near3, 1)
    near2, far3 = lax.optimization_barrier((near2, far3))
    args = prefix, halfway, near2, swap(near2, 1), near3, far3
    scratch = [pltpu.VMEM(stack, F32), pltpu.SemaphoreType.DMA((3,))]
    kernel = functools.partial(last_kernel, distance)
    return tuple(call(kernel, 9, [(1, m, m)] * 3, *args, out_space=pltpu.HBM, scratch=scratch))


def solution(mesh):
    spec = P(AXES, None, None)
    return jax.shard_map(
        shards,
        mesh=mesh,
        in_specs=(spec,) * 3,
        out_specs=(spec,) * 3,
        check_vma=False,
    )
```

```python
import functools

import jax
import jax.numpy as jnp
from jax import lax
from jax.experimental import pallas as pl
from jax.experimental.pallas import tpu as pltpu
from jax.sharding import PartitionSpec as P

AXES = ("gx", "gy")
NS_STEPS = 5
PAD = 8
F32 = jnp.float32
BF16 = jnp.bfloat16
NN = (((1,), (0,)), ((), ()))
NT = (((1,), (1,)), ((), ()))


def swap(block, distance):
    count = lax.axis_size(AXES)
    return lax.ppermute(block, AXES, [(i, i ^ distance) for i in range(count)])


def pair(block, first, second):
    count = lax.axis_size(AXES)
    quarter = count // 4
    shift = (second - first) * quarter
    step = {first: lambda i: i + shift, second: lambda i: i - shift}
    return lax.ppermute(block, AXES, [(i, step.get(i // quarter, lambda i: i ^ 1)(i)) for i in range(count)])


def split(x):
    high = x.astype(BF16)
    return high, (x - high.astype(F32)).astype(BF16)


def dot1(a, b, dims=NN):
    h = a.shape[0] // 2
    parts = [lax.dot_general(x, b, dims, preferred_element_type=F32) for x in (a[:h], a[h:])]
    return jnp.concatenate(parts, 0)


def dot3(a, b, dims=NN):
    return dot1(a[0], b[0], dims) + (dot1(a[0], b[1], dims) + dot1(a[1], b[0], dims))


def half(x):
    return x.astype(BF16)


def four_steps(power):
    rest, power = power, half(power)
    for _ in range(NS_STEPS - 1):
        squared = dot1(power, power)
        power = half(squared)
        rest = rest + squared + dot1(half(rest), power)
    return half(rest)


def before_trans(own, facing):
    near, away, out = own
    f, o, s = split(facing), split(near), split(out)
    rough = dot1(f[0], o[0])
    rest = four_steps(rough)
    coupling = rough + (dot1(f[0], o[1]) + dot1(f[1], o[0]))
    inner = split(dot3(f, s, NT))
    high, low = split(coupling)
    error = half((coupling - rest.astype(F32)) + (dot1(high, rest) + dot1(low, rest)))
    leading = out + (dot1(s[0], rest) + dot1(s[1], rest))
    mirror = near + (dot1(o[0], rest) + dot1(o[1], rest))
    leading = leading + dot1(half(leading), error)
    mirror = mirror + dot1(half(mirror), error)
    return leading, mirror, away + dot3(split(leading), inner)


def after_trans(leading, mirror, away, into):
    q = split(into)
    trans = dot3(split(leading), q)
    bounced = split(dot3(split(mirror), q))
    return trans, away + dot3(split(into.T), bounced)


def place():
    return lax.axis_index("gx") * lax.axis_size("gy") + lax.axis_index("gy")


def bit(me, distance):
    return me & distance != 0


def lower_upper(h):
    row = lax.broadcasted_iota(jnp.int32, (h, h), 0)
    col = lax.broadcasted_iota(jnp.int32, (h, h), 1)
    return row > col, row < col


def pack_symmetric(x, core, ref, start):
    h = x.shape[0] // 2
    q = h // 2
    below, above = lower_upper(h)
    a, b, c = x[:h, :h], x[:h, h:], x[h:, h:]
    diagonal = jnp.sum(jnp.where(below | above, 0.0, c), axis=0, keepdims=True)
    both = jnp.concatenate([b, jnp.where(above, c, a)], 1)
    ref[start : start + q, :] = jnp.where(core, both[q:], both[:q])
    diagonal = jnp.concatenate([diagonal, diagonal], 1)
    ref[start + q : start + q + PAD, :] = jnp.broadcast_to(diagonal, (PAD, 2 * h))


def joined(near_ref, far_ref, core, lo, hi):
    near, far = near_ref[lo:hi, :], far_ref[lo:hi, :]
    return jnp.concatenate([jnp.where(core, far, near), jnp.where(core, near, far)], 0)


def unpack_symmetric(near_ref, far_ref, core, start):
    h = near_ref.shape[1] // 2
    q = h // 2
    below, above = lower_upper(h)
    both = joined(near_ref, far_ref, core, start, start + q)
    diagonal = near_ref[start + q : start + q + 1, :h]
    b, w = both[:, :h], both[:, h:]
    turned = w.T
    a = jnp.where(above, turned, w)
    c = jnp.where(above, w, jnp.where(below, turned, diagonal))
    return jnp.concatenate([jnp.concatenate([a, b], 1), jnp.concatenate([b.T, c], 1)], 0)


def unpack_second(near_ref, far_ref, core):
    h = near_ref.shape[1] // 2
    return joined(near_ref, far_ref, core, 0, h), unpack_symmetric(near_ref, far_ref, core, h)


def send_total(own_side, other_side, trans, same, core, first_ref, second_ref, own_ref):
    turned = trans.T
    near = jnp.where(same, other_side, own_side)
    away = jnp.where(same, own_side, other_side)
    back = jnp.where(same, turned, trans)
    own_ref[0] = near
    own_ref[1] = away
    own_ref[2] = jnp.where(same, trans, turned)
    pack_symmetric(near, core, first_ref, 0)
    pack_second(back, away, core, second_ref)


def first_kernel(section_ref, got1, got2, got3, prefix_ref, *send_refs):
    me = place()
    upper = bit(me, 1)
    left, right, trans = section_ref[0], section_ref[1], section_ref[2]
    pick = lambda a, b: jnp.where(upper, a, b)
    own = pick(left, right), pick(right, left), pick(trans, trans.T)
    leading, mirror, own_side = before_trans(own, pick(got2[0], got1[0]))
    into = pick(got3[0], got3[0].T)
    through, other_side = after_trans(leading, mirror, pick(got1[0], got2[0]), into)
    send_total(own_side, other_side, through, upper == bit(me, 2), upper, *send_refs)
    prefix_ref[0] = pick(other_side, left)
    prefix_ref[1] = pick(own_side, right)
    prefix_ref[2] = pick(through, trans)


def early_kernel(own_ref, near_ref, far_ref, half_ref, *first_ref):
    core = bit(place(), 1)
    facing = unpack_symmetric(near_ref, far_ref, core, 0)
    half = before_trans((own_ref[0], own_ref[1], own_ref[2]), facing)
    for ref in first_ref:
        pack_symmetric(half[2], core, ref, 0)
    for i, x in enumerate(half):
        half_ref[i] = x


def final_kernel(half_ref, near_ref, far_ref, second_ref):
    core = bit(place(), 1)
    into, away = unpack_second(near_ref, far_ref, core)
    trans, other_side = after_trans(half_ref[0], half_ref[1], away, into)
    pack_second(trans, other_side, core, second_ref)


def pack_second(back, away, core, ref):
    h = back.shape[0] // 2
    ref[0:h, :] = jnp.where(core, back[h:], back[:h])
    pack_symmetric(away, core, ref, h)


def late_kernel(distance, half_ref, near_ref, far_ref, *send_refs):
    me = place()
    core = bit(me, 1)
    into, away = unpack_second(near_ref, far_ref, core)
    trans, other_side = after_trans(half_ref[0], half_ref[1], away, into)
    same = bit(me, distance) == bit(me, 2 * distance)
    send_total(half_ref[2], other_side, trans, same, core, *send_refs)


def prefix_kernel(distance, old_ref, near1, far1, near2, far2, new_ref):
    me = place()
    core, upper = bit(me, 1), bit(me, distance)
    facing = unpack_symmetric(near1, far1, core, 0)
    leading, mirror, right = before_trans((old_ref[0], old_ref[1], old_ref[2]), facing)
    into, away = unpack_second(near2, far2, core)
    trans, left = after_trans(leading, mirror, away, into)
    for i, x in enumerate((left, right, trans)):
        new_ref[i] = jnp.where(upper, x, old_ref[i])


def by_third(distance, me, near2, far2, near3, far3):
    third = bit(me, distance // 2)
    return jnp.where(third, near3[...], near2[...]), jnp.where(third, far3[...], far2[...])


def last_early_kernel(distance, old_ref, near2, far2, near3, far3, half_ref, left_out, right_out, trans_out, sems):
    me = place()
    upper = bit(me, distance)

    @pl.when(upper)
    def _():
        facing = unpack_symmetric(*by_third(distance, me, near2, far2, near3, far3), bit(me, 1), 0)
        for i, x in enumerate(before_trans((old_ref[0], old_ref[1], old_ref[2]), facing)):
            half_ref[i] = x

    @pl.when(jnp.logical_not(upper))
    def _():
        outs = left_out, right_out, trans_out
        copies = [pltpu.make_async_copy(old_ref.at[i : i + 1], out, sems.at[i]) for i, out in enumerate(outs)]
        for copy in copies:
            copy.start()
        for copy in copies:
            copy.wait()


def last_kernel(distance, half_ref, near2, far2, near3, far3, _l, _r, _t, left_out, right_out, trans_out, new_ref, sems):
    me = place()

    @pl.when(bit(me, distance))
    def _():
        right_copy = pltpu.make_async_copy(half_ref.at[2:3], right_out, sems.at[0])
        trans_copy = pltpu.make_async_copy(new_ref.at[0:1], trans_out, sems.at[1])
        left_copy = pltpu.make_async_copy(new_ref.at[1:2], left_out, sems.at[2])
        right_copy.start()
        into, away = unpack_second(*by_third(distance, me, near2, far2, near3, far3), bit(me, 1))
        q = split(into)
        new_ref[0] = dot3(split(half_ref[0]), q)
        trans_copy.start()
        bounced = split(dot3(split(half_ref[1]), q))
        new_ref[1] = away + dot3(split(into.T), bounced)
        left_copy.start()
        right_copy.wait()
        trans_copy.wait()
        left_copy.wait()


def call(kernel, products, outs, *args, given=(), copied=0, scratch=()):
    vmem, hbm = pl.BlockSpec(memory_space=pltpu.VMEM), pl.BlockSpec(memory_space=pltpu.HBM)
    m = args[0].shape[-1]
    return pl.pallas_call(
        kernel,
        out_shape=[jax.ShapeDtypeStruct(s, F32) for s in outs],
        in_specs=[vmem] * len(args) + [hbm] * len(given),
        out_specs=[vmem] * (len(outs) - copied) + [hbm] * copied,
        input_output_aliases={len(args) + i: len(outs) - copied + i for i in range(len(given))},
        scratch_shapes=scratch,
        cost_estimate=pl.CostEstimate(flops=2 * products * m**3, bytes_accessed=4 * m**2 * len(args), transcendentals=0),
        compiler_params=pltpu.CompilerParams(vmem_limit_bytes=40 * 2**20),
    )(*args, *given)


def shards(refl_left, refl_right, trans):
    m = trans.shape[1]
    levels = lax.axis_size(AXES).bit_length() - 1
    stack = (3, m, m)
    first, second = (m // 4 + PAD, m), (m // 2 + m // 4 + PAD, m)
    sections = refl_left, refl_right, trans
    got = [swap(x, 1) for x in sections]
    section = jnp.concatenate(sections, 0)
    prefix, send1, send2, own = call(first_kernel, 36, [stack, first, second, stack], section, *got)
    pending = None
    for level in range(1, levels - 1):
        distance = 1 << level
        bind = lambda kernel: functools.partial(kernel, distance)
        near1, near2 = swap(send1, distance), swap(send2, distance)
        if pending is not None:
            (prefix,) = pending(prefix)
            near1, prefix = lax.optimization_barrier((near1, prefix))
        far1 = swap(near1, 1)
        outs = [stack] + [first] * (level == levels - 2)
        halfway, *sends = call(early_kernel, 27, outs, own, near1, far1)
        near2, halfway = lax.optimization_barrier((near2, halfway))
        far2 = swap(near2, 1)
        pending = lambda old, kernel=bind(prefix_kernel), got=(near1, far1, near2, far2): call(kernel, 36, [stack], old, *got)
        if level < levels - 2:
            send1, send2, own = call(bind(late_kernel), 9, [first, second, stack], halfway, near2, far2)

    distance *= 2
    (send1,) = sends
    first3, first2 = pair(send1, 1, 3), pair(send1, 1, 2)
    (send2,) = call(final_kernel, 9, [second], halfway, near2, far2)
    near3, near2 = pair(send2, 1, 3), pair(send2, 1, 2)
    first3, first2, prefix = lax.optimization_barrier((first3, first2, prefix))
    (prefix,) = pending(prefix)
    args = prefix, first2, swap(first2, 1), first3, swap(first3, 1)
    one, sems = (1, m, m), pltpu.SemaphoreType.DMA((3,))
    kernel = functools.partial(last_early_kernel, distance)
    halfway, *given = call(kernel, 27, [stack, one, one, one], *args, copied=3, scratch=[sems])
    near3, halfway = lax.optimization_barrier((near3, halfway))
    far3 = swap(near3, 1)
    near2, far3 = lax.optimization_barrier((near2, far3))
    args = halfway, near2, swap(near2, 1), near3, far3
    scratch = [pltpu.VMEM((2, m, m), F32), sems]
    return tuple(call(functools.partial(last_kernel, distance), 9, [one] * 3, *args, given=given, copied=3, scratch=scratch))


def solution(mesh):
    spec = P(AXES, None, None)
    return jax.shard_map(
        shards,
        mesh=mesh,
        in_specs=(spec,) * 3,
        out_specs=(spec,) * 3,
        check_vma=False,
    )
```

```python
import functools

import jax
import jax.numpy as jnp
from jax import lax
from jax.experimental import pallas as pl
from jax.experimental.pallas import tpu as pltpu
from jax.sharding import PartitionSpec as P

AXES = ("gx", "gy")
NS_STEPS = 5
PAD = 8
F32 = jnp.float32
BF16 = jnp.bfloat16
NN = (((1,), (0,)), ((), ()))
NT = (((1,), (1,)), ((), ()))


def swap(block, distance):
    count = lax.axis_size(AXES)
    return lax.ppermute(block, AXES, [(i, i ^ distance) for i in range(count)])


def pair(block, first, second):
    count = lax.axis_size(AXES)
    quarter = count // 4
    shift = (second - first) * quarter
    step = {first: lambda i: i + shift, second: lambda i: i - shift}
    return lax.ppermute(block, AXES, [(i, step.get(i // quarter, lambda i: i ^ 1)(i)) for i in range(count)])


def split(x):
    high = x.astype(BF16)
    return high, (x - high.astype(F32)).astype(BF16)


def dot1(a, b, dims=NN):
    h = a.shape[0] // 2
    parts = [lax.dot_general(x, b, dims, preferred_element_type=F32) for x in (a[:h], a[h:])]
    return jnp.concatenate(parts, 0)


def dot3(a, b, dims=NN):
    return dot1(a[0], b[0], dims) + (dot1(a[0], b[1], dims) + dot1(a[1], b[0], dims))


def half(x):
    return x.astype(BF16)


def four_steps(power):
    rest, power = power, half(power)
    for _ in range(NS_STEPS - 1):
        squared = dot1(power, power)
        power = half(squared)
        rest = rest + squared + dot1(half(rest), power)
    return half(rest)


def before_trans(own, facing):
    near, away, out = own
    f, o, s = split(facing), split(near), split(out)
    rough = dot1(f[0], o[0])
    rest = four_steps(rough)
    coupling = rough + (dot1(f[0], o[1]) + dot1(f[1], o[0]))
    inner = split(dot3(f, s, NT))
    high, low = split(coupling)
    error = half((coupling - rest.astype(F32)) + (dot1(high, rest) + dot1(low, rest)))
    leading = out + (dot1(s[0], rest) + dot1(s[1], rest))
    mirror = near + (dot1(o[0], rest) + dot1(o[1], rest))
    leading = leading + dot1(half(leading), error)
    mirror = mirror + dot1(half(mirror), error)
    return leading, mirror, away + dot3(split(leading), inner)


def after_trans(leading, mirror, away, into):
    q = split(into)
    trans = dot3(split(leading), q)
    bounced = split(dot3(split(mirror), q))
    return trans, away + dot3(split(into.T), bounced)


def place():
    return lax.axis_index("gx") * lax.axis_size("gy") + lax.axis_index("gy")


def bit(me, distance):
    return me & distance != 0


def lower_upper(h):
    row = lax.broadcasted_iota(jnp.int32, (h, h), 0)
    col = lax.broadcasted_iota(jnp.int32, (h, h), 1)
    return row > col, row < col


def symmetric_rows(x):
    h = x.shape[0] // 2
    below, above = lower_upper(h)
    a, b, c = x[:h, :h], x[:h, h:], x[h:, h:]
    diagonal = jnp.sum(jnp.where(below | above, 0.0, c), axis=0, keepdims=True)
    return jnp.concatenate([b, jnp.where(above, c, a)], 1), diagonal


def store_half(rows, core, ref, start):
    q = rows.shape[0] // 2
    ref[start : start + q, :] = jnp.where(core, rows[q:], rows[:q])


def store_diagonals(one, two, ref, start):
    ref[start : start + PAD, :] = jnp.broadcast_to(jnp.concatenate([one, two], 1), (PAD, 2 * one.shape[1]))


def pack_symmetric(x, core, ref, start):
    rows, diagonal = symmetric_rows(x)
    store_half(rows, core, ref, start)
    store_diagonals(diagonal, diagonal, ref, start + rows.shape[0] // 2)


def joined(near_ref, far_ref, core, lo, hi):
    near, far = near_ref[lo:hi, :], far_ref[lo:hi, :]
    return jnp.concatenate([jnp.where(core, far, near), jnp.where(core, near, far)], 0)


def unpack_symmetric(near_ref, far_ref, core, start, diagonal=None):
    h = near_ref.shape[1] // 2
    q = h // 2
    below, above = lower_upper(h)
    both = joined(near_ref, far_ref, core, start, start + q)
    if diagonal is None:
        diagonal = near_ref[start + q : start + q + 1, :h]
    b, w = both[:, :h], both[:, h:]
    turned = w.T
    a = jnp.where(above, turned, w)
    c = jnp.where(above, w, jnp.where(below, turned, diagonal))
    return jnp.concatenate([jnp.concatenate([a, b], 1), jnp.concatenate([b.T, c], 1)], 0)


def unpack_second(near_ref, far_ref, core, first_ref=None):
    h = near_ref.shape[1] // 2
    diagonal = None if first_ref is None else first_ref[h // 2 : h // 2 + 1, h:]
    return joined(near_ref, far_ref, core, 0, h), unpack_symmetric(near_ref, far_ref, core, h, diagonal)


def send_total(own_side, other_side, trans, same, core, first_ref, second_ref, own_ref):
    turned = trans.T
    near = jnp.where(same, other_side, own_side)
    away = jnp.where(same, own_side, other_side)
    back = jnp.where(same, turned, trans)
    own_ref[0] = near
    own_ref[1] = away
    own_ref[2] = jnp.where(same, trans, turned)
    near_rows, near_diagonal = symmetric_rows(near)
    away_rows, away_diagonal = symmetric_rows(away)
    h = near_rows.shape[0]
    store_half(near_rows, core, first_ref, 0)
    store_diagonals(near_diagonal, away_diagonal, first_ref, h // 2)
    store_half(back, core, second_ref, 0)
    store_half(away_rows, core, second_ref, h)


def first_kernel(section_ref, got1, got2, got3, prefix_ref, *send_refs):
    me = place()
    upper = bit(me, 1)
    left, right, trans = section_ref[0], section_ref[1], section_ref[2]
    pick = lambda a, b: jnp.where(upper, a, b)
    own = pick(left, right), pick(right, left), pick(trans, trans.T)
    leading, mirror, own_side = before_trans(own, pick(got2[0], got1[0]))
    into = pick(got3[0], got3[0].T)
    through, other_side = after_trans(leading, mirror, pick(got1[0], got2[0]), into)
    send_total(own_side, other_side, through, upper == bit(me, 2), upper, *send_refs)
    prefix_ref[0] = pick(other_side, left)
    prefix_ref[1] = pick(own_side, right)
    prefix_ref[2] = pick(through, trans)


def early_kernel(own_ref, near_ref, far_ref, half_ref, *first_ref):
    core = bit(place(), 1)
    facing = unpack_symmetric(near_ref, far_ref, core, 0)
    half = before_trans((own_ref[0], own_ref[1], own_ref[2]), facing)
    for ref in first_ref:
        pack_symmetric(half[2], core, ref, 0)
    for i, x in enumerate(half):
        half_ref[i] = x


def final_kernel(half_ref, near1, near_ref, far_ref, second_ref):
    core = bit(place(), 1)
    into, away = unpack_second(near_ref, far_ref, core, near1)
    trans, other_side = after_trans(half_ref[0], half_ref[1], away, into)
    pack_second(trans, other_side, core, second_ref)


def pack_second(back, away, core, ref):
    h = back.shape[0] // 2
    store_half(back, core, ref, 0)
    pack_symmetric(away, core, ref, h)


def late_kernel(distance, half_ref, near1, near_ref, far_ref, *send_refs):
    me = place()
    core = bit(me, 1)
    into, away = unpack_second(near_ref, far_ref, core, near1)
    trans, other_side = after_trans(half_ref[0], half_ref[1], away, into)
    same = bit(me, distance) == bit(me, 2 * distance)
    send_total(half_ref[2], other_side, trans, same, core, *send_refs)


def prefix_kernel(distance, old_ref, near1, far1, near2, far2, new_ref):
    me = place()
    core, upper = bit(me, 1), bit(me, distance)
    facing = unpack_symmetric(near1, far1, core, 0)
    leading, mirror, right = before_trans((old_ref[0], old_ref[1], old_ref[2]), facing)
    into, away = unpack_second(near2, far2, core, near1)
    trans, left = after_trans(leading, mirror, away, into)
    for i, x in enumerate((left, right, trans)):
        new_ref[i] = jnp.where(upper, x, old_ref[i])


def by_third(distance, me, near2, far2, near3, far3):
    third = bit(me, distance // 2)
    return jnp.where(third, near3[...], near2[...]), jnp.where(third, far3[...], far2[...])


def last_early_kernel(distance, old_ref, near2, far2, near3, far3, half_ref, left_out, right_out, trans_out, sems):
    me = place()
    upper = bit(me, distance)

    @pl.when(upper)
    def _():
        facing = unpack_symmetric(*by_third(distance, me, near2, far2, near3, far3), bit(me, 1), 0)
        for i, x in enumerate(before_trans((old_ref[0], old_ref[1], old_ref[2]), facing)):
            half_ref[i] = x

    @pl.when(jnp.logical_not(upper))
    def _():
        outs = left_out, right_out, trans_out
        copies = [pltpu.make_async_copy(old_ref.at[i : i + 1], out, sems.at[i]) for i, out in enumerate(outs)]
        for copy in copies:
            copy.start()
        for copy in copies:
            copy.wait()


def last_kernel(distance, half_ref, near2, far2, near3, far3, _l, _r, _t, left_out, right_out, trans_out, new_ref, sems):
    me = place()

    @pl.when(bit(me, distance))
    def _():
        right_copy = pltpu.make_async_copy(half_ref.at[2:3], right_out, sems.at[0])
        trans_copy = pltpu.make_async_copy(new_ref.at[0:1], trans_out, sems.at[1])
        left_copy = pltpu.make_async_copy(new_ref.at[1:2], left_out, sems.at[2])
        right_copy.start()
        into, away = unpack_second(*by_third(distance, me, near2, far2, near3, far3), bit(me, 1))
        q = split(into)
        new_ref[0] = dot3(split(half_ref[0]), q)
        trans_copy.start()
        bounced = split(dot3(split(half_ref[1]), q))
        new_ref[1] = away + dot3(split(into.T), bounced)
        left_copy.start()
        right_copy.wait()
        trans_copy.wait()
        left_copy.wait()


def call(kernel, products, outs, *args, given=(), copied=0, scratch=()):
    vmem, hbm = pl.BlockSpec(memory_space=pltpu.VMEM), pl.BlockSpec(memory_space=pltpu.HBM)
    m = args[0].shape[-1]
    return pl.pallas_call(
        kernel,
        out_shape=[jax.ShapeDtypeStruct(s, F32) for s in outs],
        in_specs=[vmem] * len(args) + [hbm] * len(given),
        out_specs=[vmem] * (len(outs) - copied) + [hbm] * copied,
        input_output_aliases={len(args) + i: len(outs) - copied + i for i in range(len(given))},
        scratch_shapes=scratch,
        cost_estimate=pl.CostEstimate(flops=2 * products * m**3, bytes_accessed=4 * m**2 * len(args), transcendentals=0),
        compiler_params=pltpu.CompilerParams(vmem_limit_bytes=40 * 2**20),
    )(*args, *given)


def shards(refl_left, refl_right, trans):
    m = trans.shape[1]
    levels = lax.axis_size(AXES).bit_length() - 1
    stack = (3, m, m)
    first, second, padded = (m // 4 + PAD, m), (m // 2 + m // 4, m), (m // 2 + m // 4 + PAD, m)
    sections = refl_left, refl_right, trans
    got = [swap(x, 1) for x in sections]
    section = jnp.concatenate(sections, 0)
    prefix, send1, send2, own = call(first_kernel, 36, [stack, first, second, stack], section, *got)
    pending = None
    for level in range(1, levels - 1):
        distance = 1 << level
        bind = lambda kernel: functools.partial(kernel, distance)
        near1, near2 = swap(send1, distance), swap(send2, distance)
        if pending is not None:
            (prefix,) = pending(prefix)
            near1, prefix = lax.optimization_barrier((near1, prefix))
        far1 = swap(near1, 1)
        outs = [stack] + [first] * (level == levels - 2)
        halfway, *sends = call(early_kernel, 27, outs, own, near1, far1)
        near2, halfway = lax.optimization_barrier((near2, halfway))
        far2 = swap(near2, 1)
        pending = lambda old, kernel=bind(prefix_kernel), got=(near1, far1, near2, far2): call(kernel, 36, [stack], old, *got)
        if level < levels - 2:
            send1, send2, own = call(bind(late_kernel), 9, [first, second, stack], halfway, near1, near2, far2)

    distance *= 2
    (send1,) = sends
    first3, first2 = pair(send1, 1, 3), pair(send1, 1, 2)
    (send2,) = call(final_kernel, 9, [padded], halfway, near1, near2, far2)
    near3, near2 = pair(send2, 1, 3), pair(send2, 1, 2)
    first3, first2, prefix = lax.optimization_barrier((first3, first2, prefix))
    (prefix,) = pending(prefix)
    args = prefix, first2, swap(first2, 1), first3, swap(first3, 1)
    one, sems = (1, m, m), pltpu.SemaphoreType.DMA((3,))
    kernel = functools.partial(last_early_kernel, distance)
    halfway, *given = call(kernel, 27, [stack, one, one, one], *args, copied=3, scratch=[sems])
    near3, halfway = lax.optimization_barrier((near3, halfway))
    far3 = swap(near3, 1)
    near2, far3 = lax.optimization_barrier((near2, far3))
    args = halfway, near2, swap(near2, 1), near3, far3
    scratch = [pltpu.VMEM((2, m, m), F32), sems]
    return tuple(call(functools.partial(last_kernel, distance), 9, [one] * 3, *args, given=given, copied=3, scratch=scratch))


def solution(mesh):
    spec = P(AXES, None, None)
    return jax.shard_map(
        shards,
        mesh=mesh,
        in_specs=(spec,) * 3,
        out_specs=(spec,) * 3,
        check_vma=False,
    )
```

```python
import functools

import jax
import jax.numpy as jnp
from jax import lax
from jax.experimental import pallas as pl
from jax.experimental.pallas import tpu as pltpu
from jax.sharding import PartitionSpec as P

AXES = ("gx", "gy")
NS_STEPS = 5
PAD = 8
F32 = jnp.float32
BF16 = jnp.bfloat16
NN = (((1,), (0,)), ((), ()))
NT = (((1,), (1,)), ((), ()))


def swap(block, distance):
    count = lax.axis_size(AXES)
    return lax.ppermute(block, AXES, [(i, i ^ distance) for i in range(count)])


def pair(block, first, second):
    count = lax.axis_size(AXES)
    quarter = count // 4
    shift = (second - first) * quarter
    step = {first: lambda i: i + shift, second: lambda i: i - shift}
    return lax.ppermute(block, AXES, [(i, step.get(i // quarter, lambda i: i ^ 1)(i)) for i in range(count)])


def split(x):
    high = x.astype(BF16)
    return high, (x - high.astype(F32)).astype(BF16)


def dot1(a, b, dims=NN):
    h = a.shape[0] // 2
    parts = [lax.dot_general(x, b, dims, preferred_element_type=F32) for x in (a[:h], a[h:])]
    return jnp.concatenate(parts, 0)


def dot3(a, b, dims=NN):
    return dot1(a[0], b[0], dims) + (dot1(a[0], b[1], dims) + dot1(a[1], b[0], dims))


def half(x):
    return x.astype(BF16)


def four_steps(power):
    rest, power = power, half(power)
    for _ in range(NS_STEPS - 1):
        squared = dot1(power, power)
        power = half(squared)
        rest = rest + squared + dot1(half(rest), power)
    return half(rest)


def before_trans(own, facing):
    near, away, out = own
    f, o, s = split(facing), split(near), split(out)
    rough = dot1(f[0], o[0])
    rest = four_steps(rough)
    coupling = rough + (dot1(f[0], o[1]) + dot1(f[1], o[0]))
    inner = split(dot3(f, s, NT))
    high, low = split(coupling)
    error = half((coupling - rest.astype(F32)) + (dot1(high, rest) + dot1(low, rest)))
    leading = out + (dot1(s[0], rest) + dot1(s[1], rest))
    mirror = near + (dot1(o[0], rest) + dot1(o[1], rest))
    leading = leading + dot1(half(leading), error)
    mirror = mirror + dot1(half(mirror), error)
    return leading, mirror, away + dot3(split(leading), inner)


def after_trans(leading, mirror, away, into):
    q = split(into)
    trans = dot3(split(leading), q)
    bounced = split(dot3(split(mirror), q))
    return trans, away + dot3(split(into.T), bounced)


def place():
    return lax.axis_index("gx") * lax.axis_size("gy") + lax.axis_index("gy")


def bit(me, distance):
    return me & distance != 0


def lower_upper(h):
    row = lax.broadcasted_iota(jnp.int32, (h, h), 0)
    col = lax.broadcasted_iota(jnp.int32, (h, h), 1)
    return row > col, row < col


def symmetric_rows(x):
    h = x.shape[0] // 2
    below, above = lower_upper(h)
    a, b, c = x[:h, :h], x[:h, h:], x[h:, h:]
    diagonal = jnp.sum(jnp.where(below | above, 0.0, c), axis=0, keepdims=True)
    return jnp.concatenate([b, jnp.where(above, c, a)], 1), diagonal


def store_half(rows, core, ref, start):
    q = rows.shape[0] // 2
    ref[start : start + q, :] = jnp.where(core, rows[q:], rows[:q])


def store_diagonals(one, two, ref, start):
    ref[start : start + PAD, :] = jnp.broadcast_to(jnp.concatenate([one, two], 1), (PAD, 2 * one.shape[1]))


def pack_symmetric(x, core, ref, start):
    rows, diagonal = symmetric_rows(x)
    store_half(rows, core, ref, start)
    store_diagonals(diagonal, diagonal, ref, start + rows.shape[0] // 2)


def joined(near_ref, far_ref, core, lo, hi):
    near, far = near_ref[lo:hi, :], far_ref[lo:hi, :]
    return jnp.concatenate([jnp.where(core, far, near), jnp.where(core, near, far)], 0)


def unpack_symmetric(near_ref, far_ref, core, start, diagonal=None):
    h = near_ref.shape[1] // 2
    q = h // 2
    below, above = lower_upper(h)
    both = joined(near_ref, far_ref, core, start, start + q)
    if diagonal is None:
        diagonal = near_ref[start + q : start + q + 1, :h]
    b, w = both[:, :h], both[:, h:]
    turned = w.T
    a = jnp.where(above, turned, w)
    c = jnp.where(above, w, jnp.where(below, turned, diagonal))
    return jnp.concatenate([jnp.concatenate([a, b], 1), jnp.concatenate([b.T, c], 1)], 0)


def unpack_second(near_ref, far_ref, core, first_ref=None):
    h = near_ref.shape[1] // 2
    diagonal = None if first_ref is None else first_ref[h // 2 : h // 2 + 1, h:]
    return joined(near_ref, far_ref, core, 0, h), unpack_symmetric(near_ref, far_ref, core, h, diagonal)


def send_total(own_side, other_side, trans, same, core, first_ref, second_ref, own_ref):
    turned = trans.T
    near = jnp.where(same, other_side, own_side)
    away = jnp.where(same, own_side, other_side)
    back = jnp.where(same, turned, trans)
    own_ref[0] = near
    own_ref[1] = away
    own_ref[2] = jnp.where(same, trans, turned)
    near_rows, near_diagonal = symmetric_rows(near)
    away_rows, away_diagonal = symmetric_rows(away)
    h = near_rows.shape[0]
    store_half(near_rows, core, first_ref, 0)
    store_diagonals(near_diagonal, away_diagonal, first_ref, h // 2)
    store_half(back, core, second_ref, 0)
    store_half(away_rows, core, second_ref, h)


def first_kernel(section_ref, got1, got2, got3, prefix_ref, *send_refs):
    me = place()
    upper = bit(me, 1)
    left, right, trans = section_ref[0], section_ref[1], section_ref[2]
    pick = lambda a, b: jnp.where(upper, a, b)
    own = pick(left, right), pick(right, left), pick(trans, trans.T)
    leading, mirror, own_side = before_trans(own, pick(got2[0], got1[0]))
    into = pick(got3[0], got3[0].T)
    through, other_side = after_trans(leading, mirror, pick(got1[0], got2[0]), into)
    send_total(own_side, other_side, through, upper == bit(me, 2), upper, *send_refs)
    prefix_ref[0] = pick(other_side, left)
    prefix_ref[1] = pick(own_side, right)
    prefix_ref[2] = pick(through, trans)


def early_kernel(own_ref, near_ref, far_ref, half_ref, *first_ref):
    core = bit(place(), 1)
    facing = unpack_symmetric(near_ref, far_ref, core, 0)
    half = before_trans((own_ref[0], own_ref[1], own_ref[2]), facing)
    for ref in first_ref:
        pack_symmetric(half[2], core, ref, 0)
    for i, x in enumerate(half):
        half_ref[i] = x


def final_kernel(half_ref, near1, near_ref, far_ref, second_ref, trans_ref):
    core = bit(place(), 1)
    into, away = unpack_second(near_ref, far_ref, core, near1)
    trans, other_side = after_trans(half_ref[0], half_ref[1], away, into)
    pack_second(trans, other_side, core, second_ref)
    store_half(trans, core, trans_ref, 0)


def pack_second(back, away, core, ref):
    h = back.shape[0] // 2
    store_half(back, core, ref, 0)
    pack_symmetric(away, core, ref, h)


def late_kernel(distance, half_ref, near1, near_ref, far_ref, *send_refs):
    me = place()
    core = bit(me, 1)
    into, away = unpack_second(near_ref, far_ref, core, near1)
    trans, other_side = after_trans(half_ref[0], half_ref[1], away, into)
    same = bit(me, distance) == bit(me, 2 * distance)
    send_total(half_ref[2], other_side, trans, same, core, *send_refs)


def prefix_kernel(distance, old_ref, near1, far1, near2, far2, new_ref):
    me = place()
    core, upper = bit(me, 1), bit(me, distance)
    facing = unpack_symmetric(near1, far1, core, 0)
    leading, mirror, right = before_trans((old_ref[0], old_ref[1], old_ref[2]), facing)
    into, away = unpack_second(near2, far2, core, near1)
    trans, left = after_trans(leading, mirror, away, into)
    for i, x in enumerate((left, right, trans)):
        new_ref[i] = jnp.where(upper, x, old_ref[i])


def by_third(distance, me, near2, far2, near3, far3):
    third = bit(me, distance // 2)
    return jnp.where(third, near3[...], near2[...]), jnp.where(third, far3[...], far2[...])


def last_early_kernel(distance, old_ref, near2, far2, near3, far3, half_ref, left_out, right_out, trans_out, sems):
    me = place()
    upper = bit(me, distance)

    @pl.when(upper)
    def _():
        facing = unpack_symmetric(*by_third(distance, me, near2, far2, near3, far3), bit(me, 1), 0)
        for i, x in enumerate(before_trans((old_ref[0], old_ref[1], old_ref[2]), facing)):
            half_ref[i] = x

    @pl.when(jnp.logical_not(upper))
    def _():
        outs = left_out, right_out, trans_out
        copies = [pltpu.make_async_copy(old_ref.at[i : i + 1], out, sems.at[i]) for i, out in enumerate(outs)]
        for copy in copies:
            copy.start()
        for copy in copies:
            copy.wait()


def last_kernel(distance, half_ref, near2, far2, near3, far3, near_left, far_left, _l, _r, _t, left_out, right_out, trans_out, new_ref, sems):
    me = place()

    @pl.when(bit(me, distance))
    def _():
        right_copy = pltpu.make_async_copy(half_ref.at[2:3], right_out, sems.at[0])
        trans_copy = pltpu.make_async_copy(new_ref.at[0:1], trans_out, sems.at[1])
        left_copy = pltpu.make_async_copy(new_ref.at[1:2], left_out, sems.at[2])
        right_copy.start()
        core, third, h = bit(me, 1), bit(me, distance // 2), near2.shape[0]
        near = jnp.where(third, near3[:h, :], near2[...])
        far = jnp.where(third, far3[:h, :], far2[...])
        into = joined(near, far, core, 0, h)
        near = jnp.where(third, near3[h:, :], near_left[...])
        far = jnp.where(third, far3[h:, :], far_left[...])
        away = unpack_symmetric(near, far, core, 0)
        q = split(into)
        new_ref[0] = dot3(split(half_ref[0]), q)
        trans_copy.start()
        bounced = split(dot3(split(half_ref[1]), q))
        new_ref[1] = away + dot3(split(into.T), bounced)
        left_copy.start()
        right_copy.wait()
        trans_copy.wait()
        left_copy.wait()


def call(kernel, products, outs, *args, given=(), copied=0, scratch=()):
    vmem, hbm = pl.BlockSpec(memory_space=pltpu.VMEM), pl.BlockSpec(memory_space=pltpu.HBM)
    m = args[0].shape[-1]
    return pl.pallas_call(
        kernel,
        out_shape=[jax.ShapeDtypeStruct(s, F32) for s in outs],
        in_specs=[vmem] * len(args) + [hbm] * len(given),
        out_specs=[vmem] * (len(outs) - copied) + [hbm] * copied,
        input_output_aliases={len(args) + i: len(outs) - copied + i for i in range(len(given))},
        scratch_shapes=scratch,
        cost_estimate=pl.CostEstimate(flops=2 * products * m**3, bytes_accessed=4 * m**2 * len(args), transcendentals=0),
        compiler_params=pltpu.CompilerParams(vmem_limit_bytes=40 * 2**20),
    )(*args, *given)


def shards(refl_left, refl_right, trans):
    m = trans.shape[1]
    levels = lax.axis_size(AXES).bit_length() - 1
    stack = (3, m, m)
    first, second, padded = (m // 4 + PAD, m), (m // 2 + m // 4, m), (m // 2 + m // 4 + PAD, m)
    sections = refl_left, refl_right, trans
    got = [swap(x, 1) for x in sections]
    section = jnp.concatenate(sections, 0)
    prefix, send1, send2, own = call(first_kernel, 36, [stack, first, second, stack], section, *got)
    pending = None
    for level in range(1, levels - 1):
        distance = 1 << level
        bind = lambda kernel: functools.partial(kernel, distance)
        near1, near2 = swap(send1, distance), swap(send2, distance)
        if pending is not None:
            (prefix,) = pending(prefix)
            near1, prefix = lax.optimization_barrier((near1, prefix))
        far1 = swap(near1, 1)
        outs = [stack] + [first] * (level == levels - 2)
        halfway, *sends = call(early_kernel, 27, outs, own, near1, far1)
        near2, halfway = lax.optimization_barrier((near2, halfway))
        far2 = swap(near2, 1)
        pending = lambda old, kernel=bind(prefix_kernel), got=(near1, far1, near2, far2): call(kernel, 36, [stack], old, *got)
        if level < levels - 2:
            send1, send2, own = call(bind(late_kernel), 9, [first, second, stack], halfway, near1, near2, far2)

    distance *= 2
    (send1,) = sends
    first3, first2, left = pair(send1, 1, 3), pair(send1, 1, 2), pair(send1, 0, 2)
    send2, send3 = call(final_kernel, 9, [padded, (m // 2, m)], halfway, near1, near2, far2)
    near3, near2 = pair(send2, 1, 3), pair(send3, 1, 2)
    first3, first2, left, prefix = lax.optimization_barrier((first3, first2, left, prefix))
    (prefix,) = pending(prefix)
    args = prefix, first2, swap(first2, 1), first3, swap(first3, 1)
    far_left, prefix = lax.optimization_barrier((swap(left, 1), prefix))
    args = prefix, *args[1:]
    one, sems = (1, m, m), pltpu.SemaphoreType.DMA((3,))
    kernel = functools.partial(last_early_kernel, distance)
    halfway, *given = call(kernel, 27, [stack, one, one, one], *args, copied=3, scratch=[sems])
    near2, near3, halfway = lax.optimization_barrier((near2, near3, halfway))
    args = halfway, near2, swap(near2, 1), near3, swap(near3, 1), left, far_left
    scratch = [pltpu.VMEM((2, m, m), F32), sems]
    return tuple(call(functools.partial(last_kernel, distance), 9, [one] * 3, *args, given=given, copied=3, scratch=scratch))


def solution(mesh):
    spec = P(AXES, None, None)
    return jax.shard_map(
        shards,
        mesh=mesh,
        in_specs=(spec,) * 3,
        out_specs=(spec,) * 3,
        check_vma=False,
    )
```

```python
import functools

import jax
import jax.numpy as jnp
from jax import lax
from jax.experimental import pallas as pl
from jax.experimental.pallas import tpu as pltpu
from jax.sharding import PartitionSpec as P

AXES = ("gx", "gy")
NS_STEPS = 5
PAD = 8
F32 = jnp.float32
BF16 = jnp.bfloat16
NN = (((1,), (0,)), ((), ()))
NT = (((1,), (1,)), ((), ()))


def swap(block, distance):
    count = lax.axis_size(AXES)
    return lax.ppermute(block, AXES, [(i, i ^ distance) for i in range(count)])


def pair(block, first, second):
    count = lax.axis_size(AXES)
    quarter = count // 4
    shift = (second - first) * quarter
    step = {first: lambda i: i + shift, second: lambda i: i - shift}
    return lax.ppermute(block, AXES, [(i, step.get(i // quarter, lambda i: i ^ 1)(i)) for i in range(count)])


def split(x):
    high = x.astype(BF16)
    return high, (x - high.astype(F32)).astype(BF16)


def dot1(a, b, dims=NN):
    h = a.shape[0] // 2
    parts = [lax.dot_general(x, b, dims, preferred_element_type=F32) for x in (a[:h], a[h:])]
    return jnp.concatenate(parts, 0)


def dot3(a, b, dims=NN):
    return dot1(a[0], b[0], dims) + (dot1(a[0], b[1], dims) + dot1(a[1], b[0], dims))


def half(x):
    return x.astype(BF16)


def four_steps(power):
    rest, power = power, half(power)
    for _ in range(NS_STEPS - 1):
        squared = dot1(power, power)
        power = half(squared)
        rest = rest + squared + dot1(half(rest), power)
    return half(rest)


def before_trans(own, facing):
    near, away, out = own
    f, o, s = split(facing), split(near), split(out)
    rough = dot1(f[0], o[0])
    rest = four_steps(rough)
    coupling = rough + (dot1(f[0], o[1]) + dot1(f[1], o[0]))
    inner = split(dot3(f, s, NT))
    high, low = split(coupling)
    error = half((coupling - rest.astype(F32)) + (dot1(high, rest) + dot1(low, rest)))
    leading = out + (dot1(s[0], rest) + dot1(s[1], rest))
    mirror = near + (dot1(o[0], rest) + dot1(o[1], rest))
    leading = leading + dot1(half(leading), error)
    mirror = mirror + dot1(half(mirror), error)
    return leading, mirror, away + dot3(split(leading), inner)


def after_trans(leading, mirror, away, into):
    q = split(into)
    trans = dot3(split(leading), q)
    bounced = split(dot3(split(mirror), q))
    return trans, away + dot3(split(into.T), bounced)


def place():
    return lax.axis_index("gx") * lax.axis_size("gy") + lax.axis_index("gy")


def bit(me, distance):
    return me & distance != 0


def lower_upper(h):
    row = lax.broadcasted_iota(jnp.int32, (h, h), 0)
    col = lax.broadcasted_iota(jnp.int32, (h, h), 1)
    return row > col, row < col


def symmetric_rows(x):
    h = x.shape[0] // 2
    below, above = lower_upper(h)
    a, b, c = x[:h, :h], x[:h, h:], x[h:, h:]
    diagonal = jnp.sum(jnp.where(below | above, 0.0, c), axis=0, keepdims=True)
    return jnp.concatenate([b, jnp.where(above, c, a)], 1), diagonal


def store_half(rows, core, ref, start):
    q = rows.shape[0] // 2
    ref[start : start + q, :] = jnp.where(core, rows[q:], rows[:q])


def store_diagonals(one, two, ref, start):
    ref[start : start + PAD, :] = jnp.broadcast_to(jnp.concatenate([one, two], 1), (PAD, 2 * one.shape[1]))


def pack_symmetric(x, core, ref, start):
    rows, diagonal = symmetric_rows(x)
    store_half(rows, core, ref, start)
    store_diagonals(diagonal, diagonal, ref, start + rows.shape[0] // 2)


def joined(near_ref, far_ref, core, lo, hi):
    near, far = near_ref[lo:hi, :], far_ref[lo:hi, :]
    return jnp.concatenate([jnp.where(core, far, near), jnp.where(core, near, far)], 0)


def unpack_symmetric(near_ref, far_ref, core, start, diagonal=None):
    h = near_ref.shape[1] // 2
    q = h // 2
    below, above = lower_upper(h)
    both = joined(near_ref, far_ref, core, start, start + q)
    if diagonal is None:
        diagonal = near_ref[start + q : start + q + 1, :h]
    b, w = both[:, :h], both[:, h:]
    turned = w.T
    a = jnp.where(above, turned, w)
    c = jnp.where(above, w, jnp.where(below, turned, diagonal))
    return jnp.concatenate([jnp.concatenate([a, b], 1), jnp.concatenate([b.T, c], 1)], 0)


def unpack_second(near_ref, far_ref, core, first_ref=None):
    h = near_ref.shape[1] // 2
    diagonal = None if first_ref is None else first_ref[h // 2 : h // 2 + 1, h:]
    return joined(near_ref, far_ref, core, 0, h), unpack_symmetric(near_ref, far_ref, core, h, diagonal)


def send_total(own_side, other_side, trans, same, core, first_ref, second_ref, own_ref):
    turned = trans.T
    near = jnp.where(same, other_side, own_side)
    away = jnp.where(same, own_side, other_side)
    back = jnp.where(same, turned, trans)
    own_ref[0] = near
    own_ref[1] = away
    own_ref[2] = jnp.where(same, trans, turned)
    near_rows, near_diagonal = symmetric_rows(near)
    away_rows, away_diagonal = symmetric_rows(away)
    h = near_rows.shape[0]
    store_half(near_rows, core, first_ref, 0)
    store_diagonals(near_diagonal, away_diagonal, first_ref, h // 2)
    store_half(back, core, second_ref, 0)
    store_half(away_rows, core, second_ref, h)


def first_kernel(section_ref, got1, got2, got3, prefix_ref, *send_refs):
    me = place()
    upper = bit(me, 1)
    left, right, trans = section_ref[0], section_ref[1], section_ref[2]
    pick = lambda a, b: jnp.where(upper, a, b)
    own = pick(left, right), pick(right, left), pick(trans, trans.T)
    leading, mirror, own_side = before_trans(own, pick(got2[0], got1[0]))
    into = pick(got3[0], got3[0].T)
    through, other_side = after_trans(leading, mirror, pick(got1[0], got2[0]), into)
    send_total(own_side, other_side, through, upper == bit(me, 2), upper, *send_refs)
    prefix_ref[0] = pick(other_side, left)
    prefix_ref[1] = pick(own_side, right)
    prefix_ref[2] = pick(through, trans)


def early_kernel(own_ref, near_ref, far_ref, half_ref):
    facing = unpack_symmetric(near_ref, far_ref, bit(place(), 1), 0)
    for i, x in enumerate(before_trans((own_ref[0], own_ref[1], own_ref[2]), facing)):
        half_ref[i] = x


def only_quarter_1(distance, body, *out_refs):
    mine = place() // distance == 1
    pl.when(mine)(body)

    @pl.when(jnp.logical_not(mine))
    def _():
        for ref in out_refs:
            ref[...] = jnp.zeros_like(ref)


def final_early_kernel(distance, own_ref, near_ref, far_ref, half_ref, first_ref):
    def body():
        early_kernel(own_ref, near_ref, far_ref, half_ref)
        pack_symmetric(half_ref[2], bit(place(), 1), first_ref, 0)

    only_quarter_1(distance, body, half_ref, first_ref)


def final_kernel(distance, half_ref, near1, near_ref, far_ref, second_ref):
    def body():
        core = bit(place(), 1)
        into, away = unpack_second(near_ref, far_ref, core, near1)
        trans, other_side = after_trans(half_ref[0], half_ref[1], away, into)
        pack_second(trans, other_side, core, second_ref)

    only_quarter_1(distance, body, second_ref)


def pack_second(back, away, core, ref):
    h = back.shape[0] // 2
    store_half(back, core, ref, 0)
    pack_symmetric(away, core, ref, h)


def late_kernel(distance, half_ref, near1, near_ref, far_ref, *send_refs):
    me = place()
    core = bit(me, 1)
    into, away = unpack_second(near_ref, far_ref, core, near1)
    trans, other_side = after_trans(half_ref[0], half_ref[1], away, into)
    same = bit(me, distance) == bit(me, 2 * distance)
    send_total(half_ref[2], other_side, trans, same, core, *send_refs)


def prefix_kernel(distance, old_ref, near1, far1, near2, far2, new_ref):
    me = place()
    core, upper = bit(me, 1), bit(me, distance)
    facing = unpack_symmetric(near1, far1, core, 0)
    leading, mirror, right = before_trans((old_ref[0], old_ref[1], old_ref[2]), facing)
    into, away = unpack_second(near2, far2, core, near1)
    trans, left = after_trans(leading, mirror, away, into)
    for i, x in enumerate((left, right, trans)):
        new_ref[i] = jnp.where(upper, x, old_ref[i])


def by_third(distance, me, near2, far2, near3, far3):
    third = bit(me, distance // 2)
    return jnp.where(third, near3[...], near2[...]), jnp.where(third, far3[...], far2[...])


def last_early_kernel(distance, old_ref, near2, far2, near3, far3, half_ref, left_out, right_out, trans_out, sems):
    me = place()
    upper = bit(me, distance)

    @pl.when(upper)
    def _():
        facing = unpack_symmetric(*by_third(distance, me, near2, far2, near3, far3), bit(me, 1), 0)
        for i, x in enumerate(before_trans((old_ref[0], old_ref[1], old_ref[2]), facing)):
            half_ref[i] = x

    @pl.when(jnp.logical_not(upper))
    def _():
        outs = left_out, right_out, trans_out
        copies = [pltpu.make_async_copy(old_ref.at[i : i + 1], out, sems.at[i]) for i, out in enumerate(outs)]
        for copy in copies:
            copy.start()
        for copy in copies:
            copy.wait()


def last_kernel(distance, half_ref, near2, far2, near3, far3, _l, _r, _t, left_out, right_out, trans_out, new_ref, sems):
    me = place()

    @pl.when(bit(me, distance))
    def _():
        right_copy = pltpu.make_async_copy(half_ref.at[2:3], right_out, sems.at[0])
        trans_copy = pltpu.make_async_copy(new_ref.at[0:1], trans_out, sems.at[1])
        left_copy = pltpu.make_async_copy(new_ref.at[1:2], left_out, sems.at[2])
        right_copy.start()
        into, away = unpack_second(*by_third(distance, me, near2, far2, near3, far3), bit(me, 1))
        q = split(into)
        new_ref[0] = dot3(split(half_ref[0]), q)
        trans_copy.start()
        bounced = split(dot3(split(half_ref[1]), q))
        new_ref[1] = away + dot3(split(into.T), bounced)
        left_copy.start()
        right_copy.wait()
        trans_copy.wait()
        left_copy.wait()


def call(kernel, products, outs, *args, given=(), copied=0, scratch=()):
    vmem, hbm = pl.BlockSpec(memory_space=pltpu.VMEM), pl.BlockSpec(memory_space=pltpu.HBM)
    m = args[0].shape[-1]
    return pl.pallas_call(
        kernel,
        out_shape=[jax.ShapeDtypeStruct(s, F32) for s in outs],
        in_specs=[vmem] * len(args) + [hbm] * len(given),
        out_specs=[vmem] * (len(outs) - copied) + [hbm] * copied,
        input_output_aliases={len(args) + i: len(outs) - copied + i for i in range(len(given))},
        scratch_shapes=scratch,
        cost_estimate=pl.CostEstimate(flops=2 * products * m**3, bytes_accessed=4 * m**2 * len(args), transcendentals=0),
        compiler_params=pltpu.CompilerParams(vmem_limit_bytes=40 * 2**20),
    )(*args, *given)


def shards(refl_left, refl_right, trans):
    m = trans.shape[1]
    levels = lax.axis_size(AXES).bit_length() - 1
    stack = (3, m, m)
    first, second, padded = (m // 4 + PAD, m), (m // 2 + m // 4, m), (m // 2 + m // 4 + PAD, m)
    sections = refl_left, refl_right, trans
    got = [swap(x, 1) for x in sections]
    section = jnp.concatenate(sections, 0)
    prefix, send1, send2, own = call(first_kernel, 36, [stack, first, second, stack], section, *got)
    pending = None
    for level in range(1, levels - 1):
        distance = 1 << level
        bind = lambda kernel: functools.partial(kernel, distance)
        near1, near2 = swap(send1, distance), swap(send2, distance)
        if pending is not None:
            (prefix,) = pending(prefix)
            near1, prefix = lax.optimization_barrier((near1, prefix))
        far1 = swap(near1, 1)
        if level < levels - 2:
            (halfway,) = call(early_kernel, 27, [stack], own, near1, far1)
        else:
            halfway, send1 = call(bind(final_early_kernel), 27, [stack, first], own, near1, far1)
        near2, halfway = lax.optimization_barrier((near2, halfway))
        far2 = swap(near2, 1)
        pending = lambda old, kernel=bind(prefix_kernel), got=(near1, far1, near2, far2): call(kernel, 36, [stack], old, *got)
        if level < levels - 2:
            send1, send2, own = call(bind(late_kernel), 9, [first, second, stack], halfway, near1, near2, far2)

    first3, first2 = pair(send1, 1, 3), pair(send1, 1, 2)
    (send2,) = call(bind(final_kernel), 9, [padded], halfway, near1, near2, far2)
    distance *= 2
    near3, near2 = pair(send2, 1, 3), pair(send2, 1, 2)
    first3, first2, prefix = lax.optimization_barrier((first3, first2, prefix))
    (prefix,) = pending(prefix)
    args = prefix, first2, swap(first2, 1), first3, swap(first3, 1)
    one, sems = (1, m, m), pltpu.SemaphoreType.DMA((3,))
    kernel = functools.partial(last_early_kernel, distance)
    halfway, *given = call(kernel, 27, [stack, one, one, one], *args, copied=3, scratch=[sems])
    near3, halfway = lax.optimization_barrier((near3, halfway))
    far3 = swap(near3, 1)
    near2, far3 = lax.optimization_barrier((near2, far3))
    args = halfway, near2, swap(near2, 1), near3, far3
    scratch = [pltpu.VMEM((2, m, m), F32), sems]
    return tuple(call(functools.partial(last_kernel, distance), 9, [one] * 3, *args, given=given, copied=3, scratch=scratch))


def solution(mesh):
    spec = P(AXES, None, None)
    return jax.shard_map(
        shards,
        mesh=mesh,
        in_specs=(spec,) * 3,
        out_specs=(spec,) * 3,
        check_vma=False,
    )
```

```python
import functools

import jax
import jax.numpy as jnp
from jax import lax
from jax.experimental import pallas as pl
from jax.experimental.pallas import tpu as pltpu
from jax.sharding import PartitionSpec as P

AXES = ("gx", "gy")
NS_STEPS = 5
PAD = 8
F32 = jnp.float32
BF16 = jnp.bfloat16
NN = (((1,), (0,)), ((), ()))
NT = (((1,), (1,)), ((), ()))


def swap(block, distance):
    count = lax.axis_size(AXES)
    return lax.ppermute(block, AXES, [(i, i ^ distance) for i in range(count)])


def pair(block, first, second):
    count = lax.axis_size(AXES)
    quarter = count // 4
    shift = (second - first) * quarter
    step = {first: lambda i: i + shift, second: lambda i: i - shift}
    return lax.ppermute(block, AXES, [(i, step.get(i // quarter, lambda i: i ^ 1)(i)) for i in range(count)])


def split(x):
    high = x.astype(BF16)
    return high, (x - high.astype(F32)).astype(BF16)


def dot(a, b, dims=NN):
    return lax.dot_general(a, b, dims, preferred_element_type=F32)


def dot1(a, b, dims=NN):
    h = a.shape[0] // 2
    return jnp.concatenate([dot(a[:h], b, dims), dot(a[h:], b, dims)], 0)


def dot3(a, b, dims=NN, one=dot1):
    return one(a[0], b[0], dims) + (one(a[0], b[1], dims) + one(a[1], b[0], dims))


def half(x):
    return x.astype(BF16)


def four_steps(power):
    rest, high = power, half(power)
    squared = dot1(high, high)
    for step in range(1, NS_STEPS):
        high = half(squared)
        following = dot1(high, high) if step < NS_STEPS - 1 else None
        rest = rest + squared + dot1(half(rest), high)
        squared = following
    return half(rest)


def before_trans(own, facing):
    near, away, out = own
    f, o, s = split(facing), split(near), split(out)
    rough = dot1(f[0], o[0])
    coupling = rough + (dot1(f[0], o[1]) + dot1(f[1], o[0]))
    inner = split(dot3(f, s, NT, dot))
    rest = four_steps(rough)
    high, low = split(coupling)
    error = half((coupling - rest.astype(F32)) + (dot1(high, rest) + dot1(low, rest)))
    leading = out + (dot1(s[0], rest) + dot1(s[1], rest))
    mirror = near + (dot1(o[0], rest) + dot1(o[1], rest))
    leading = leading + dot1(half(leading), error)
    mirror = mirror + dot1(half(mirror), error)
    return leading, mirror, away + dot3(split(leading), inner, NN, dot)


def after_trans(leading, mirror, away, into):
    q = split(into)
    trans = dot3(split(leading), q)
    bounced = split(dot3(split(mirror), q))
    return trans, away + dot3(split(into.T), bounced)


def place():
    return lax.axis_index("gx") * lax.axis_size("gy") + lax.axis_index("gy")


def bit(me, distance):
    return me & distance != 0


def lower_upper(h):
    row = lax.broadcasted_iota(jnp.int32, (h, h), 0)
    col = lax.broadcasted_iota(jnp.int32, (h, h), 1)
    return row > col, row < col


def symmetric_rows(x):
    h = x.shape[0] // 2
    below, above = lower_upper(h)
    a, b, c = x[:h, :h], x[:h, h:], x[h:, h:]
    diagonal = jnp.sum(jnp.where(below | above, 0.0, c), axis=0, keepdims=True)
    return jnp.concatenate([b, jnp.where(above, c, a)], 1), diagonal


def store_half(rows, core, ref, start):
    q = rows.shape[0] // 2
    ref[start : start + q, :] = jnp.where(core, rows[q:], rows[:q])


def store_diagonals(one, two, ref, start):
    ref[start : start + PAD, :] = jnp.broadcast_to(jnp.concatenate([one, two], 1), (PAD, 2 * one.shape[1]))


def pack_symmetric(x, core, ref, start):
    rows, diagonal = symmetric_rows(x)
    store_half(rows, core, ref, start)
    store_diagonals(diagonal, diagonal, ref, start + rows.shape[0] // 2)


def joined(near_ref, far_ref, core, lo, hi):
    near, far = near_ref[lo:hi, :], far_ref[lo:hi, :]
    return jnp.concatenate([jnp.where(core, far, near), jnp.where(core, near, far)], 0)


def unpack_symmetric(near_ref, far_ref, core, start, diagonal=None):
    h = near_ref.shape[1] // 2
    q = h // 2
    below, above = lower_upper(h)
    both = joined(near_ref, far_ref, core, start, start + q)
    if diagonal is None:
        diagonal = near_ref[start + q : start + q + 1, :h]
    b, w = both[:, :h], both[:, h:]
    turned = w.T
    a = jnp.where(above, turned, w)
    c = jnp.where(above, w, jnp.where(below, turned, diagonal))
    return jnp.concatenate([jnp.concatenate([a, b], 1), jnp.concatenate([b.T, c], 1)], 0)


def unpack_second(near_ref, far_ref, core, first_ref=None):
    h = near_ref.shape[1] // 2
    diagonal = None if first_ref is None else first_ref[h // 2 : h // 2 + 1, h:]
    return joined(near_ref, far_ref, core, 0, h), unpack_symmetric(near_ref, far_ref, core, h, diagonal)


def send_total(own_side, other_side, trans, same, core, first_ref, second_ref, own_ref):
    turned = trans.T
    near = jnp.where(same, other_side, own_side)
    away = jnp.where(same, own_side, other_side)
    back = jnp.where(same, turned, trans)
    own_ref[0] = near
    own_ref[1] = away
    own_ref[2] = jnp.where(same, trans, turned)
    near_rows, near_diagonal = symmetric_rows(near)
    away_rows, away_diagonal = symmetric_rows(away)
    h = near_rows.shape[0]
    store_half(near_rows, core, first_ref, 0)
    store_diagonals(near_diagonal, away_diagonal, first_ref, h // 2)
    store_half(back, core, second_ref, 0)
    store_half(away_rows, core, second_ref, h)


def first_kernel(section_ref, got1, got2, got3, prefix_ref, *send_refs):
    me = place()
    upper = bit(me, 1)
    left, right, trans = section_ref[0], section_ref[1], section_ref[2]
    pick = lambda a, b: jnp.where(upper, a, b)
    own = pick(left, right), pick(right, left), pick(trans, trans.T)
    leading, mirror, own_side = before_trans(own, pick(got2[0], got1[0]))
    into = pick(got3[0], got3[0].T)
    through, other_side = after_trans(leading, mirror, pick(got1[0], got2[0]), into)
    send_total(own_side, other_side, through, upper == bit(me, 2), upper, *send_refs)
    prefix_ref[0] = pick(other_side, left)
    prefix_ref[1] = pick(own_side, right)
    prefix_ref[2] = pick(through, trans)


def early_kernel(own_ref, near_ref, far_ref, half_ref):
    facing = unpack_symmetric(near_ref, far_ref, bit(place(), 1), 0)
    for i, x in enumerate(before_trans((own_ref[0], own_ref[1], own_ref[2]), facing)):
        half_ref[i] = x


def only_quarter_1(distance, body, *out_refs):
    mine = place() // distance == 1
    pl.when(mine)(body)

    @pl.when(jnp.logical_not(mine))
    def _():
        for ref in out_refs:
            ref[...] = jnp.zeros_like(ref)


def final_early_kernel(distance, own_ref, near_ref, far_ref, half_ref, first_ref):
    def body():
        early_kernel(own_ref, near_ref, far_ref, half_ref)
        pack_symmetric(half_ref[2], bit(place(), 1), first_ref, 0)

    only_quarter_1(distance, body, half_ref, first_ref)


def final_kernel(distance, half_ref, near1, near_ref, far_ref, second_ref):
    def body():
        core = bit(place(), 1)
        into, away = unpack_second(near_ref, far_ref, core, near1)
        trans, other_side = after_trans(half_ref[0], half_ref[1], away, into)
        pack_second(trans, other_side, core, second_ref)

    only_quarter_1(distance, body, second_ref)


def pack_second(back, away, core, ref):
    h = back.shape[0] // 2
    store_half(back, core, ref, 0)
    pack_symmetric(away, core, ref, h)


def late_kernel(distance, half_ref, near1, near_ref, far_ref, *send_refs):
    me = place()
    core = bit(me, 1)
    into, away = unpack_second(near_ref, far_ref, core, near1)
    trans, other_side = after_trans(half_ref[0], half_ref[1], away, into)
    same = bit(me, distance) == bit(me, 2 * distance)
    send_total(half_ref[2], other_side, trans, same, core, *send_refs)


def prefix_kernel(distance, old_ref, near1, far1, near2, far2, new_ref):
    me = place()
    core, upper = bit(me, 1), bit(me, distance)
    facing = unpack_symmetric(near1, far1, core, 0)
    leading, mirror, right = before_trans((old_ref[0], old_ref[1], old_ref[2]), facing)
    into, away = unpack_second(near2, far2, core, near1)
    trans, left = after_trans(leading, mirror, away, into)
    for i, x in enumerate((left, right, trans)):
        new_ref[i] = jnp.where(upper, x, old_ref[i])


def by_third(distance, me, near2, far2, near3, far3):
    third = bit(me, distance // 2)
    return jnp.where(third, near3[...], near2[...]), jnp.where(third, far3[...], far2[...])


def last_early_kernel(distance, old_ref, near2, far2, near3, far3, half_ref, left_out, right_out, trans_out, sems):
    me = place()
    upper = bit(me, distance)

    @pl.when(upper)
    def _():
        facing = unpack_symmetric(*by_third(distance, me, near2, far2, near3, far3), bit(me, 1), 0)
        for i, x in enumerate(before_trans((old_ref[0], old_ref[1], old_ref[2]), facing)):
            half_ref[i] = x

    @pl.when(jnp.logical_not(upper))
    def _():
        outs = left_out, right_out, trans_out
        copies = [pltpu.make_async_copy(old_ref.at[i : i + 1], out, sems.at[i]) for i, out in enumerate(outs)]
        for copy in copies:
            copy.start()
        for copy in copies:
            copy.wait()


def last_kernel(distance, half_ref, near2, far2, near3, far3, _l, _r, _t, left_out, right_out, trans_out, new_ref, sems):
    me = place()

    @pl.when(bit(me, distance))
    def _():
        right_copy = pltpu.make_async_copy(half_ref.at[2:3], right_out, sems.at[0])
        trans_copy = pltpu.make_async_copy(new_ref.at[0:1], trans_out, sems.at[1])
        left_copy = pltpu.make_async_copy(new_ref.at[1:2], left_out, sems.at[2])
        right_copy.start()
        into, away = unpack_second(*by_third(distance, me, near2, far2, near3, far3), bit(me, 1))
        q = split(into)
        new_ref[0] = dot3(split(half_ref[0]), q)
        trans_copy.start()
        bounced = split(dot3(split(half_ref[1]), q))
        new_ref[1] = away + dot3(split(into.T), bounced)
        left_copy.start()
        right_copy.wait()
        trans_copy.wait()
        left_copy.wait()


def call(kernel, products, outs, *args, given=(), copied=0, scratch=()):
    vmem, hbm = pl.BlockSpec(memory_space=pltpu.VMEM), pl.BlockSpec(memory_space=pltpu.HBM)
    m = args[0].shape[-1]
    return pl.pallas_call(
        kernel,
        out_shape=[jax.ShapeDtypeStruct(s, F32) for s in outs],
        in_specs=[vmem] * len(args) + [hbm] * len(given),
        out_specs=[vmem] * (len(outs) - copied) + [hbm] * copied,
        input_output_aliases={len(args) + i: len(outs) - copied + i for i in range(len(given))},
        scratch_shapes=scratch,
        cost_estimate=pl.CostEstimate(flops=2 * products * m**3, bytes_accessed=4 * m**2 * len(args), transcendentals=0),
        compiler_params=pltpu.CompilerParams(vmem_limit_bytes=40 * 2**20),
    )(*args, *given)


def shards(refl_left, refl_right, trans):
    m = trans.shape[1]
    levels = lax.axis_size(AXES).bit_length() - 1
    stack = (3, m, m)
    first, second, padded = (m // 4 + PAD, m), (m // 2 + m // 4, m), (m // 2 + m // 4 + PAD, m)
    sections = refl_left, refl_right, trans
    got = [swap(x, 1) for x in sections]
    section = jnp.concatenate(sections, 0)
    prefix, send1, send2, own = call(first_kernel, 36, [stack, first, second, stack], section, *got)
    pending = None
    for level in range(1, levels - 1):
        distance = 1 << level
        bind = lambda kernel: functools.partial(kernel, distance)
        near1, near2 = swap(send1, distance), swap(send2, distance)
        if pending is not None:
            (prefix,) = pending(prefix)
            near1, prefix = lax.optimization_barrier((near1, prefix))
        far1 = swap(near1, 1)
        if level < levels - 2:
            (halfway,) = call(early_kernel, 27, [stack], own, near1, far1)
        else:
            halfway, send1 = call(bind(final_early_kernel), 27, [stack, first], own, near1, far1)
        near2, halfway = lax.optimization_barrier((near2, halfway))
        far2 = swap(near2, 1)
        pending = lambda old, kernel=bind(prefix_kernel), got=(near1, far1, near2, far2): call(kernel, 36, [stack], old, *got)
        if level < levels - 2:
            send1, send2, own = call(bind(late_kernel), 9, [first, second, stack], halfway, near1, near2, far2)

    first3, first2 = pair(send1, 1, 3), pair(send1, 1, 2)
    (send2,) = call(bind(final_kernel), 9, [padded], halfway, near1, near2, far2)
    distance *= 2
    near3, near2 = pair(send2, 1, 3), pair(send2, 1, 2)
    first3, first2, prefix = lax.optimization_barrier((first3, first2, prefix))
    (prefix,) = pending(prefix)
    args = prefix, first2, swap(first2, 1), first3, swap(first3, 1)
    one, sems = (1, m, m), pltpu.SemaphoreType.DMA((3,))
    kernel = functools.partial(last_early_kernel, distance)
    halfway, *given = call(kernel, 27, [stack, one, one, one], *args, copied=3, scratch=[sems])
    near3, halfway = lax.optimization_barrier((near3, halfway))
    far3 = swap(near3, 1)
    near2, far3 = lax.optimization_barrier((near2, far3))
    args = halfway, near2, swap(near2, 1), near3, far3
    scratch = [pltpu.VMEM((2, m, m), F32), sems]
    return tuple(call(functools.partial(last_kernel, distance), 9, [one] * 3, *args, given=given, copied=3, scratch=scratch))


def solution(mesh):
    spec = P(AXES, None, None)
    return jax.shard_map(
        shards,
        mesh=mesh,
        in_specs=(spec,) * 3,
        out_specs=(spec,) * 3,
        check_vma=False,
    )
```

```python
import functools

import jax
import jax.numpy as jnp
from jax import lax
from jax.experimental import pallas as pl
from jax.experimental.pallas import tpu as pltpu
from jax.sharding import PartitionSpec as P

AXES = ("gx", "gy")
NS_STEPS = 5
PAD = 8
F32 = jnp.float32
BF16 = jnp.bfloat16
NN = (((1,), (0,)), ((), ()))
NT = (((1,), (1,)), ((), ()))


def swap(block, distance):
    count = lax.axis_size(AXES)
    return lax.ppermute(block, AXES, [(i, i ^ distance) for i in range(count)])


def pair(block, first, second):
    count = lax.axis_size(AXES)
    quarter = count // 4
    shift = (second - first) * quarter
    step = {first: lambda i: i + shift, second: lambda i: i - shift}
    return lax.ppermute(block, AXES, [(i, step.get(i // quarter, lambda i: i ^ 1)(i)) for i in range(count)])


def split(x):
    high = x.astype(BF16)
    return high, (x - high.astype(F32)).astype(BF16)


def dot(a, b, dims=NN):
    return lax.dot_general(a, b, dims, preferred_element_type=F32)


def dot1(a, b, dims=NN):
    h = a.shape[0] // 2
    return jnp.concatenate([dot(a[:h], b, dims), dot(a[h:], b, dims)], 0)


def dot3(a, b, dims=NN, one=dot1):
    return one(a[0], b[0], dims) + (one(a[0], b[1], dims) + one(a[1], b[0], dims))


def half(x):
    return x.astype(BF16)


def four_steps(power):
    rest, high = power, half(power)
    squared = dot1(high, high)
    for step in range(1, NS_STEPS):
        high = half(squared)
        following = dot1(high, high) if step < NS_STEPS - 1 else None
        rest = rest + squared + dot1(half(rest), high)
        squared = following
    return half(rest)


def before_trans(own, facing):
    near, away, out = own
    f, o, s = split(facing), split(near), split(out)
    rough = dot1(f[0], o[0])
    coupling = rough + (dot1(f[0], o[1]) + dot1(f[1], o[0]))
    inner = split(dot3(f, s, NT, dot))
    rest = four_steps(rough)
    high, low = split(coupling)
    error = half((coupling - rest.astype(F32)) + (dot1(high, rest) + dot1(low, rest)))
    leading = out + (dot1(s[0], rest) + dot1(s[1], rest))
    mirror = near + (dot1(o[0], rest) + dot1(o[1], rest))
    leading = leading + dot1(half(leading), error)
    mirror = mirror + dot1(half(mirror), error)
    return leading, mirror, away + dot3(split(leading), inner, NN, dot)


def after_trans(leading, mirror, away, into):
    q = split(into)
    bounced = split(dot3(split(mirror), q))
    trans = dot3(split(leading), q)
    return trans, away + dot3(split(into.T), bounced)


def place():
    return lax.axis_index("gx") * lax.axis_size("gy") + lax.axis_index("gy")


def bit(me, distance):
    return me & distance != 0


def lower_upper(h):
    row = lax.broadcasted_iota(jnp.int32, (h, h), 0)
    col = lax.broadcasted_iota(jnp.int32, (h, h), 1)
    return row > col, row < col


def symmetric_rows(x):
    h = x.shape[0] // 2
    below, above = lower_upper(h)
    a, b, c = x[:h, :h], x[:h, h:], x[h:, h:]
    diagonal = jnp.sum(jnp.where(below | above, 0.0, c), axis=0, keepdims=True)
    return jnp.concatenate([b, jnp.where(above, c, a)], 1), diagonal


def store_half(rows, core, ref, start):
    q = rows.shape[0] // 2
    ref[start : start + q, :] = jnp.where(core, rows[q:], rows[:q])


def store_diagonals(one, two, ref, start):
    ref[start : start + PAD, :] = jnp.broadcast_to(jnp.concatenate([one, two], 1), (PAD, 2 * one.shape[1]))


def pack_symmetric(x, core, ref, start):
    rows, diagonal = symmetric_rows(x)
    store_half(rows, core, ref, start)
    store_diagonals(diagonal, diagonal, ref, start + rows.shape[0] // 2)


def joined(near_ref, far_ref, core, lo, hi):
    near, far = near_ref[lo:hi, :], far_ref[lo:hi, :]
    return jnp.concatenate([jnp.where(core, far, near), jnp.where(core, near, far)], 0)


def unpack_symmetric(near_ref, far_ref, core, start, diagonal=None):
    h = near_ref.shape[1] // 2
    q = h // 2
    below, above = lower_upper(h)
    both = joined(near_ref, far_ref, core, start, start + q)
    if diagonal is None:
        diagonal = near_ref[start + q : start + q + 1, :h]
    b, w = both[:, :h], both[:, h:]
    turned = w.T
    a = jnp.where(above, turned, w)
    c = jnp.where(above, w, jnp.where(below, turned, diagonal))
    return jnp.concatenate([jnp.concatenate([a, b], 1), jnp.concatenate([b.T, c], 1)], 0)


def unpack_second(near_ref, far_ref, core, first_ref=None):
    h = near_ref.shape[1] // 2
    diagonal = None if first_ref is None else first_ref[h // 2 : h // 2 + 1, h:]
    return joined(near_ref, far_ref, core, 0, h), unpack_symmetric(near_ref, far_ref, core, h, diagonal)


def send_total(own_side, other_side, trans, same, core, first_ref, second_ref, own_ref):
    turned = trans.T
    near = jnp.where(same, other_side, own_side)
    away = jnp.where(same, own_side, other_side)
    back = jnp.where(same, turned, trans)
    own_ref[0] = near
    own_ref[1] = away
    own_ref[2] = jnp.where(same, trans, turned)
    near_rows, near_diagonal = symmetric_rows(near)
    away_rows, away_diagonal = symmetric_rows(away)
    h = near_rows.shape[0]
    store_half(near_rows, core, first_ref, 0)
    store_diagonals(near_diagonal, away_diagonal, first_ref, h // 2)
    store_half(back, core, second_ref, 0)
    store_half(away_rows, core, second_ref, h)


def first_early_kernel(section_ref, got1, got2, half_ref):
    upper = bit(place(), 1)
    left, right, trans = section_ref[0], section_ref[1], section_ref[2]
    pick = lambda a, b: jnp.where(upper, a, b)
    own = pick(left, right), pick(right, left), pick(trans, trans.T)
    for i, x in enumerate(before_trans(own, pick(got2[0], got1[0]))):
        half_ref[i] = x


def first_late_kernel(section_ref, half_ref, got1, got2, got3, prefix_ref, *send_refs):
    me = place()
    upper = bit(me, 1)
    pick = lambda a, b: jnp.where(upper, a, b)
    own_side, into = half_ref[2], pick(got3[0], got3[0].T)
    through, other_side = after_trans(half_ref[0], half_ref[1], pick(got1[0], got2[0]), into)
    send_total(own_side, other_side, through, upper == bit(me, 2), upper, *send_refs)
    prefix_ref[0] = pick(other_side, section_ref[0])
    prefix_ref[1] = pick(own_side, section_ref[1])
    prefix_ref[2] = pick(through, section_ref[2])


def early_kernel(own_ref, near_ref, far_ref, half_ref):
    facing = unpack_symmetric(near_ref, far_ref, bit(place(), 1), 0)
    for i, x in enumerate(before_trans((own_ref[0], own_ref[1], own_ref[2]), facing)):
        half_ref[i] = x


def only_quarter_1(distance, body, *out_refs):
    mine = place() // distance == 1
    pl.when(mine)(body)

    @pl.when(jnp.logical_not(mine))
    def _():
        for ref in out_refs:
            ref[...] = jnp.zeros_like(ref)


def final_early_kernel(distance, own_ref, near_ref, far_ref, half_ref, first_ref):
    def body():
        early_kernel(own_ref, near_ref, far_ref, half_ref)
        pack_symmetric(half_ref[2], bit(place(), 1), first_ref, 0)

    only_quarter_1(distance, body, half_ref, first_ref)


def final_kernel(distance, half_ref, near1, near_ref, far_ref, second_ref):
    def body():
        core = bit(place(), 1)
        into, away = unpack_second(near_ref, far_ref, core, near1)
        trans, other_side = after_trans(half_ref[0], half_ref[1], away, into)
        pack_second(trans, other_side, core, second_ref)

    only_quarter_1(distance, body, second_ref)


def pack_second(back, away, core, ref):
    h = back.shape[0] // 2
    store_half(back, core, ref, 0)
    pack_symmetric(away, core, ref, h)


def late_kernel(distance, half_ref, near1, near_ref, far_ref, *send_refs):
    me = place()
    core = bit(me, 1)
    into, away = unpack_second(near_ref, far_ref, core, near1)
    trans, other_side = after_trans(half_ref[0], half_ref[1], away, into)
    same = bit(me, distance) == bit(me, 2 * distance)
    send_total(half_ref[2], other_side, trans, same, core, *send_refs)


def prefix_kernel(distance, old_ref, near1, far1, near2, far2, new_ref):
    me = place()
    core, upper = bit(me, 1), bit(me, distance)
    facing = unpack_symmetric(near1, far1, core, 0)
    leading, mirror, right = before_trans((old_ref[0], old_ref[1], old_ref[2]), facing)
    into, away = unpack_second(near2, far2, core, near1)
    trans, left = after_trans(leading, mirror, away, into)
    for i, x in enumerate((left, right, trans)):
        new_ref[i] = jnp.where(upper, x, old_ref[i])


def by_third(distance, me, near2, far2, near3, far3):
    third = bit(me, distance // 2)
    return jnp.where(third, near3[...], near2[...]), jnp.where(third, far3[...], far2[...])


def last_early_kernel(distance, old_ref, near2, far2, near3, far3, half_ref, left_out, right_out, trans_out, sems):
    me = place()
    upper = bit(me, distance)

    @pl.when(upper)
    def _():
        facing = unpack_symmetric(*by_third(distance, me, near2, far2, near3, far3), bit(me, 1), 0)
        for i, x in enumerate(before_trans((old_ref[0], old_ref[1], old_ref[2]), facing)):
            half_ref[i] = x

    @pl.when(jnp.logical_not(upper))
    def _():
        outs = left_out, right_out, trans_out
        copies = [pltpu.make_async_copy(old_ref.at[i : i + 1], out, sems.at[i]) for i, out in enumerate(outs)]
        for copy in copies:
            copy.start()
        for copy in copies:
            copy.wait()


def last_kernel(distance, half_ref, near2, far2, near3, far3, _l, _r, _t, left_out, right_out, trans_out, new_ref, sems):
    me = place()

    @pl.when(bit(me, distance))
    def _():
        right_copy = pltpu.make_async_copy(half_ref.at[2:3], right_out, sems.at[0])
        trans_copy = pltpu.make_async_copy(new_ref.at[0:1], trans_out, sems.at[1])
        left_copy = pltpu.make_async_copy(new_ref.at[1:2], left_out, sems.at[2])
        right_copy.start()
        into, away = unpack_second(*by_third(distance, me, near2, far2, near3, far3), bit(me, 1))
        q = split(into)
        bounced = split(dot3(split(half_ref[1]), q))
        new_ref[0] = dot3(split(half_ref[0]), q)
        trans_copy.start()
        new_ref[1] = away + dot3(split(into.T), bounced)
        left_copy.start()
        right_copy.wait()
        trans_copy.wait()
        left_copy.wait()


def call(kernel, products, outs, *args, given=(), copied=0, scratch=()):
    vmem, hbm = pl.BlockSpec(memory_space=pltpu.VMEM), pl.BlockSpec(memory_space=pltpu.HBM)
    m = args[0].shape[-1]
    return pl.pallas_call(
        kernel,
        out_shape=[jax.ShapeDtypeStruct(s, F32) for s in outs],
        in_specs=[vmem] * len(args) + [hbm] * len(given),
        out_specs=[vmem] * (len(outs) - copied) + [hbm] * copied,
        input_output_aliases={len(args) + i: len(outs) - copied + i for i in range(len(given))},
        scratch_shapes=scratch,
        cost_estimate=pl.CostEstimate(flops=2 * products * m**3, bytes_accessed=4 * m**2 * len(args), transcendentals=0),
        compiler_params=pltpu.CompilerParams(vmem_limit_bytes=40 * 2**20),
    )(*args, *given)


def shards(refl_left, refl_right, trans):
    m = trans.shape[1]
    levels = lax.axis_size(AXES).bit_length() - 1
    stack = (3, m, m)
    first, second, padded = (m // 4 + PAD, m), (m // 2 + m // 4, m), (m // 2 + m // 4 + PAD, m)
    sections = refl_left, refl_right, trans
    got = [swap(x, 1) for x in sections]
    section = jnp.concatenate(sections, 0)
    (halfway,) = call(first_early_kernel, 27, [stack], section, *got[:2])
    prefix, send1, send2, own = call(first_late_kernel, 9, [stack, first, second, stack], section, halfway, *got)
    pending = None
    for level in range(1, levels - 1):
        distance = 1 << level
        bind = lambda kernel: functools.partial(kernel, distance)
        near1, near2 = swap(send1, distance), swap(send2, distance)
        if pending is not None:
            (prefix,) = pending(prefix)
            near1, prefix = lax.optimization_barrier((near1, prefix))
        far1 = swap(near1, 1)
        if level < levels - 2:
            (halfway,) = call(early_kernel, 27, [stack], own, near1, far1)
        else:
            halfway, send1 = call(bind(final_early_kernel), 27, [stack, first], own, near1, far1)
        near2, halfway = lax.optimization_barrier((near2, halfway))
        far2 = swap(near2, 1)
        pending = lambda old, kernel=bind(prefix_kernel), got=(near1, far1, near2, far2): call(kernel, 36, [stack], old, *got)
        if level < levels - 2:
            send1, send2, own = call(bind(late_kernel), 9, [first, second, stack], halfway, near1, near2, far2)

    first3, first2 = pair(send1, 1, 3), pair(send1, 1, 2)
    (send2,) = call(bind(final_kernel), 9, [padded], halfway, near1, near2, far2)
    distance *= 2
    near3, near2 = pair(send2, 1, 3), pair(send2, 1, 2)
    first3, first2, prefix = lax.optimization_barrier((first3, first2, prefix))
    (prefix,) = pending(prefix)
    args = prefix, first2, swap(first2, 1), first3, swap(first3, 1)
    one, sems = (1, m, m), pltpu.SemaphoreType.DMA((3,))
    kernel = functools.partial(last_early_kernel, distance)
    halfway, *given = call(kernel, 27, [stack, one, one, one], *args, copied=3, scratch=[sems])
    near3, halfway = lax.optimization_barrier((near3, halfway))
    far3 = swap(near3, 1)
    near2, far3 = lax.optimization_barrier((near2, far3))
    args = halfway, near2, swap(near2, 1), near3, far3
    scratch = [pltpu.VMEM((2, m, m), F32), sems]
    return tuple(call(functools.partial(last_kernel, distance), 9, [one] * 3, *args, given=given, copied=3, scratch=scratch))


def solution(mesh):
    spec = P(AXES, None, None)
    return jax.shard_map(
        shards,
        mesh=mesh,
        in_specs=(spec,) * 3,
        out_specs=(spec,) * 3,
        check_vma=False,
    )
```

```python
import functools

import jax
import jax.numpy as jnp
from jax import lax
from jax.experimental import pallas as pl
from jax.experimental.pallas import tpu as pltpu
from jax.sharding import PartitionSpec as P

AXES = ("gx", "gy")
NS_STEPS = 5
PAD = 8
F32 = jnp.float32
BF16 = jnp.bfloat16
NN = (((1,), (0,)), ((), ()))
NT = (((1,), (1,)), ((), ()))


def swap(block, distance):
    count = lax.axis_size(AXES)
    return lax.ppermute(block, AXES, [(i, i ^ distance) for i in range(count)])


def pair(block, first, second):
    count = lax.axis_size(AXES)
    quarter = count // 4
    shift = (second - first) * quarter
    step = {first: lambda i: i + shift, second: lambda i: i - shift}
    return lax.ppermute(block, AXES, [(i, step.get(i // quarter, lambda i: i ^ 1)(i)) for i in range(count)])


def split(x):
    high = x.astype(BF16)
    return high, (x - high.astype(F32)).astype(BF16)


def dot(a, b, dims=NN):
    return lax.dot_general(a, b, dims, preferred_element_type=F32)


def dot1(a, b, dims=NN):
    h = a.shape[0] // 2
    return jnp.concatenate([dot(a[:h], b, dims), dot(a[h:], b, dims)], 0)


def dot3(a, b, dims=NN, one=dot1):
    return one(a[0], b[0], dims) + (one(a[0], b[1], dims) + one(a[1], b[0], dims))


def half(x):
    return x.astype(BF16)


def four_steps(power):
    rest, high = power, half(power)
    squared = dot1(high, high)
    for step in range(1, NS_STEPS):
        high = half(squared)
        following = dot1(high, high) if step < NS_STEPS - 1 else None
        rest = rest + squared + dot1(half(rest), high)
        squared = following
    return half(rest)


def before_trans(own, facing):
    near, away, out = own
    f, o, s = split(facing), split(near), split(out)
    rough = dot1(f[0], o[0])
    coupling = rough + (dot1(f[0], o[1]) + dot1(f[1], o[0]))
    inner = split(dot3(f, s, NT, dot))
    rest = four_steps(rough)
    high, low = split(coupling)
    error = half((coupling - rest.astype(F32)) + (dot1(high, rest) + dot1(low, rest)))
    leading = out + (dot1(s[0], rest) + dot1(s[1], rest))
    mirror = near + (dot1(o[0], rest) + dot1(o[1], rest))
    leading = leading + dot1(half(leading), error)
    mirror = mirror + dot1(half(mirror), error)
    return leading, mirror, away + dot3(split(leading), inner, NN, dot)


def after_trans(leading, mirror, away, into):
    q = split(into)
    bounced = split(dot3(split(mirror), q))
    trans = dot3(split(leading), q)
    return trans, away + dot3(split(into.T), bounced)


def place():
    return lax.axis_index("gx") * lax.axis_size("gy") + lax.axis_index("gy")


def bit(me, distance):
    return me & distance != 0


def lower_upper(h):
    row = lax.broadcasted_iota(jnp.int32, (h, h), 0)
    col = lax.broadcasted_iota(jnp.int32, (h, h), 1)
    return row > col, row < col


def symmetric_rows(x):
    h = x.shape[0] // 2
    below, above = lower_upper(h)
    a, b, c = x[:h, :h], x[:h, h:], x[h:, h:]
    diagonal = jnp.sum(jnp.where(below | above, 0.0, c), axis=0, keepdims=True)
    return jnp.concatenate([b, jnp.where(above, c, a)], 1), diagonal


def store_half(rows, core, ref, start):
    q = rows.shape[0] // 2
    ref[start : start + q, :] = jnp.where(core, rows[q:], rows[:q])


def store_diagonals(one, two, ref, start):
    ref[start : start + PAD, :] = jnp.broadcast_to(jnp.concatenate([one, two], 1), (PAD, 2 * one.shape[1]))


def pack_symmetric(x, core, ref, start):
    rows, diagonal = symmetric_rows(x)
    store_half(rows, core, ref, start)
    store_diagonals(diagonal, diagonal, ref, start + rows.shape[0] // 2)


def joined(near_ref, far_ref, core, lo, hi):
    near, far = near_ref[lo:hi, :], far_ref[lo:hi, :]
    return jnp.concatenate([jnp.where(core, far, near), jnp.where(core, near, far)], 0)


def unpack_symmetric(near_ref, far_ref, core, start, diagonal=None):
    h = near_ref.shape[1] // 2
    q = h // 2
    below, above = lower_upper(h)
    both = joined(near_ref, far_ref, core, start, start + q)
    if diagonal is None:
        diagonal = near_ref[start + q : start + q + 1, :h]
    b, w = both[:, :h], both[:, h:]
    turned = w.T
    a = jnp.where(above, turned, w)
    c = jnp.where(above, w, jnp.where(below, turned, diagonal))
    return jnp.concatenate([jnp.concatenate([a, b], 1), jnp.concatenate([b.T, c], 1)], 0)


def unpack_second(near_ref, far_ref, core, first_ref=None):
    h = near_ref.shape[1] // 2
    diagonal = None if first_ref is None else first_ref[h // 2 : h // 2 + 1, h:]
    return joined(near_ref, far_ref, core, 0, h), unpack_symmetric(near_ref, far_ref, core, h, diagonal)


def send_total(own_side, other_side, trans, same, core, first_ref, second_ref, own_ref):
    turned = trans.T
    near = jnp.where(same, other_side, own_side)
    away = jnp.where(same, own_side, other_side)
    back = jnp.where(same, turned, trans)
    own_ref[0] = near
    own_ref[1] = away
    own_ref[2] = jnp.where(same, trans, turned)
    near_rows, near_diagonal = symmetric_rows(near)
    away_rows, away_diagonal = symmetric_rows(away)
    h = near_rows.shape[0]
    store_half(near_rows, core, first_ref, 0)
    store_diagonals(near_diagonal, away_diagonal, first_ref, h // 2)
    store_half(back, core, second_ref, 0)
    store_half(away_rows, core, second_ref, h)


def first_kernel(section_ref, got1, got2, got3, prefix_ref, *send_refs):
    me = place()
    upper = bit(me, 1)
    left, right, trans = section_ref[0], section_ref[1], section_ref[2]
    pick = lambda a, b: jnp.where(upper, a, b)
    own = pick(left, right), pick(right, left), pick(trans, trans.T)
    leading, mirror, own_side = before_trans(own, pick(got2[0], got1[0]))
    into = pick(got3[0], got3[0].T)
    through, other_side = after_trans(leading, mirror, pick(got1[0], got2[0]), into)
    send_total(own_side, other_side, through, upper == bit(me, 2), upper, *send_refs)
    prefix_ref[0] = pick(other_side, left)
    prefix_ref[1] = pick(own_side, right)
    prefix_ref[2] = pick(through, trans)


def early_kernel(own_ref, near_ref, far_ref, half_ref):
    facing = unpack_symmetric(near_ref, far_ref, bit(place(), 1), 0)
    for i, x in enumerate(before_trans((own_ref[0], own_ref[1], own_ref[2]), facing)):
        half_ref[i] = x


def only_quarter_1(distance, body, *out_refs):
    mine = place() // distance == 1
    pl.when(mine)(body)

    @pl.when(jnp.logical_not(mine))
    def _():
        for ref in out_refs:
            ref[...] = jnp.zeros_like(ref)


def final_early_kernel(distance, own_ref, near_ref, far_ref, half_ref, first_ref):
    def body():
        early_kernel(own_ref, near_ref, far_ref, half_ref)
        pack_symmetric(half_ref[2], bit(place(), 1), first_ref, 0)

    only_quarter_1(distance, body, half_ref, first_ref)


def final_kernel(distance, half_ref, near1, near_ref, far_ref, second_ref):
    def body():
        core = bit(place(), 1)
        into, away = unpack_second(near_ref, far_ref, core, near1)
        trans, other_side = after_trans(half_ref[0], half_ref[1], away, into)
        pack_second(trans, other_side, core, second_ref)

    only_quarter_1(distance, body, second_ref)


def pack_second(back, away, core, ref):
    h = back.shape[0] // 2
    store_half(back, core, ref, 0)
    pack_symmetric(away, core, ref, h)


def late_kernel(distance, half_ref, near1, near_ref, far_ref, *send_refs):
    me = place()
    core = bit(me, 1)
    into, away = unpack_second(near_ref, far_ref, core, near1)
    trans, other_side = after_trans(half_ref[0], half_ref[1], away, into)
    same = bit(me, distance) == bit(me, 2 * distance)
    send_total(half_ref[2], other_side, trans, same, core, *send_refs)


def prefix_kernel(distance, old_ref, near1, far1, near2, far2, new_ref):
    me = place()
    core, upper = bit(me, 1), bit(me, distance)
    facing = unpack_symmetric(near1, far1, core, 0)
    leading, mirror, right = before_trans((old_ref[0], old_ref[1], old_ref[2]), facing)
    into, away = unpack_second(near2, far2, core, near1)
    trans, left = after_trans(leading, mirror, away, into)
    for i, x in enumerate((left, right, trans)):
        new_ref[i] = jnp.where(upper, x, old_ref[i])


def by_third(distance, me, near2, far2, near3, far3):
    third = bit(me, distance // 2)
    return jnp.where(third, near3[...], near2[...]), jnp.where(third, far3[...], far2[...])


def last_early_kernel(distance, old_ref, near2, far2, near3, far3, half_ref, left_out, right_out, trans_out, sems):
    me = place()
    upper = bit(me, distance)

    @pl.when(upper)
    def _():
        facing = unpack_symmetric(*by_third(distance, me, near2, far2, near3, far3), bit(me, 1), 0)
        for i, x in enumerate(before_trans((old_ref[0], old_ref[1], old_ref[2]), facing)):
            half_ref[i] = x

    @pl.when(jnp.logical_not(upper))
    def _():
        outs = left_out, right_out, trans_out
        copies = [pltpu.make_async_copy(old_ref.at[i : i + 1], out, sems.at[i]) for i, out in enumerate(outs)]
        for copy in copies:
            copy.start()
        for copy in copies:
            copy.wait()


def last_kernel(distance, half_ref, near2, far2, near3, far3, _l, _r, _t, left_out, right_out, trans_out, new_ref, sems):
    me = place()

    @pl.when(bit(me, distance))
    def _():
        right_copy = pltpu.make_async_copy(half_ref.at[2:3], right_out, sems.at[0])
        trans_copy = pltpu.make_async_copy(new_ref.at[0:1], trans_out, sems.at[1])
        left_copy = pltpu.make_async_copy(new_ref.at[1:2], left_out, sems.at[2])
        right_copy.start()
        into, away = unpack_second(*by_third(distance, me, near2, far2, near3, far3), bit(me, 1))
        q = split(into)
        bounced = split(dot3(split(half_ref[1]), q))
        new_ref[0] = dot3(split(half_ref[0]), q)
        trans_copy.start()
        new_ref[1] = away + dot3(split(into.T), bounced)
        left_copy.start()
        right_copy.wait()
        trans_copy.wait()
        left_copy.wait()


def call(kernel, products, outs, *args, given=(), copied=0, scratch=()):
    vmem, hbm = pl.BlockSpec(memory_space=pltpu.VMEM), pl.BlockSpec(memory_space=pltpu.HBM)
    m = args[0].shape[-1]
    return pl.pallas_call(
        kernel,
        out_shape=[jax.ShapeDtypeStruct(s, F32) for s in outs],
        in_specs=[vmem] * len(args) + [hbm] * len(given),
        out_specs=[vmem] * (len(outs) - copied) + [hbm] * copied,
        input_output_aliases={len(args) + i: len(outs) - copied + i for i in range(len(given))},
        scratch_shapes=scratch,
        cost_estimate=pl.CostEstimate(flops=2 * products * m**3, bytes_accessed=4 * m**2 * len(args), transcendentals=0),
        compiler_params=pltpu.CompilerParams(vmem_limit_bytes=40 * 2**20),
    )(*args, *given)


def shards(refl_left, refl_right, trans):
    m = trans.shape[1]
    levels = lax.axis_size(AXES).bit_length() - 1
    stack = (3, m, m)
    first, second, padded = (m // 4 + PAD, m), (m // 2 + m // 4, m), (m // 2 + m // 4 + PAD, m)
    sections = refl_left, refl_right, trans
    got = [swap(x, 1) for x in sections]
    section = jnp.concatenate(sections, 0)
    prefix, send1, send2, own = call(first_kernel, 36, [stack, first, second, stack], section, *got)
    pending = None
    for level in range(1, levels - 1):
        distance = 1 << level
        bind = lambda kernel: functools.partial(kernel, distance)
        near1, near2 = swap(send1, distance), swap(send2, distance)
        if pending is not None:
            (prefix,) = pending(prefix)
            near1, prefix = lax.optimization_barrier((near1, prefix))
        far1 = swap(near1, 1)
        if level < levels - 2:
            (halfway,) = call(early_kernel, 27, [stack], own, near1, far1)
        else:
            halfway, send1 = call(bind(final_early_kernel), 27, [stack, first], own, near1, far1)
        near2, halfway = lax.optimization_barrier((near2, halfway))
        far2 = swap(near2, 1)
        pending = lambda old, kernel=bind(prefix_kernel), got=(near1, far1, near2, far2): call(kernel, 36, [stack], old, *got)
        if level < levels - 2:
            send1, send2, own = call(bind(late_kernel), 9, [first, second, stack], halfway, near1, near2, far2)

    first3, first2 = pair(send1, 1, 3), pair(send1, 1, 2)
    (send2,) = call(bind(final_kernel), 9, [padded], halfway, near1, near2, far2)
    distance *= 2
    near3, near2 = pair(send2, 1, 3), pair(send2, 1, 2)
    first3, first2, prefix = lax.optimization_barrier((first3, first2, prefix))
    (prefix,) = pending(prefix)
    args = prefix, first2, swap(first2, 1), first3, swap(first3, 1)
    one, sems = (1, m, m), pltpu.SemaphoreType.DMA((3,))
    kernel = functools.partial(last_early_kernel, distance)
    halfway, *given = call(kernel, 27, [stack, one, one, one], *args, copied=3, scratch=[sems])
    near3, halfway = lax.optimization_barrier((near3, halfway))
    far3 = swap(near3, 1)
    near2, far3 = lax.optimization_barrier((near2, far3))
    args = halfway, near2, swap(near2, 1), near3, far3
    scratch = [pltpu.VMEM((2, m, m), F32), sems]
    return tuple(call(functools.partial(last_kernel, distance), 9, [one] * 3, *args, given=given, copied=3, scratch=scratch))


def solution(mesh):
    spec = P(AXES, None, None)
    return jax.shard_map(
        shards,
        mesh=mesh,
        in_specs=(spec,) * 3,
        out_specs=(spec,) * 3,
        check_vma=False,
    )
```

```python
import functools

import jax
import jax.numpy as jnp
from jax import lax
from jax.experimental import pallas as pl
from jax.experimental.pallas import tpu as pltpu
from jax.sharding import PartitionSpec as P

AXES = ("gx", "gy")
NS_STEPS = 5
PAD = 8
F32 = jnp.float32
BF16 = jnp.bfloat16
NN = (((1,), (0,)), ((), ()))
NT = (((1,), (1,)), ((), ()))


def swap(block, distance):
    count = lax.axis_size(AXES)
    return lax.ppermute(block, AXES, [(i, i ^ distance) for i in range(count)])


def pair(block, first, second):
    count = lax.axis_size(AXES)
    quarter = count // 4
    shift = (second - first) * quarter
    step = {first: lambda i: i + shift, second: lambda i: i - shift}
    return lax.ppermute(block, AXES, [(i, step.get(i // quarter, lambda i: i ^ 1)(i)) for i in range(count)])


def split(x):
    high = x.astype(BF16)
    return high, (x - high.astype(F32)).astype(BF16)


def dot(a, b, dims=NN):
    return lax.dot_general(a, b, dims, preferred_element_type=F32)


def dot1(a, b, dims=NN):
    h = a.shape[0] // 2
    return jnp.concatenate([dot(a[:h], b, dims), dot(a[h:], b, dims)], 0)


def dot3(a, b, dims=NN, one=dot1):
    return one(a[0], b[0], dims) + (one(a[0], b[1], dims) + one(a[1], b[0], dims))


def half(x):
    return x.astype(BF16)


def four_steps(power):
    rest, high = power, half(power)
    squared = dot1(high, high)
    for step in range(1, NS_STEPS):
        high = half(squared)
        following = dot1(high, high) if step < NS_STEPS - 1 else None
        rest = rest + squared + dot1(half(rest), high)
        squared = following
    return half(rest)


def before_trans(own, facing):
    near, away, out = own
    f, o, s = split(facing), split(near), split(out)
    rough = dot1(f[0], o[0])
    coupling = rough + (dot1(f[0], o[1]) + dot1(f[1], o[0]))
    inner = split(dot3(f, s, NT, dot))
    rest = four_steps(rough)
    high, low = split(coupling)
    error = half((coupling - rest.astype(F32)) + (dot1(high, rest) + dot1(low, rest)))
    leading = out + (dot1(s[0], rest) + dot1(s[1], rest))
    mirror = near + (dot1(o[0], rest) + dot1(o[1], rest))
    leading = leading + dot1(half(leading), error)
    mirror = mirror + dot1(half(mirror), error)
    return leading, mirror, away + dot3(split(leading), inner, NN, dot)


def after_trans(leading, mirror, away, into):
    q = split(into)
    bounced = split(dot3(split(mirror), q))
    trans = dot3(split(leading), q)
    return trans, away + dot3(split(into.T), bounced)


def place():
    return lax.axis_index("gx") * lax.axis_size("gy") + lax.axis_index("gy")


def bit(me, distance):
    return me & distance != 0


def lower_upper(h):
    row = lax.broadcasted_iota(jnp.int32, (h, h), 0)
    col = lax.broadcasted_iota(jnp.int32, (h, h), 1)
    return row > col, row < col


def symmetric_rows(x):
    h = x.shape[0] // 2
    below, above = lower_upper(h)
    a, b, c = x[:h, :h], x[:h, h:], x[h:, h:]
    diagonal = jnp.sum(jnp.where(below | above, 0.0, c), axis=0, keepdims=True)
    return jnp.concatenate([b, jnp.where(above, c, a)], 1), diagonal


def store_half(rows, core, ref, start):
    q = rows.shape[0] // 2
    ref[start : start + q, :] = jnp.where(core, rows[q:], rows[:q])


def store_diagonals(one, two, ref, start):
    ref[start : start + PAD, :] = jnp.broadcast_to(jnp.concatenate([one, two], 1), (PAD, 2 * one.shape[1]))


def pack_symmetric(x, core, ref, start):
    rows, diagonal = symmetric_rows(x)
    store_half(rows, core, ref, start)
    store_diagonals(diagonal, diagonal, ref, start + rows.shape[0] // 2)


def joined(near_ref, far_ref, core, lo, hi):
    near, far = near_ref[lo:hi, :], far_ref[lo:hi, :]
    return jnp.concatenate([jnp.where(core, far, near), jnp.where(core, near, far)], 0)


def unpack_symmetric(near_ref, far_ref, core, start, diagonal=None):
    h = near_ref.shape[1] // 2
    q = h // 2
    below, above = lower_upper(h)
    both = joined(near_ref, far_ref, core, start, start + q)
    if diagonal is None:
        diagonal = near_ref[start + q : start + q + 1, :h]
    b, w = both[:, :h], both[:, h:]
    turned = w.T
    a = jnp.where(above, turned, w)
    c = jnp.where(above, w, jnp.where(below, turned, diagonal))
    return jnp.concatenate([jnp.concatenate([a, b], 1), jnp.concatenate([b.T, c], 1)], 0)


def unpack_second(near_ref, far_ref, core, first_ref=None):
    h = near_ref.shape[1] // 2
    diagonal = None if first_ref is None else first_ref[h // 2 : h // 2 + 1, h:]
    return joined(near_ref, far_ref, core, 0, h), unpack_symmetric(near_ref, far_ref, core, h, diagonal)


def send_total(own_side, other_side, trans, same, core, first_ref, second_ref, own_ref):
    turned = trans.T
    near = jnp.where(same, other_side, own_side)
    away = jnp.where(same, own_side, other_side)
    back = jnp.where(same, turned, trans)
    own_ref[0] = near
    own_ref[1] = away
    own_ref[2] = jnp.where(same, trans, turned)
    near_rows, near_diagonal = symmetric_rows(near)
    away_rows, away_diagonal = symmetric_rows(away)
    h = near_rows.shape[0]
    store_half(near_rows, core, first_ref, 0)
    store_diagonals(near_diagonal, away_diagonal, first_ref, h // 2)
    store_half(back, core, second_ref, 0)
    store_half(away_rows, core, second_ref, h)


def first_kernel(section_ref, got1, got2, got3, prefix_ref, *send_refs):
    me = place()
    upper = bit(me, 1)
    left, right, trans = section_ref[0], section_ref[1], section_ref[2]
    pick = lambda a, b: jnp.where(upper, a, b)
    own = pick(left, right), pick(right, left), pick(trans, trans.T)
    leading, mirror, own_side = before_trans(own, pick(got2[0], got1[0]))
    into = pick(got3[0], got3[0].T)
    through, other_side = after_trans(leading, mirror, pick(got1[0], got2[0]), into)
    send_total(own_side, other_side, through, upper == bit(me, 2), upper, *send_refs)
    prefix_ref[0] = pick(other_side, left)
    prefix_ref[1] = pick(own_side, right)
    prefix_ref[2] = pick(through, trans)


def early_kernel(own_ref, near_ref, far_ref, half_ref):
    facing = unpack_symmetric(near_ref, far_ref, bit(place(), 1), 0)
    for i, x in enumerate(before_trans((own_ref[0], own_ref[1], own_ref[2]), facing)):
        half_ref[i] = x


def only_quarter_1(distance, body, *out_refs):
    mine = place() // distance == 1
    pl.when(mine)(body)

    @pl.when(jnp.logical_not(mine))
    def _():
        for ref in out_refs:
            ref[...] = jnp.zeros_like(ref)


def final_early_kernel(distance, own_ref, near_ref, far_ref, half_ref, first_ref):
    def body():
        early_kernel(own_ref, near_ref, far_ref, half_ref)
        pack_symmetric(half_ref[2], bit(place(), 1), first_ref, 0)

    only_quarter_1(distance, body, half_ref, first_ref)


def final_kernel(distance, half_ref, near1, near_ref, far_ref, second_ref):
    def body():
        core = bit(place(), 1)
        into, away = unpack_second(near_ref, far_ref, core, near1)
        trans, other_side = after_trans(half_ref[0], half_ref[1], away, into)
        pack_second(trans, other_side, core, second_ref)

    only_quarter_1(distance, body, second_ref)


def pack_second(back, away, core, ref):
    h = back.shape[0] // 2
    store_half(back, core, ref, 0)
    pack_symmetric(away, core, ref, h)


def late_kernel(distance, half_ref, near1, near_ref, far_ref, *send_refs):
    me = place()
    core = bit(me, 1)
    into, away = unpack_second(near_ref, far_ref, core, near1)
    trans, other_side = after_trans(half_ref[0], half_ref[1], away, into)
    same = bit(me, distance) == bit(me, 2 * distance)
    send_total(half_ref[2], other_side, trans, same, core, *send_refs)


def prefix_kernel(distance, old_ref, near1, far1, near2, far2, new_ref):
    me = place()
    core, upper = bit(me, 1), bit(me, distance)
    facing = unpack_symmetric(near1, far1, core, 0)
    leading, mirror, right = before_trans((old_ref[0], old_ref[1], old_ref[2]), facing)
    into, away = unpack_second(near2, far2, core, near1)
    trans, left = after_trans(leading, mirror, away, into)
    for i, x in enumerate((left, right, trans)):
        new_ref[i] = jnp.where(upper, x, old_ref[i])


def by_third(distance, me, near2, far2, near3, far3):
    third = bit(me, distance // 2)
    return jnp.where(third, near3[...], near2[...]), jnp.where(third, far3[...], far2[...])


def last_early_kernel(distance, old_ref, near2, far2, near3, far3, half_ref, left_out, right_out, trans_out, sems):
    me = place()
    upper = bit(me, distance)

    @pl.when(upper)
    def _():
        facing = unpack_symmetric(*by_third(distance, me, near2, far2, near3, far3), bit(me, 1), 0)
        for i, x in enumerate(before_trans((old_ref[0], old_ref[1], old_ref[2]), facing)):
            half_ref[i] = x

    @pl.when(jnp.logical_not(upper))
    def _():
        outs = left_out, right_out, trans_out
        copies = [pltpu.make_async_copy(old_ref.at[i : i + 1], out, sems.at[i]) for i, out in enumerate(outs)]
        for copy in copies:
            copy.start()
        for copy in copies:
            copy.wait()


def last_kernel(distance, half_ref, near2, far2, near3, far3, _l, _r, _t, left_out, right_out, trans_out, new_ref, sems):
    me = place()

    @pl.when(bit(me, distance))
    def _():
        right_copy = pltpu.make_async_copy(half_ref.at[2:3], right_out, sems.at[0])
        trans_copy = pltpu.make_async_copy(new_ref.at[0:1], trans_out, sems.at[1])
        left_copy = pltpu.make_async_copy(new_ref.at[1:2], left_out, sems.at[2])
        right_copy.start()
        into, away = unpack_second(*by_third(distance, me, near2, far2, near3, far3), bit(me, 1))
        q = split(into)
        bounced = split(dot3(split(half_ref[1]), q))
        new_ref[0] = dot3(split(half_ref[0]), q)
        trans_copy.start()
        new_ref[1] = away + dot3(split(into.T), bounced)
        left_copy.start()
        right_copy.wait()
        trans_copy.wait()
        left_copy.wait()


def call(kernel, products, outs, *args, given=(), copied=0, scratch=()):
    vmem, hbm = pl.BlockSpec(memory_space=pltpu.VMEM), pl.BlockSpec(memory_space=pltpu.HBM)
    m = args[0].shape[-1]
    return pl.pallas_call(
        kernel,
        out_shape=[jax.ShapeDtypeStruct(s, F32) for s in outs],
        in_specs=[vmem] * len(args) + [hbm] * len(given),
        out_specs=[vmem] * (len(outs) - copied) + [hbm] * copied,
        input_output_aliases={len(args) + i: len(outs) - copied + i for i in range(len(given))},
        scratch_shapes=scratch,
        cost_estimate=pl.CostEstimate(flops=2 * products * m**3, bytes_accessed=4 * m**2 * len(args), transcendentals=0),
        compiler_params=pltpu.CompilerParams(vmem_limit_bytes=40 * 2**20),
    )(*args, *given)


def shards(refl_left, refl_right, trans):
    m = trans.shape[1]
    levels = lax.axis_size(AXES).bit_length() - 1
    stack = (3, m, m)
    first, second, padded = (m // 4 + PAD, m), (m // 2 + m // 4, m), (m // 2 + m // 4 + PAD, m)
    sections = refl_left, refl_right, trans
    got = [swap(x, 1) for x in sections]
    section = jnp.concatenate(sections, 0)
    prefix, send1, send2, own = call(first_kernel, 36, [stack, first, second, stack], section, *got)
    pending = None
    for level in range(1, levels - 1):
        distance = 1 << level
        bind = lambda kernel: functools.partial(kernel, distance)
        near1, near2 = swap(send1, distance), swap(send2, distance)
        if pending is not None:
            (prefix,) = pending(prefix)
            near1, prefix = lax.optimization_barrier((near1, prefix))
        far1 = swap(near1, 1)
        if level < levels - 2:
            (halfway,) = call(early_kernel, 27, [stack], own, near1, far1)
        else:
            halfway, send1 = call(bind(final_early_kernel), 27, [stack, first], own, near1, far1)
        near2, halfway = lax.optimization_barrier((near2, halfway))
        far2 = swap(near2, 1)
        pending = lambda old, kernel=bind(prefix_kernel), got=(near1, far1, near2, far2): call(kernel, 36, [stack], old, *got)
        if level < levels - 2:
            send1, send2, own = call(bind(late_kernel), 9, [first, second, stack], halfway, near1, near2, far2)

    first3, first2 = pair(send1, 1, 3), pair(send1, 1, 2)
    (send2,) = call(bind(final_kernel), 9, [padded], halfway, near1, near2, far2)
    distance *= 2
    near3, near2 = pair(send2, 1, 3), pair(send2, 1, 2)
    first3, first2, prefix = lax.optimization_barrier((first3, first2, prefix))
    (prefix,) = pending(prefix)
    args = prefix, first2, swap(first2, 1), first3, swap(first3, 1)
    one, sems = (1, m, m), pltpu.SemaphoreType.DMA((3,))
    kernel = functools.partial(last_early_kernel, distance)
    halfway, *given = call(kernel, 27, [stack, one, one, one], *args, copied=3, scratch=[sems])
    near2, near3, halfway = lax.optimization_barrier((near2, near3, halfway))
    args = halfway, near2, swap(near2, 1), near3, swap(near3, 1)
    scratch = [pltpu.VMEM((2, m, m), F32), sems]
    return tuple(call(functools.partial(last_kernel, distance), 9, [one] * 3, *args, given=given, copied=3, scratch=scratch))


def solution(mesh):
    spec = P(AXES, None, None)
    return jax.shard_map(
        shards,
        mesh=mesh,
        in_specs=(spec,) * 3,
        out_specs=(spec,) * 3,
        check_vma=False,
    )
```

```python
import functools

import jax
import jax.numpy as jnp
from jax import lax
from jax.experimental import pallas as pl
from jax.experimental.pallas import tpu as pltpu
from jax.sharding import PartitionSpec as P

AXES = ("gx", "gy")
NS_STEPS = 5
PAD = 8
F32 = jnp.float32
BF16 = jnp.bfloat16
NN = (((1,), (0,)), ((), ()))
NT = (((1,), (1,)), ((), ()))


def swap(block, distance):
    count = lax.axis_size(AXES)
    return lax.ppermute(block, AXES, [(i, i ^ distance) for i in range(count)])


def pair(block, first, second):
    count = lax.axis_size(AXES)
    quarter = count // 4
    shift = (second - first) * quarter
    step = {first: lambda i: i + shift, second: lambda i: i - shift}
    return lax.ppermute(block, AXES, [(i, step.get(i // quarter, lambda i: i ^ 1)(i)) for i in range(count)])


def split(x):
    high = x.astype(BF16)
    return high, (x - high.astype(F32)).astype(BF16)


def dot(a, b, dims=NN):
    return lax.dot_general(a, b, dims, preferred_element_type=F32)


def dot1(a, b, dims=NN):
    h = a.shape[0] // 2
    return jnp.concatenate([dot(a[:h], b, dims), dot(a[h:], b, dims)], 0)


def dot3(a, b, dims=NN, one=dot1):
    return one(a[0], b[0], dims) + (one(a[0], b[1], dims) + one(a[1], b[0], dims))


def half(x):
    return x.astype(BF16)


def four_steps(power):
    rest, high = power, half(power)
    squared = dot1(high, high)
    for step in range(1, NS_STEPS):
        high = half(squared)
        following = dot1(high, high) if step < NS_STEPS - 1 else None
        rest = rest + squared + dot1(half(rest), high)
        squared = following
    return half(rest)


def before_trans(own, facing):
    near, away, out = own
    f, o, s = split(facing), split(near), split(out)
    rough = dot1(f[0], o[0])
    coupling = rough + (dot1(f[0], o[1]) + dot1(f[1], o[0]))
    inner = split(dot3(f, s, NT, dot))
    rest = four_steps(rough)
    high, low = split(coupling)
    error = half((coupling - rest.astype(F32)) + (dot1(high, rest) + dot1(low, rest)))
    leading = out + (dot1(s[0], rest) + dot1(s[1], rest))
    mirror = near + (dot1(o[0], rest) + dot1(o[1], rest))
    leading = leading + dot1(half(leading), error)
    mirror = mirror + dot1(half(mirror), error)
    return leading, mirror, away + dot3(split(leading), inner, NN, dot)


def after_trans(leading, mirror, away, into):
    q = split(into)
    bounced = split(dot3(split(mirror), q))
    trans = dot3(split(leading), q)
    return trans, away + dot3(split(into.T), bounced)


def place():
    return lax.axis_index("gx") * lax.axis_size("gy") + lax.axis_index("gy")


def bit(me, distance):
    return me & distance != 0


def lower_upper(h):
    row = lax.broadcasted_iota(jnp.int32, (h, h), 0)
    col = lax.broadcasted_iota(jnp.int32, (h, h), 1)
    return row > col, row < col


def symmetric_rows(x):
    h = x.shape[0] // 2
    below, above = lower_upper(h)
    a, b, c = x[:h, :h], x[:h, h:], x[h:, h:]
    diagonal = jnp.sum(jnp.where(below | above, 0.0, c), axis=0, keepdims=True)
    return jnp.concatenate([b, jnp.where(above, c, a)], 1), diagonal


def store_half(rows, core, ref, start):
    q = rows.shape[0] // 2
    ref[start : start + q, :] = jnp.where(core, rows[q:], rows[:q])


def store_diagonals(one, two, ref, start):
    ref[start : start + PAD, :] = jnp.broadcast_to(jnp.concatenate([one, two], 1), (PAD, 2 * one.shape[1]))


def pack_symmetric(x, core, ref, start):
    rows, diagonal = symmetric_rows(x)
    store_half(rows, core, ref, start)
    store_diagonals(diagonal, diagonal, ref, start + rows.shape[0] // 2)


def joined(near_ref, far_ref, core, lo, hi):
    near, far = near_ref[lo:hi, :], far_ref[lo:hi, :]
    return jnp.concatenate([jnp.where(core, far, near), jnp.where(core, near, far)], 0)


def unpack_symmetric(near_ref, far_ref, core, start, diagonal=None):
    h = near_ref.shape[1] // 2
    q = h // 2
    below, above = lower_upper(h)
    both = joined(near_ref, far_ref, core, start, start + q)
    if diagonal is None:
        diagonal = near_ref[start + q : start + q + 1, :h]
    b, w = both[:, :h], both[:, h:]
    turned = w.T
    a = jnp.where(above, turned, w)
    c = jnp.where(above, w, jnp.where(below, turned, diagonal))
    return jnp.concatenate([jnp.concatenate([a, b], 1), jnp.concatenate([b.T, c], 1)], 0)


def unpack_second(near_ref, far_ref, core, first_ref=None):
    h = near_ref.shape[1] // 2
    diagonal = None if first_ref is None else first_ref[h // 2 : h // 2 + 1, h:]
    return joined(near_ref, far_ref, core, 0, h), unpack_symmetric(near_ref, far_ref, core, h, diagonal)


def send_total(own_side, other_side, trans, same, core, first_ref, second_ref, own_ref):
    turned = trans.T
    near = jnp.where(same, other_side, own_side)
    away = jnp.where(same, own_side, other_side)
    back = jnp.where(same, turned, trans)
    own_ref[0] = near
    own_ref[1] = away
    own_ref[2] = jnp.where(same, trans, turned)
    near_rows, near_diagonal = symmetric_rows(near)
    away_rows, away_diagonal = symmetric_rows(away)
    h = near_rows.shape[0]
    store_half(near_rows, core, first_ref, 0)
    store_diagonals(near_diagonal, away_diagonal, first_ref, h // 2)
    store_half(back, core, second_ref, 0)
    store_half(away_rows, core, second_ref, h)


def first_kernel(section_ref, got1, got2, got3, prefix_ref, *send_refs):
    me = place()
    upper = bit(me, 1)
    left, right, trans = section_ref[0], section_ref[1], section_ref[2]
    pick = lambda a, b: jnp.where(upper, a, b)
    own = pick(left, right), pick(right, left), pick(trans, trans.T)
    leading, mirror, own_side = before_trans(own, pick(got2[0], got1[0]))
    into = pick(got3[0], got3[0].T)
    through, other_side = after_trans(leading, mirror, pick(got1[0], got2[0]), into)
    send_total(own_side, other_side, through, upper == bit(me, 2), upper, *send_refs)
    prefix_ref[0] = pick(other_side, left)
    prefix_ref[1] = pick(own_side, right)
    prefix_ref[2] = pick(through, trans)


def early_kernel(own_ref, near_ref, far_ref, half_ref):
    facing = unpack_symmetric(near_ref, far_ref, bit(place(), 1), 0)
    for i, x in enumerate(before_trans((own_ref[0], own_ref[1], own_ref[2]), facing)):
        half_ref[i] = x


def only_quarter_1(distance, body, *out_refs):
    mine = place() // distance == 1
    pl.when(mine)(body)

    @pl.when(jnp.logical_not(mine))
    def _():
        for ref in out_refs:
            ref[...] = jnp.zeros_like(ref)


def final_early_kernel(distance, own_ref, near_ref, far_ref, half_ref, first_ref):
    def body():
        early_kernel(own_ref, near_ref, far_ref, half_ref)
        pack_symmetric(half_ref[2], bit(place(), 1), first_ref, 0)

    only_quarter_1(distance, body, half_ref, first_ref)


def final_kernel(distance, half_ref, near1, near_ref, far_ref, second_ref):
    def body():
        core = bit(place(), 1)
        into, away = unpack_second(near_ref, far_ref, core, near1)
        trans, other_side = after_trans(half_ref[0], half_ref[1], away, into)
        pack_second(trans, other_side, core, second_ref)

    only_quarter_1(distance, body, second_ref)


def pack_second(back, away, core, ref):
    h = back.shape[0] // 2
    store_half(back, core, ref, 0)
    pack_symmetric(away, core, ref, h)


def late_kernel(distance, half_ref, near1, near_ref, far_ref, *send_refs):
    me = place()
    core = bit(me, 1)
    into, away = unpack_second(near_ref, far_ref, core, near1)
    trans, other_side = after_trans(half_ref[0], half_ref[1], away, into)
    same = bit(me, distance) == bit(me, 2 * distance)
    send_total(half_ref[2], other_side, trans, same, core, *send_refs)


def prefix_kernel(distance, old_ref, near1, far1, near2, far2, new_ref):
    me = place()
    core, upper = bit(me, 1), bit(me, distance)

    @pl.when(upper)
    def _():
        facing = unpack_symmetric(near1, far1, core, 0)
        leading, mirror, right = before_trans((old_ref[0], old_ref[1], old_ref[2]), facing)
        into, away = unpack_second(near2, far2, core, near1)
        trans, left = after_trans(leading, mirror, away, into)
        for i, x in enumerate((left, right, trans)):
            new_ref[i] = x

    @pl.when(jnp.logical_not(upper))
    def _():
        new_ref[...] = old_ref[...]


def by_third(distance, me, near2, far2, near3, far3):
    third = bit(me, distance // 2)
    return jnp.where(third, near3[...], near2[...]), jnp.where(third, far3[...], far2[...])


def last_early_kernel(distance, old_ref, near2, far2, near3, far3, half_ref, left_out, right_out, trans_out, sems):
    me = place()
    upper = bit(me, distance)

    @pl.when(upper)
    def _():
        facing = unpack_symmetric(*by_third(distance, me, near2, far2, near3, far3), bit(me, 1), 0)
        for i, x in enumerate(before_trans((old_ref[0], old_ref[1], old_ref[2]), facing)):
            half_ref[i] = x

    @pl.when(jnp.logical_not(upper))
    def _():
        outs = left_out, right_out, trans_out
        copies = [pltpu.make_async_copy(old_ref.at[i : i + 1], out, sems.at[i]) for i, out in enumerate(outs)]
        for copy in copies:
            copy.start()
        for copy in copies:
            copy.wait()


def last_kernel(distance, half_ref, near2, far2, near3, far3, _l, _r, _t, left_out, right_out, trans_out, new_ref, sems):
    me = place()

    @pl.when(bit(me, distance))
    def _():
        right_copy = pltpu.make_async_copy(half_ref.at[2:3], right_out, sems.at[0])
        trans_copy = pltpu.make_async_copy(new_ref.at[0:1], trans_out, sems.at[1])
        left_copy = pltpu.make_async_copy(new_ref.at[1:2], left_out, sems.at[2])
        right_copy.start()
        into, away = unpack_second(*by_third(distance, me, near2, far2, near3, far3), bit(me, 1))
        q = split(into)
        bounced = split(dot3(split(half_ref[1]), q))
        new_ref[0] = dot3(split(half_ref[0]), q)
        trans_copy.start()
        new_ref[1] = away + dot3(split(into.T), bounced)
        left_copy.start()
        right_copy.wait()
        trans_copy.wait()
        left_copy.wait()


def call(kernel, products, outs, *args, given=(), copied=0, scratch=()):
    vmem, hbm = pl.BlockSpec(memory_space=pltpu.VMEM), pl.BlockSpec(memory_space=pltpu.HBM)
    m = args[0].shape[-1]
    return pl.pallas_call(
        kernel,
        out_shape=[jax.ShapeDtypeStruct(s, F32) for s in outs],
        in_specs=[vmem] * len(args) + [hbm] * len(given),
        out_specs=[vmem] * (len(outs) - copied) + [hbm] * copied,
        input_output_aliases={len(args) + i: len(outs) - copied + i for i in range(len(given))},
        scratch_shapes=scratch,
        cost_estimate=pl.CostEstimate(flops=2 * products * m**3, bytes_accessed=4 * m**2 * len(args), transcendentals=0),
        compiler_params=pltpu.CompilerParams(vmem_limit_bytes=40 * 2**20),
    )(*args, *given)


def shards(refl_left, refl_right, trans):
    m = trans.shape[1]
    levels = lax.axis_size(AXES).bit_length() - 1
    stack = (3, m, m)
    first, second, padded = (m // 4 + PAD, m), (m // 2 + m // 4, m), (m // 2 + m // 4 + PAD, m)
    sections = refl_left, refl_right, trans
    got = [swap(x, 1) for x in sections]
    section = jnp.concatenate(sections, 0)
    prefix, send1, send2, own = call(first_kernel, 36, [stack, first, second, stack], section, *got)
    pending = None
    for level in range(1, levels - 1):
        distance = 1 << level
        bind = lambda kernel: functools.partial(kernel, distance)
        near1, near2 = swap(send1, distance), swap(send2, distance)
        if pending is not None:
            (prefix,) = pending(prefix)
            near1, prefix = lax.optimization_barrier((near1, prefix))
        far1 = swap(near1, 1)
        if level < levels - 2:
            (halfway,) = call(early_kernel, 27, [stack], own, near1, far1)
        else:
            halfway, send1 = call(bind(final_early_kernel), 27, [stack, first], own, near1, far1)
        near2, halfway = lax.optimization_barrier((near2, halfway))
        far2 = swap(near2, 1)
        pending = lambda old, kernel=bind(prefix_kernel), got=(near1, far1, near2, far2): call(kernel, 36, [stack], old, *got)
        if level < levels - 2:
            send1, send2, own = call(bind(late_kernel), 9, [first, second, stack], halfway, near1, near2, far2)

    first3, first2 = pair(send1, 1, 3), pair(send1, 1, 2)
    (send2,) = call(bind(final_kernel), 9, [padded], halfway, near1, near2, far2)
    distance *= 2
    near3, near2 = pair(send2, 1, 3), pair(send2, 1, 2)
    first3, first2, prefix = lax.optimization_barrier((first3, first2, prefix))
    (prefix,) = pending(prefix)
    args = prefix, first2, swap(first2, 1), first3, swap(first3, 1)
    one, sems = (1, m, m), pltpu.SemaphoreType.DMA((3,))
    kernel = functools.partial(last_early_kernel, distance)
    halfway, *given = call(kernel, 27, [stack, one, one, one], *args, copied=3, scratch=[sems])
    near3, halfway = lax.optimization_barrier((near3, halfway))
    far3 = swap(near3, 1)
    near2, far3 = lax.optimization_barrier((near2, far3))
    args = halfway, near2, swap(near2, 1), near3, far3
    scratch = [pltpu.VMEM((2, m, m), F32), sems]
    return tuple(call(functools.partial(last_kernel, distance), 9, [one] * 3, *args, given=given, copied=3, scratch=scratch))


def solution(mesh):
    spec = P(AXES, None, None)
    return jax.shard_map(
        shards,
        mesh=mesh,
        in_specs=(spec,) * 3,
        out_specs=(spec,) * 3,
        check_vma=False,
    )
```

```python
import functools

import jax
import jax.numpy as jnp
from jax import lax
from jax.experimental import pallas as pl
from jax.experimental.pallas import tpu as pltpu
from jax.sharding import PartitionSpec as P

AXES = ("gx", "gy")
NS_STEPS = 5
PAD = 8
F32 = jnp.float32
BF16 = jnp.bfloat16
NN = (((1,), (0,)), ((), ()))
NT = (((1,), (1,)), ((), ()))


def swap(block, distance):
    count = lax.axis_size(AXES)
    return lax.ppermute(block, AXES, [(i, i ^ distance) for i in range(count)])


def pair(block, first, second):
    count = lax.axis_size(AXES)
    quarter = count // 4
    shift = (second - first) * quarter
    step = {first: lambda i: i + shift, second: lambda i: i - shift}
    return lax.ppermute(block, AXES, [(i, step.get(i // quarter, lambda i: i ^ 1)(i)) for i in range(count)])


def split(x):
    high = x.astype(BF16)
    return high, (x - high.astype(F32)).astype(BF16)


def dot(a, b, dims=NN):
    return lax.dot_general(a, b, dims, preferred_element_type=F32)


def dot1(a, b, dims=NN):
    h = a.shape[0] // 2
    return jnp.concatenate([dot(a[:h], b, dims), dot(a[h:], b, dims)], 0)


def dot3(a, b, dims=NN, one=dot1):
    return one(a[0], b[0], dims) + (one(a[0], b[1], dims) + one(a[1], b[0], dims))


def half(x):
    return x.astype(BF16)


def four_steps(power):
    rest, high = power, half(power)
    squared = dot1(high, high)
    for step in range(1, NS_STEPS):
        high = half(squared)
        following = dot1(high, high) if step < NS_STEPS - 1 else None
        rest = rest + squared + dot1(half(rest), high)
        squared = following
    return half(rest)


def before_trans(own, facing):
    near, away, out = own
    f, o, s = split(facing), split(near), split(out)
    rough = dot1(f[0], o[0])
    coupling = rough + (dot1(f[0], o[1]) + dot1(f[1], o[0]))
    inner = split(dot3(f, s, NT, dot))
    rest = four_steps(rough)
    high, low = split(coupling)
    error = half((coupling - rest.astype(F32)) + (dot1(high, rest) + dot1(low, rest)))
    leading = out + (dot1(s[0], rest) + dot1(s[1], rest))
    mirror = near + (dot1(o[0], rest) + dot1(o[1], rest))
    leading = leading + dot1(half(leading), error)
    mirror = mirror + dot1(half(mirror), error)
    return leading, mirror, away + dot3(split(leading), inner, NN, dot)


def after_trans(leading, mirror, away, into):
    q = split(into)
    bounced = split(dot3(split(mirror), q))
    trans = dot3(split(leading), q)
    return trans, away + dot3(split(into.T), bounced)


def place():
    return lax.axis_index("gx") * lax.axis_size("gy") + lax.axis_index("gy")


def bit(me, distance):
    return me & distance != 0


def lower_upper(h):
    row = lax.broadcasted_iota(jnp.int32, (h, h), 0)
    col = lax.broadcasted_iota(jnp.int32, (h, h), 1)
    return row > col, row < col


def symmetric_rows(x):
    h = x.shape[0] // 2
    below, above = lower_upper(h)
    a, b, c = x[:h, :h], x[:h, h:], x[h:, h:]
    diagonal = jnp.sum(jnp.where(below | above, 0.0, c), axis=0, keepdims=True)
    return jnp.concatenate([b, jnp.where(above, c, a)], 1), diagonal


def store_half(rows, core, ref, start):
    q = rows.shape[0] // 2
    ref[start : start + q, :] = jnp.where(core, rows[q:], rows[:q])


def store_diagonals(one, two, ref, start):
    ref[start : start + PAD, :] = jnp.broadcast_to(jnp.concatenate([one, two], 1), (PAD, 2 * one.shape[1]))


def pack_symmetric(x, core, ref, start):
    rows, diagonal = symmetric_rows(x)
    store_half(rows, core, ref, start)
    store_diagonals(diagonal, diagonal, ref, start + rows.shape[0] // 2)


def joined(near_ref, far_ref, core, lo, hi):
    near, far = near_ref[lo:hi, :], far_ref[lo:hi, :]
    return jnp.concatenate([jnp.where(core, far, near), jnp.where(core, near, far)], 0)


def unpack_symmetric(near_ref, far_ref, core, start, diagonal=None):
    h = near_ref.shape[1] // 2
    q = h // 2
    below, above = lower_upper(h)
    both = joined(near_ref, far_ref, core, start, start + q)
    if diagonal is None:
        diagonal = near_ref[start + q : start + q + 1, :h]
    b, w = both[:, :h], both[:, h:]
    turned = w.T
    a = jnp.where(above, turned, w)
    c = jnp.where(above, w, jnp.where(below, turned, diagonal))
    return jnp.concatenate([jnp.concatenate([a, b], 1), jnp.concatenate([b.T, c], 1)], 0)


def unpack_second(near_ref, far_ref, core, first_ref=None):
    h = near_ref.shape[1] // 2
    diagonal = None if first_ref is None else first_ref[h // 2 : h // 2 + 1, h:]
    return joined(near_ref, far_ref, core, 0, h), unpack_symmetric(near_ref, far_ref, core, h, diagonal)


def send_total(own_side, other_side, trans, same, core, first_ref, second_ref, own_ref):
    turned = trans.T
    near = jnp.where(same, other_side, own_side)
    away = jnp.where(same, own_side, other_side)
    back = jnp.where(same, turned, trans)
    own_ref[0] = near
    own_ref[1] = away
    own_ref[2] = jnp.where(same, trans, turned)
    near_rows, near_diagonal = symmetric_rows(near)
    away_rows, away_diagonal = symmetric_rows(away)
    h = near_rows.shape[0]
    store_half(near_rows, core, first_ref, 0)
    store_diagonals(near_diagonal, away_diagonal, first_ref, h // 2)
    store_half(back, core, second_ref, 0)
    store_half(away_rows, core, second_ref, h)


def first_kernel(section_ref, got1, got2, got3, prefix_ref, *send_refs):
    me = place()
    upper = bit(me, 1)
    left, right, trans = section_ref[0], section_ref[1], section_ref[2]
    pick = lambda a, b: jnp.where(upper, a, b)
    own = pick(left, right), pick(right, left), pick(trans, trans.T)
    leading, mirror, own_side = before_trans(own, pick(got2[0], got1[0]))
    into = pick(got3[0], got3[0].T)
    through, other_side = after_trans(leading, mirror, pick(got1[0], got2[0]), into)
    send_total(own_side, other_side, through, upper == bit(me, 2), upper, *send_refs)
    prefix_ref[0] = pick(other_side, left)
    prefix_ref[1] = pick(own_side, right)
    prefix_ref[2] = pick(through, trans)


def early_kernel(own_ref, near_ref, far_ref, half_ref):
    facing = unpack_symmetric(near_ref, far_ref, bit(place(), 1), 0)
    for i, x in enumerate(before_trans((own_ref[0], own_ref[1], own_ref[2]), facing)):
        half_ref[i] = x


def only_quarter_1(distance, body, *out_refs):
    mine = place() // distance == 1
    pl.when(mine)(body)

    @pl.when(jnp.logical_not(mine))
    def _():
        for ref in out_refs:
            ref[...] = jnp.zeros_like(ref)


def final_early_kernel(distance, own_ref, near_ref, far_ref, half_ref, first_ref):
    def body():
        core = bit(place(), 1)
        facing = unpack_symmetric(near_ref, far_ref, core, 0)
        half = before_trans((own_ref[0], own_ref[1], own_ref[2]), facing)
        pack_symmetric(half[2], core, first_ref, 0)
        for i, x in enumerate(half):
            half_ref[i] = x

    only_quarter_1(distance, body, half_ref, first_ref)


def final_kernel(distance, half_ref, near1, near_ref, far_ref, second_ref):
    def body():
        core = bit(place(), 1)
        into, away = unpack_second(near_ref, far_ref, core, near1)
        trans, other_side = after_trans(half_ref[0], half_ref[1], away, into)
        pack_second(trans, other_side, core, second_ref)

    only_quarter_1(distance, body, second_ref)


def pack_second(back, away, core, ref):
    h = back.shape[0] // 2
    store_half(back, core, ref, 0)
    pack_symmetric(away, core, ref, h)


def late_kernel(distance, half_ref, near1, near_ref, far_ref, *send_refs):
    me = place()
    core = bit(me, 1)
    into, away = unpack_second(near_ref, far_ref, core, near1)
    trans, other_side = after_trans(half_ref[0], half_ref[1], away, into)
    same = bit(me, distance) == bit(me, 2 * distance)
    send_total(half_ref[2], other_side, trans, same, core, *send_refs)


def prefix_kernel(distance, old_ref, near1, far1, near2, far2, new_ref):
    me = place()
    core, upper = bit(me, 1), bit(me, distance)
    facing = unpack_symmetric(near1, far1, core, 0)
    leading, mirror, right = before_trans((old_ref[0], old_ref[1], old_ref[2]), facing)
    into, away = unpack_second(near2, far2, core, near1)
    trans, left = after_trans(leading, mirror, away, into)
    for i, x in enumerate((left, right, trans)):
        new_ref[i] = jnp.where(upper, x, old_ref[i])


def by_third(distance, me, near2, far2, near3, far3):
    third = bit(me, distance // 2)
    return jnp.where(third, near3[...], near2[...]), jnp.where(third, far3[...], far2[...])


def last_early_kernel(distance, old_ref, near2, far2, near3, far3, half_ref, left_out, right_out, trans_out, sems):
    me = place()
    upper = bit(me, distance)

    @pl.when(upper)
    def _():
        facing = unpack_symmetric(*by_third(distance, me, near2, far2, near3, far3), bit(me, 1), 0)
        for i, x in enumerate(before_trans((old_ref[0], old_ref[1], old_ref[2]), facing)):
            half_ref[i] = x

    @pl.when(jnp.logical_not(upper))
    def _():
        outs = left_out, right_out, trans_out
        copies = [pltpu.make_async_copy(old_ref.at[i : i + 1], out, sems.at[i]) for i, out in enumerate(outs)]
        for copy in copies:
            copy.start()
        for copy in copies:
            copy.wait()


def last_kernel(distance, half_ref, near2, far2, near3, far3, _l, _r, _t, left_out, right_out, trans_out, new_ref, sems):
    me = place()

    @pl.when(bit(me, distance))
    def _():
        right_copy = pltpu.make_async_copy(half_ref.at[2:3], right_out, sems.at[0])
        trans_copy = pltpu.make_async_copy(new_ref.at[0:1], trans_out, sems.at[1])
        left_copy = pltpu.make_async_copy(new_ref.at[1:2], left_out, sems.at[2])
        right_copy.start()
        into, away = unpack_second(*by_third(distance, me, near2, far2, near3, far3), bit(me, 1))
        q = split(into)
        bounced = split(dot3(split(half_ref[1]), q))
        new_ref[0] = dot3(split(half_ref[0]), q)
        trans_copy.start()
        new_ref[1] = away + dot3(split(into.T), bounced)
        left_copy.start()
        right_copy.wait()
        trans_copy.wait()
        left_copy.wait()


def call(kernel, products, outs, *args, given=(), copied=0, scratch=()):
    vmem, hbm = pl.BlockSpec(memory_space=pltpu.VMEM), pl.BlockSpec(memory_space=pltpu.HBM)
    m = args[0].shape[-1]
    return pl.pallas_call(
        kernel,
        out_shape=[jax.ShapeDtypeStruct(s, F32) for s in outs],
        in_specs=[vmem] * len(args) + [hbm] * len(given),
        out_specs=[vmem] * (len(outs) - copied) + [hbm] * copied,
        input_output_aliases={len(args) + i: len(outs) - copied + i for i in range(len(given))},
        scratch_shapes=scratch,
        cost_estimate=pl.CostEstimate(flops=2 * products * m**3, bytes_accessed=4 * m**2 * len(args), transcendentals=0),
        compiler_params=pltpu.CompilerParams(vmem_limit_bytes=40 * 2**20),
    )(*args, *given)


def shards(refl_left, refl_right, trans):
    m = trans.shape[1]
    levels = lax.axis_size(AXES).bit_length() - 1
    stack = (3, m, m)
    first, second, padded = (m // 4 + PAD, m), (m // 2 + m // 4, m), (m // 2 + m // 4 + PAD, m)
    sections = refl_left, refl_right, trans
    got = [swap(x, 1) for x in sections]
    section = jnp.concatenate(sections, 0)
    prefix, send1, send2, own = call(first_kernel, 36, [stack, first, second, stack], section, *got)
    pending = None
    for level in range(1, levels - 1):
        distance = 1 << level
        bind = lambda kernel: functools.partial(kernel, distance)
        near1, near2 = swap(send1, distance), swap(send2, distance)
        if pending is not None:
            (prefix,) = pending(prefix)
            near1, prefix = lax.optimization_barrier((near1, prefix))
        far1 = swap(near1, 1)
        if level < levels - 2:
            (halfway,) = call(early_kernel, 27, [stack], own, near1, far1)
        else:
            halfway, send1 = call(bind(final_early_kernel), 27, [stack, first], own, near1, far1)
        near2, halfway = lax.optimization_barrier((near2, halfway))
        far2 = swap(near2, 1)
        pending = lambda old, kernel=bind(prefix_kernel), got=(near1, far1, near2, far2): call(kernel, 36, [stack], old, *got)
        if level < levels - 2:
            send1, send2, own = call(bind(late_kernel), 9, [first, second, stack], halfway, near1, near2, far2)

    first3, first2 = pair(send1, 1, 3), pair(send1, 1, 2)
    (send2,) = call(bind(final_kernel), 9, [padded], halfway, near1, near2, far2)
    distance *= 2
    near3, near2 = pair(send2, 1, 3), pair(send2, 1, 2)
    first3, first2, prefix = lax.optimization_barrier((first3, first2, prefix))
    (prefix,) = pending(prefix)
    args = prefix, first2, swap(first2, 1), first3, swap(first3, 1)
    one, sems = (1, m, m), pltpu.SemaphoreType.DMA((3,))
    kernel = functools.partial(last_early_kernel, distance)
    halfway, *given = call(kernel, 27, [stack, one, one, one], *args, copied=3, scratch=[sems])
    near3, halfway = lax.optimization_barrier((near3, halfway))
    far3 = swap(near3, 1)
    near2, far3 = lax.optimization_barrier((near2, far3))
    args = halfway, near2, swap(near2, 1), near3, far3
    scratch = [pltpu.VMEM((2, m, m), F32), sems]
    return tuple(call(functools.partial(last_kernel, distance), 9, [one] * 3, *args, given=given, copied=3, scratch=scratch))


def solution(mesh):
    spec = P(AXES, None, None)
    return jax.shard_map(
        shards,
        mesh=mesh,
        in_specs=(spec,) * 3,
        out_specs=(spec,) * 3,
        check_vma=False,
    )
```
